32 devices in a mesh: section: 2 (over core), dp: 16 (over z, y, x).
Axes of the slice: x: 2, y: 2, z: 4, core: 2. Of those that a mesh axis runs over, the one named last changes fastest.
Arguments:
- layer_input: bfloat16 [128, 340, 256], P('dp'), may hold values from -6 to 6
- out_cotangent: bfloat16 [128, 340, 256], P('dp'), may hold values from -6 to 6
- segment_ids: int32 [128, 340], P('dp'), may hold values from 0 to 3, never falling along the last dimension, each value on 1 to 170 neighbouring positions
- gain_attn: bfloat16 [2, 256], P('section'), may hold values from 0.099609375 to 1.8984375
- weight_qkv: bfloat16 [2, 256, 768], P('section'), may hold values from -0.375 to 0.375
- weight_out: bfloat16 [2, 256, 256], P('section'), may hold values from -1.5 to 1.5
- gain_mlp: bfloat16 [2, 256], P('section'), may hold values from 0.099609375 to 1.8984375
- weight_up: bfloat16 [2, 256, 1024], P('section'), may hold values from -0.375 to 0.375
- weight_down: bfloat16 [2, 1024, 256], P('section'), may hold values from -0.25 to 0.25
Outputs:
- activations: bfloat16 [2, 128, 340, 256], P('section', 'dp')
- input_grads: float32 [2, 128, 340, 256], P('section', 'dp')
- grad_qkv: float32 [2, 256, 768], P('section')
- grad_out: float32 [2, 256, 256], P('section')
- grad_up: float32 [2, 256, 1024], P('section')
- grad_down: float32 [2, 1024, 256], P('section')
- grad_gain_attn: float32 [2, 256], P('section')
- grad_gain_mlp: float32 [2, 256], P('section')
The draws below stay inside these ranges and needn't reach their ends.
Inputs may be any that keep to these rules, and one draw needn't show every extreme that they name: `segment_ids`: within each row the ids never fall; each of 0 to 3 occurs as one run of 1 to 170 tokens.
All inputs are finite; a program needn't handle non-finite values.
Results may differ from the reference program's by a relative error of at most 0.019.
Values may be sent and summed in bfloat16 or wider, within the bound.
No kernel may reach another device: no remote copies, remote signals or barrier semaphores. Data moves between devices by JAX's collectives and lax.ppermute only.
A program may use at most 128 MiB of HBM per device.

```python
import math
import jax
import jax.numpy as jnp
import numpy as np
from jax import lax

D = 256
HEADS = 4
FF = 1024
FRAME = 17
SEGS = 4
L = 340
ROWS = 128


def block_scale(rng, shape, shards, least, top_value):
    loudness = 1.0
    for position, shards_of in shards:
        draws = jax.random.uniform(jax.random.fold_in(jax.random.fold_in(rng, 6), position), (shards_of,), jnp.float32, least / len(shards), top_value / len(shards))
        loudness = loudness * jnp.repeat(jnp.exp(draws), shape[position] // shards_of).reshape((-1,) + (1,) * (len(shape) - 1 - position))
    return loudness


def profile(amount, total, most, slope):
    loads = [(1 << 20) // math.isqrt(rank ** slope) + 1 for rank in range(2, amount + 1)]
    surplus, given = total - most - (amount - 1), [1] * (amount - 1)
    while surplus > 0:
        movable = [i for i in range(amount - 1) if given[i] < most]
        whole, remaining = sum([loads[i] for i in movable]), surplus
        for i in movable:
            extra = min(most - given[i], max(1, remaining * loads[i] // whole), surplus)
            given[i] = given[i] + extra
            surplus = surplus - extra
    return np.array([most] + given)


def ragged(own_key, amount, total, most, skew):
    if amount == 2:
        one = jax.random.randint(own_key, (), max(1, total - most), min(most, total - 1) + 1)
        return jnp.stack([one, total - one])
    tallies = jnp.asarray(profile(amount, total, most, skew), jnp.int32)
    twos = (amount - 1) // 2
    donor, receiver = tallies[1:1 + 2 * twos:2], tallies[2:2 + 2 * twos:2]
    room = jnp.minimum(donor - 1, most - receiver)
    shifted = jax.random.randint(jax.random.fold_in(own_key, 1), (twos,), 0, 1 << 20) % (room + 1)
    tallies = tallies.at[1:1 + 2 * twos:2].set(donor - shifted).at[2:2 + 2 * twos:2].set(receiver + shifted)
    return tallies[jax.random.permutation(jax.random.fold_in(own_key, 2), amount)]


def noise(own_key, dims, deviation, reach, pieces=(), kind=jnp.bfloat16):
    level = block_scale(own_key, dims, pieces, -0.22, 0.18) if pieces else 1.0
    entries = jax.random.normal(own_key, dims, jnp.float32) * deviation * level
    return jnp.minimum(jnp.maximum(entries, -reach), reach).astype(kind)


def setup_inputs(seed: int = 0) -> dict:
    seeds = jax.random.split(jax.random.key(seed), 10)
    return {
        "layer_input": noise(seeds[0], (ROWS, L, D), 1.0, 6.0, ((0, 16),)),
        "out_cotangent": noise(seeds[1], (ROWS, L, D), 1.0, 6.0, ((0, 16),)),
        "segment_ids": jax.vmap(lambda own: jnp.searchsorted(jnp.cumsum(ragged(own, SEGS, L, L // 2, 0)), jnp.arange(L), side="right"))(jax.random.split(seeds[2], ROWS)).reshape((ROWS, L)).astype(jnp.int32),
        "gain_attn": jnp.clip(1.0 + 0.18 * jax.random.normal(seeds[3], (2, D), jnp.float32), 0.099609375, 1.8984375).astype(jnp.bfloat16),
        "weight_qkv": noise(seeds[4], (2, D, 3 * D), D ** -0.5, 0.375, ((0, 2),)),
        "weight_out": noise(seeds[5], (2, D, D), (D // 16) ** -0.5, 1.5, ((0, 2),)),
        "gain_mlp": jnp.clip(1.0 + 0.18 * jax.random.normal(seeds[6], (2, D), jnp.float32), 0.099609375, 1.8984375).astype(jnp.bfloat16),
        "weight_up": noise(seeds[7], (2, D, FF), D ** -0.5, 0.375, ((0, 2),)),
        "weight_down": noise(seeds[8], (2, FF, D), (FF // 2) ** -0.5, 0.25, ((0, 2),)),
    }


EPS = 1e-05
NEG = -1e+30

@jax.custom_vjp
def low(v):
    return lax.optimization_barrier(v.astype(jnp.bfloat16)).astype(jnp.float32)

@jax.custom_vjp
def low_back(v):
    return v

def low_keep(v):
    return (low(v), None)

def low_pass(kept, grad):
    return (grad,)

def back_keep(v):
    return (v, None)

def back_low(kept, grad):
    return (low(grad),)
low.defvjp(low_keep, low_pass)
low_back.defvjp(back_keep, back_low)

def normalize(values, gain):
    center = values - lax.optimization_barrier(jnp.mean(values, axis=-1, keepdims=True))
    scale = lax.rsqrt(lax.optimization_barrier(jnp.mean(center * center, axis=-1, keepdims=True)) + EPS)
    return center * scale * gain

def softmax_rows(scores):
    highest = lax.optimization_barrier(jnp.max(scores, axis=-1, keepdims=True))
    expo = jnp.exp(scores - highest)
    return expo / lax.optimization_barrier(jnp.sum(expo, axis=-1, keepdims=True))

def gelu_exact(values):
    return jax.nn.gelu(values, approximate=False)

def block_mask(segments):
    length = segments.shape[1]
    frames = lax.iota(jnp.int32, length) // FRAME
    causal = frames[None, :] <= frames[:, None]
    same = segments[:, :, None] == segments[:, None, :]
    return jnp.logical_and(same, causal[None])

def matmul(left, right):
    return jnp.dot(left, right, precision=lax.Precision.HIGHEST, preferred_element_type=jnp.float32)

def layer(values, params, mask):
    gain_attn, weight_qkv, weight_out, gain_mlp, weight_up, weight_down = params
    count, length, width = values.shape
    flat = values.reshape(count * length, width)
    normed = low(normalize(flat, gain_attn))
    packed = low(low_back(matmul(normed, weight_qkv)))
    packed = packed.reshape(count, length, 3, HEADS, width // HEADS)
    query, key, value = (packed[:, :, 0], packed[:, :, 1], packed[:, :, 2])
    factor = (width // HEADS) ** (-0.5)
    raw = jnp.einsum('bqhd,bkhd->bhqk', query, key, precision=lax.Precision.HIGHEST, preferred_element_type=jnp.float32)
    scores = low_back(raw * factor)
    scores = jnp.where(mask[:, None], scores, NEG)
    probs = low(softmax_rows(scores))
    mixed = jnp.einsum('bhqk,bkhd->bqhd', probs, value, precision=lax.Precision.HIGHEST, preferred_element_type=jnp.float32)
    mixed = low(low_back(mixed)).reshape(count * length, width)
    middle = flat + low_back(matmul(mixed, weight_out))
    normed_mlp = low(normalize(middle, gain_mlp))
    upper = low_back(matmul(normed_mlp, weight_up))
    active = low(gelu_exact(upper))
    result = middle + low_back(matmul(active, weight_down))
    return result.reshape(count, length, width)

def forward(first_in, params_first, params_second, probe, mask):
    hidden = layer(first_in, params_first, mask)
    passed = low_back(low(hidden)) + probe
    return (layer(passed, params_second, mask), hidden)

def reference(layer_input, out_cotangent, segment_ids, gain_attn, weight_qkv, weight_out, gain_mlp, weight_up, weight_down):
    stacked = tuple((w.astype(jnp.float32) for w in (gain_attn, weight_qkv, weight_out, gain_mlp, weight_up, weight_down)))
    params_first = tuple((w[0] for w in stacked))
    params_second = tuple((w[1] for w in stacked))
    rows, length, width = layer_input.shape
    group = 8 if rows % 8 == 0 else 4
    groups = rows // group
    inputs = layer_input.reshape(groups, group, length, width)
    cotangents = out_cotangent.reshape(groups, group, length, width)
    segments = segment_ids.reshape(groups, group, length)
    zero_first = tuple((jnp.zeros_like(w) for w in params_first))
    zero_second = tuple((jnp.zeros_like(w) for w in params_second))

    def one_group(carry, batch):
        inp, cot, seg = batch
        mask = block_mask(seg)
        values = inp.astype(jnp.float32)
        probe = jnp.zeros(values.shape, jnp.float32)

        def apply(first_in, pf, ps, pr):
            return forward(first_in, pf, ps, pr, mask)
        out, back, hidden = jax.vjp(apply, values, params_first, params_second, probe, has_aux=True)
        d_input, g_first, g_second, d_probe = back(cot.astype(jnp.float32))
        new_first = tuple((a + b for a, b in zip(carry[0], g_first)))
        new_second = tuple((a + b for a, b in zip(carry[1], g_second)))
        return ((new_first, new_second), (hidden.astype(jnp.bfloat16), out.astype(jnp.bfloat16), d_input, d_probe))
    (g_first, g_second), (hidden, out, d_input, d_probe) = lax.scan(one_group, (zero_first, zero_second), (inputs, cotangents, segments))
    shape = (rows, length, width)
    activations = jnp.stack([hidden.reshape(shape), out.reshape(shape)])
    input_grads = jnp.stack([d_input.reshape(shape), d_probe.reshape(shape)])
    grads = [jnp.stack([a, b]) for a, b in zip(g_first, g_second)]
    return (activations, input_grads, grads[1], grads[2], grads[4], grads[5], grads[0], grads[3])
```

```python
import jax
import jax.numpy as jnp
from jax import lax
from jax.experimental import pallas as pl
from jax.experimental.pallas import tpu as pltpu
from jax.sharding import PartitionSpec as P

D = 256
FF = 1024
FRAME = 17
LP = 352
EPS = 1e-05
BIG = -(2.0**100)
BLOCKS = ((0, 112, 0, 128), (112, 240, 0, 256), (240, 304, 64, 320), (304, 352, 96, 352))
ERF = (7.97884531e-01, 3.63337968e-02, -3.28609901e-05, -5.53091310e-05, 3.97786435e-06, -1.33973644e-07, 1.81750064e-09)
F32 = jnp.float32
BF = jnp.bfloat16


def mm(a, b):
    return jnp.dot(a, b, preferred_element_type=F32)


def mm_t(a, b):
    return lax.dot_general(a, b, (((1,), (1,)), ((), ())), preferred_element_type=F32)


def tmm(a, b):
    return lax.dot_general(a, b, (((0,), (0,)), ((), ())), preferred_element_type=F32)


def norm_stats(x):
    mean = jnp.sum(x, axis=-1, keepdims=True) * (1.0 / D)
    center = x - mean
    var = jnp.sum(center * center, axis=-1, keepdims=True) * (1.0 / D)
    rstd = lax.rsqrt(var + EPS)
    return center * rstd, rstd


def norm_back(d_out, gain, xhat, rstd):
    dy = d_out * gain
    s1 = jnp.sum(dy, axis=-1, keepdims=True) * (1.0 / D)
    s2 = jnp.sum(dy * xhat, axis=-1, keepdims=True) * (1.0 / D)
    return rstd * (dy - s1 - xhat * s2)


def gain_rows(d_out, xhat):
    prod = d_out * xhat
    return jnp.sum(prod.reshape(LP // 8, 8, D), axis=0)


def gelu_pair(u):
    u2 = u * u
    p = jnp.full_like(u, ERF[-1])
    for c in ERF[-2::-1]:
        p = p * u2 + c
    cdf = 0.5 + 0.5 * jnp.tanh(u * p)
    pdf = 0.3989422804014327 * jnp.exp(-0.5 * u2)
    return u * cdf, cdf + u * pdf


def two_heads(block, lane_low):
    zero = jnp.zeros_like(block)
    return jnp.concatenate(
        [jnp.where(lane_low, block, zero), jnp.where(lane_low, zero, block)], axis=0
    )


def one_pair(stacked, n, lane_low):
    return jnp.where(lane_low, stacked[:n], stacked[n:])


def kernel(
    x_ref, cot_ref, eq_ref, ek_ref, wqkv_ref, wout_ref, wup_ref, wdown_ref, gains_ref,
    y_ref, d_ref, grads_ref,
    hid_ref, xhat1_ref, rstd1_ref, xhat2_ref, rstd2_ref, a_ref, b_ref, o_ref, qs_ref, ke_ref,
    v1_ref, p_ref, m_ref, gp_ref, h_ref, dup_ref, up_ref, do_ref, dqkv_ref, dk_ref, dv_ref,
    aqkv_ref, aout_ref, aup_ref, adown_ref, again_ref,
):
    step = pl.program_id(0)
    last = pl.num_programs(0) - 1

    @pl.when(step == 0)
    def _():
        for ref in (aqkv_ref, aout_ref, aup_ref, adown_ref, again_ref):
            ref[...] = jnp.zeros_like(ref)

    eq = eq_ref[0]
    ek = ek_ref[0]

    def low_mask(n):
        return lax.broadcasted_iota(jnp.int32, (n, 128), 1) < 64

    def forward(l, x):
        xhat, rstd = norm_stats(x)
        xhat1_ref[l] = xhat
        rstd1_ref[l] = jnp.broadcast_to(rstd, (LP, 128))
        a = (xhat * gains_ref[l, 0:1, :]).astype(BF)
        a_ref[l] = a
        for p in range(2):
            qs = (mm(a, wqkv_ref[l, :, 128 * p : 128 * p + 128])).astype(BF) * jnp.array(0.125, BF)
            for q0, q1, _, _ in BLOCKS:
                qs_ref[l, p, 2 * q0 : 2 * q1, 0:128] = two_heads(qs[q0:q1], low_mask(q1 - q0))
                qs_ref[l, p, 2 * q0 : 2 * q1, 128:256] = jnp.concatenate([eq[q0:q1], eq[q0:q1]], axis=0)
            ke_ref[l, p, :, 0:128] = mm(a, wqkv_ref[l, :, 256 + 128 * p : 384 + 128 * p]).astype(BF)
            ke_ref[l, p, :, 128:256] = ek
            v1_ref[l, p, :, 0:128] = mm(a, wqkv_ref[l, :, 512 + 128 * p : 640 + 128 * p]).astype(BF)
            v1_ref[l, p, :, 128:256] = jnp.ones((LP, 128), BF)
        for p in range(2):
            for q0, q1, k0, k1 in BLOCKS:
                n = q1 - q0
                s = mm_t(qs_ref[l, p, 2 * q0 : 2 * q1, :], ke_ref[l, p, k0:k1, :])
                e = jnp.exp(s - jnp.max(s, axis=-1, keepdims=True))
                prob = (e * (1.0 / jnp.sum(e, axis=-1, keepdims=True))).astype(BF)
                p_ref[l, p, 2 * q0 : 2 * q1, 0 : k1 - k0] = prob
                o = mm(prob, v1_ref[l, p, k0:k1, 0:128])
                o_ref[l, q0:q1, 128 * p : 128 * p + 128] = one_pair(o, n, low_mask(n)).astype(BF)
        h = x + mm(o_ref[l], wout_ref[l])
        xhat, rstd = norm_stats(h)
        xhat2_ref[l] = xhat
        rstd2_ref[l] = jnp.broadcast_to(rstd, (LP, 128))
        b = (xhat * gains_ref[l, 1:2, :]).astype(BF)
        b_ref[l] = b
        y = h
        for c in range(4):
            cols = slice(256 * c, 256 * c + 256)
            m, gp = gelu_pair(mm(b, wup_ref[l, :, cols]))
            m = m.astype(BF)
            m_ref[l, :, cols] = m
            gp_ref[l, :, cols] = gp.astype(BF)
            y = y + mm(m, wdown_ref[l, cols, :])
        return y

    def backward(l, g):
        gb = g.astype(BF)
        d_b = jnp.zeros((LP, D), F32)
        b = b_ref[l]
        for c in range(4):
            cols = slice(256 * c, 256 * c + 256)
            du = (mm_t(gb, wdown_ref[l, cols, :]) * gp_ref[l, :, cols].astype(F32)).astype(BF)
            adown_ref[l, :, cols] += tmm(gb, m_ref[l, :, cols])
            aup_ref[l, :, cols] += tmm(b, du)
            d_b = d_b + mm_t(du, wup_ref[l, :, cols])
        xhat = xhat2_ref[l]
        again_ref[l, 1] += gain_rows(d_b, xhat)
        d_h = g + norm_back(d_b, gains_ref[l, 1:2, :], xhat, rstd2_ref[l, :, 0:1])
        d_hb = d_h.astype(BF)
        o = o_ref[l]
        aout_ref[l] += tmm(o, d_hb)
        d_o = mm_t(d_hb, wout_ref[l]).astype(BF)
        prod = (-(d_o.astype(F32) * o.astype(F32))).astype(BF)
        for p in range(2):
            lanes = slice(128 * p, 128 * p + 128)
            for q0, q1, _, _ in BLOCKS:
                mask = low_mask(q1 - q0)
                do_ref[p, 2 * q0 : 2 * q1, 0:128] = two_heads(d_o[q0:q1, lanes], mask)
                do_ref[p, 2 * q0 : 2 * q1, 128:256] = two_heads(prod[q0:q1, lanes], mask)
        for p in range(2):
            dk_ref[...] = jnp.zeros_like(dk_ref)
            dv_ref[...] = jnp.zeros_like(dv_ref)
            for q0, q1, k0, k1 in BLOCKS:
                n = q1 - q0
                rows = slice(2 * q0, 2 * q1)
                dp = mm_t(do_ref[p, rows, :], v1_ref[l, p, k0:k1, :])
                prob = p_ref[l, p, rows, 0 : k1 - k0]
                ds = (prob.astype(F32) * dp).astype(BF)
                dq = mm(ds, ke_ref[l, p, k0:k1, 0:128])
                dqkv_ref[q0:q1, 128 * p : 128 * p + 128] = (one_pair(dq, n, low_mask(n)) * 0.125).astype(BF)
                dv_ref[k0:k1, :] += tmm(prob, do_ref[p, rows, 0:128])
                dk_ref[k0:k1, :] += tmm(ds, qs_ref[l, p, rows, 0:128])
            dqkv_ref[:, 256 + 128 * p : 384 + 128 * p] = dk_ref[...].astype(BF)
            dqkv_ref[:, 512 + 128 * p : 640 + 128 * p] = dv_ref[...].astype(BF)
        d_qkv = dqkv_ref[...]
        aqkv_ref[l] += tmm(a_ref[l], d_qkv)
        d_a = mm_t(d_qkv, wqkv_ref[l])
        xhat = xhat1_ref[l]
        again_ref[l, 0] += gain_rows(d_a, xhat)
        return d_h + norm_back(d_a, gains_ref[l, 0:1, :], xhat, rstd1_ref[l, :, 0:1])

    y0 = forward(0, x_ref[0].astype(F32)).astype(BF)
    y_ref[0, 0] = y0
    y1 = forward(1, y0.astype(F32)).astype(BF)
    y_ref[1, 0] = y1
    d1 = backward(1, cot_ref[0].astype(F32)).astype(BF)
    d_ref[1, 0] = d1
    d0 = backward(0, d1.astype(F32)).astype(BF)
    d_ref[0, 0] = d0

    @pl.when(step == last)
    def _():
        for l in range(2):
            for j in range(3):
                grads_ref[l, 256 * j : 256 * j + 256, :] = aqkv_ref[l, :, 256 * j : 256 * j + 256].astype(BF)
            grads_ref[l, 768:1024, :] = aout_ref[l].astype(BF)
            for j in range(4):
                cols = slice(256 * j, 256 * j + 256)
                grads_ref[l, 1024 + 256 * j : 1280 + 256 * j, :] = aup_ref[l, :, cols].astype(BF)
                grads_ref[l, 2048 + 256 * j : 2304 + 256 * j, :] = adown_ref[l, :, cols].T.astype(BF)
            row = lax.broadcasted_iota(jnp.int32, (16, D), 0)
            attn = jnp.sum(again_ref[l, 0], axis=0, keepdims=True)
            mlp = jnp.sum(again_ref[l, 1], axis=0, keepdims=True)
            grads_ref[l, 3072:3088, :] = jnp.where(row == 0, attn, jnp.where(row == 1, mlp, 0.0)).astype(BF)


def local_step(x, cot, eq, ek, wqkv, wout, wup, wdown, gains):
    rows = x.shape[0]
    tok = lambda w: pl.BlockSpec((1, LP, w), lambda i: (i, 0, 0))
    whole = lambda a: pl.BlockSpec(a.shape, lambda i: (0,) * a.ndim, pipeline_mode=pl.Buffered(1))
    out_tok = pl.BlockSpec((2, 1, LP, D), lambda i: (0, i, 0, 0))
    vm = pltpu.VMEM
    return pl.pallas_call(
        kernel,
        grid=(rows,),
        in_specs=[tok(D), tok(D), tok(128), tok(128)] + [whole(a) for a in (wqkv, wout, wup, wdown, gains)],
        out_specs=[out_tok, out_tok, pl.BlockSpec((2, 3088, D), lambda i: (0, 0, 0), pipeline_mode=pl.Buffered(1))],
        out_shape=[
            jax.ShapeDtypeStruct((2, rows, LP, D), BF),
            jax.ShapeDtypeStruct((2, rows, LP, D), BF),
            jax.ShapeDtypeStruct((2, 3088, D), BF),
        ],
        scratch_shapes=[
            vm((LP, D), F32),
            vm((2, LP, D), F32), vm((2, LP, 128), F32), vm((2, LP, D), F32), vm((2, LP, 128), F32),
            vm((2, LP, D), BF), vm((2, LP, D), BF), vm((2, LP, D), BF),
            vm((2, 2, 2 * LP, D), BF), vm((2, 2, LP, D), BF), vm((2, 2, LP, D), BF),
            vm((2, 2, 2 * LP, D), BF), vm((2, LP, FF), BF), vm((2, LP, FF), BF),
            vm((LP, D), F32), vm((LP, D), F32), vm((LP, D), F32),
            vm((2, 2 * LP, D), BF), vm((LP, 3 * D), BF), vm((LP, 128), F32), vm((LP, 128), F32),
            vm((2, D, 3 * D), F32), vm((2, D, D), F32), vm((2, D, FF), F32), vm((2, D, FF), F32), vm((2, 2, 8, D), F32),
        ],
        compiler_params=pltpu.CompilerParams(
            dimension_semantics=("arbitrary",), vmem_limit_bytes=60 * 1024 * 1024
        ),
    )(x, cot, eq, ek, wqkv, wout, wup, wdown, gains)


def codes(segments):
    rows, length = segments.shape
    seg = jnp.pad(segments, ((0, 0), (0, LP - length)), constant_values=-1)[:, :, None]
    frame = (lax.iota(jnp.int32, LP) // FRAME)[None, :, None]
    lane = lax.iota(jnp.int32, 128)[None, None, :]
    eq = jnp.where(lane < 64, frame == lane, seg == lane - 64)
    ek = jnp.where(lane < 64, frame > lane, (seg != lane - 64) & (lane < 68))
    return eq.astype(BF), jnp.where(ek, BIG, 0.0).astype(BF)


def partner(value):
    return lax.ppermute(value, "section", [(0, 1), (1, 0)])


def cross(value, count, bits):
    pairs = [(s * count + i, s * count + (i ^ (1 << bits[s]))) for s in range(2) for i in range(count)]
    return lax.ppermute(value, ("section", "dp"), pairs)


def add(a, b):
    return (a.astype(F32) + b.astype(F32)).astype(BF)


def sum_over_dp(main, extra, section):
    count = lax.axis_size("dp")
    place = lax.axis_index("dp")
    depth = count.bit_length() - 1
    orders = [(i, i) for i in range(depth)]
    if depth > 1:
        orders[0], orders[1] = (0, 1), (1, 0)
    uppers = []
    for bits in orders:
        upper = jnp.where(section == 0, place >> bits[0], place >> bits[1]) & 1
        uppers.append(upper)
        half = main.shape[0] // 2
        send = lax.dynamic_slice_in_dim(main, (1 - upper) * half, half, 0)
        got = cross(jnp.concatenate([send, extra], axis=0), count, bits)
        main = add(lax.dynamic_slice_in_dim(main, upper * half, half, 0), got[:half])
        extra = add(extra, got[half:])
    for bits, upper in zip(orders[::-1], uppers[::-1]):
        got = cross(main, count, bits)
        main = jnp.where(
            upper == 0, jnp.concatenate([main, got], axis=0), jnp.concatenate([got, main], axis=0)
        )
    return main, extra


def shards(
    layer_input, out_cotangent, segment_ids, gain_attn, weight_qkv, weight_out, gain_mlp, weight_up, weight_down
):
    section = lax.axis_index("section")
    first = section == 0
    rows, length, width = layer_input.shape
    half = rows // 2

    def both(mine):
        theirs = partner(mine)
        return jnp.concatenate([jnp.where(first, mine, theirs), jnp.where(first, theirs, mine)], axis=0)

    gains = both(jnp.stack([gain_attn, gain_mlp], axis=1)).astype(F32)
    weights = [both(w) for w in (weight_qkv, weight_out, weight_up, weight_down)]
    pad = ((0, 0), (0, LP - length), (0, 0))
    mine = lambda a: lax.dynamic_slice_in_dim(a, section * half, half, 0)
    eq, ek = codes(mine(segment_ids))
    y, d, grads = local_step(
        jnp.pad(mine(layer_input), pad), jnp.pad(mine(out_cotangent), pad), eq, ek, *weights, gains
    )

    def split(a):
        take = lambda j: lax.dynamic_index_in_dim(a, j, 0, False)
        return take(section), take(1 - section)

    keep_g, send_g = split(grads)
    keep_y, send_y = split(y[:, :, :length])
    keep_d, send_d = split(d[:, :, :length])
    total = add(keep_g, partner(send_g))
    main, extra = sum_over_dp(total[:3072], total[3072:], section)

    def whole_rows(keep, send):
        got = partner(send)
        return jnp.where(
            first, jnp.concatenate([keep, got], axis=0), jnp.concatenate([got, keep], axis=0)
        )

    activations = whole_rows(keep_y, send_y)
    input_grads = whole_rows(keep_d, send_d).astype(F32)
    main = main.astype(F32)
    extra = extra.astype(F32)
    side = lambda first_row, n: jnp.concatenate(
        [main[first_row + D * j : first_row + D * j + D] for j in range(n)], axis=1
    )
    return (
        activations[None],
        input_grads[None],
        side(0, 3)[None],
        main[768:1024][None],
        side(1024, 4)[None],
        main[2048:3072][None],
        extra[0][None],
        extra[1][None],
    )


def solution(mesh):
    placed = (
        P("dp", None, None),
        P("dp", None, None),
        P("dp", None),
        P("section", None),
        P("section", None, None),
        P("section", None, None),
        P("section", None),
        P("section", None, None),
        P("section", None, None),
    )
    return jax.shard_map(
        shards,
        mesh=mesh,
        in_specs=placed,
        out_specs=(
            P("section", "dp", None, None),
            P("section", "dp", None, None),
            P("section", None, None),
            P("section", None, None),
            P("section", None, None),
            P("section", None, None),
            P("section", None),
            P("section", None),
        ),
        check_vma=False,
    )
```

```python
import jax
import jax.numpy as jnp
from jax import lax
from jax.experimental import pallas as pl
from jax.experimental.pallas import tpu as pltpu
from jax.sharding import PartitionSpec as P

D = 256
FF = 1024
FRAME = 17
LP = 352
EPS = 1e-05
BIG = -(2.0**100)
BLOCKS = ((0, 112, 0, 128), (112, 240, 0, 256), (240, 304, 64, 320), (304, 352, 96, 352))
ERF = (7.97852379e-01, 3.64383569e-02, -1.13746830e-04, -3.20493527e-05, 1.18025665e-06)
TWO = 2
F32 = jnp.float32
BF = jnp.bfloat16


def mm(a, b):
    return jnp.dot(a, b, preferred_element_type=F32)


def mm_t(a, b):
    return lax.dot_general(a, b, (((1,), (1,)), ((), ())), preferred_element_type=F32)


def tmm(a, b):
    return lax.dot_general(a, b, (((0,), (0,)), ((), ())), preferred_element_type=F32)


def norm_stats(x):
    mean = jnp.sum(x, axis=-1, keepdims=True) * (1.0 / D)
    center = x - mean
    var = jnp.sum(center * center, axis=-1, keepdims=True) * (1.0 / D)
    rstd = lax.rsqrt(var + EPS)
    return center * rstd, rstd


def norm_back(d_out, gain, xhat, rstd):
    dy = d_out * gain
    s1 = jnp.sum(dy, axis=-1, keepdims=True) * (1.0 / D)
    s2 = jnp.sum(dy * xhat, axis=-1, keepdims=True) * (1.0 / D)
    return rstd * (dy - s1 - xhat * s2)


def gain_rows(d_out, xhat):
    prod = d_out * xhat
    return jnp.sum(prod.reshape(prod.shape[0] // 8, 8, D), axis=0)


def gelu_pair(u):
    u2 = u * u
    p = jnp.full_like(u, ERF[-1])
    for c in ERF[-2::-1]:
        p = p * u2 + c
    cdf = 0.5 + 0.5 * jnp.tanh(u * p)
    pdf = jnp.exp2(u2 * -0.7213475204444817 - 1.3257480647361593)
    return u * cdf, cdf + u * pdf


def two_heads(block, lane_low):
    zero = jnp.zeros_like(block)
    return jnp.concatenate(
        [jnp.where(lane_low, block, zero), jnp.where(lane_low, zero, block)], axis=0
    )


def one_pair(stacked, n, lane_low):
    return jnp.where(lane_low, stacked[:n], stacked[n:])


def low_mask(n):
    return lax.broadcasted_iota(jnp.int32, (n, 128), 1) < 64


def merged(*lists):
    tagged = [((i + 0.5) / len(units), j, unit) for j, units in enumerate(lists) for i, unit in enumerate(units)]
    for _, _, unit in sorted(tagged, key=lambda t: t[:2]):
        unit()


def wide(column):
    return jnp.concatenate([column, column], axis=1)


PARTS = ((0, 176), (176, 352))
PAIRS = ((0, slice(0, 128)), (1, slice(128, 256)))


def kernel(
    sec_ref, x_ref, cot_ref, seg_ref, gmine_ref, gother_ref,
    wqkv_mine, wout_mine, wup_mine, wdown_mine, wqkv_other, wout_other, wup_other, wdown_other,
    yk_ref, ys_ref, dk_out_ref, ds_out_ref, pk_ref, qk_ref, psend_ref, qsend_ref,
    wqkv_ref, wout_ref, wup_ref, wdown_ref, wsem, gains_ref, eq_ref, ek_ref, ybuf_ref, dbuf_ref,
    res_ref, xhat1_ref, rstd1_ref, xhat2_ref, rstd2_ref, a_ref, b_ref, o_ref, qs_ref, k_ref, v_ref,
    p_ref, m_ref, gp_ref, gb_ref, du_ref, dh_ref, dhb_ref, do_ref, dqkv_ref, dk_ref, dv_ref,
    left_ref, aqkv_ref, aout_ref, aup_ref, adown_ref, again_ref,
):
    step = pl.program_id(0)
    last = pl.num_programs(0) - 1
    sec = sec_ref[0]
    first = sec == 0
    length = x_ref.shape[1]

    @pl.when(step == 0)
    def _():
        copies = []
        for mine, other, held in (
            (wqkv_mine, wqkv_other, wqkv_ref), (wout_mine, wout_other, wout_ref),
            (wup_mine, wup_other, wup_ref), (wdown_mine, wdown_other, wdown_ref),
        ):
            copies.append(pltpu.make_async_copy(mine.at[0], held.at[sec], wsem.at[len(copies)]))
            copies.append(pltpu.make_async_copy(other.at[0], held.at[1 - sec], wsem.at[len(copies)]))
        for copy in copies:
            copy.start()
        gains_ref[0] = jnp.where(first, gmine_ref[...], gother_ref[...])
        gains_ref[1] = jnp.where(first, gother_ref[...], gmine_ref[...])
        for ref in (aqkv_ref, aout_ref, aup_ref, adown_ref, again_ref):
            ref[...] = jnp.zeros_like(ref)
        for copy in copies:
            copy.wait()

    parts = ((0, 176), (176, length))

    def load(r):
        def tokens(lo, hi):
            res_ref[r, lo:hi, :] = x_ref[r, lo:hi, :].astype(F32)
            gb_ref[1, LP * r + lo : LP * r + hi, :] = cot_ref[r, lo:hi, :]

        def visibility():
            seg = jnp.broadcast_to(seg_ref[r], (128, seg_ref.shape[2])).astype(F32).T[:LP]
            lane = lax.broadcasted_iota(jnp.int32, (LP, 128), 1)
            token = lax.broadcasted_iota(jnp.int32, (LP, 128), 0)
            same = seg == (lane - 64).astype(F32)
            start = FRAME * lane
            here = jnp.logical_and(token >= start, token < start + FRAME)
            later = token >= start + FRAME
            other = jnp.logical_and(jnp.logical_not(same), lane < 68)
            eq_ref[r] = jnp.where(lane < 64, jnp.where(here, 1.0, 0.0), jnp.where(same, 1.0, 0.0)).astype(BF)
            ek_ref[r] = jnp.where(lane < 64, jnp.where(later, BIG, 0.0), jnp.where(other, BIG, 0.0)).astype(BF)

        res_ref[r, LP - 16 : LP, :] = jnp.zeros((16, D), F32)
        gb_ref[1, LP * r + LP - 16 : LP * r + LP, :] = jnp.zeros((16, D), BF)
        return [lambda lo=lo, hi=hi: tokens(lo, hi) for lo, hi in parts] + [visibility]

    ones = jnp.ones((LP, 128), BF)

    def attn_forward(r, l):
        base = LP * r
        units = []

        def norm(lo, hi):
            xhat, rstd = norm_stats(res_ref[r, lo:hi, :])
            xhat1_ref[l, r, lo:hi, :] = xhat
            rstd1_ref[l, r, lo:hi, :] = jnp.broadcast_to(rstd, (hi - lo, 128))
            a_ref[l, base + lo : base + hi, :] = (xhat * gains_ref[l, 0:1, :]).astype(BF)

        def query():
            q = mm(a_ref[l, base : base + LP, :], wqkv_ref[l, :, 0:256]).astype(BF) * jnp.array(0.125, BF)
            for p in range(2):
                for q0, q1, _, _ in BLOCKS:
                    qs_ref[l, r, p, 2 * q0 : 2 * q1, :] = two_heads(q[q0:q1, 128 * p : 128 * p + 128], low_mask(q1 - q0))

        def key():
            k_ref[l, r] = mm(a_ref[l, base : base + LP, :], wqkv_ref[l, :, 256:512]).astype(BF)

        def value():
            v_ref[l, r] = mm(a_ref[l, base : base + LP, :], wqkv_ref[l, :, 512:768]).astype(BF)

        held = {}

        def scores(q0, q1, k0, k1):
            eq = eq_ref[r, q0:q1, :]
            eq = jnp.concatenate([eq, eq], axis=0)
            ek = ek_ref[r, k0:k1, :]
            held[q0] = [
                mm_t(
                    jnp.concatenate([qs_ref[l, r, p, 2 * q0 : 2 * q1, :], eq], axis=1),
                    jnp.concatenate([k_ref[l, r, k0:k1, lanes], ek], axis=1),
                )
                for p, lanes in PAIRS
            ]

        def mix(q0, q1, k0, k1):
            n = q1 - q0
            probs = []
            for p, _ in PAIRS:
                s = held[q0][p]
                e = jnp.exp(s - jnp.max(s, axis=-1, keepdims=True))
                prob = (e * (1.0 / jnp.sum(e, axis=-1, keepdims=True))).astype(BF)
                p_ref[l, r, p, 2 * q0 : 2 * q1, 0 : k1 - k0] = prob
                probs.append(prob)
            for p, lanes in PAIRS:
                o = mm(probs[p], v_ref[l, r, k0:k1, lanes])
                o_ref[l, base + q0 : base + q1, lanes] = one_pair(o, n, low_mask(n)).astype(BF)

        def out(lo, hi):
            h = res_ref[r, lo:hi, :] + mm(o_ref[l, base + lo : base + hi, :], wout_ref[l])
            res_ref[r, lo:hi, :] = h
            xhat, rstd = norm_stats(h)
            xhat2_ref[l, r, lo:hi, :] = xhat
            rstd2_ref[l, r, lo:hi, :] = jnp.broadcast_to(rstd, (hi - lo, 128))
            b_ref[l, base + lo : base + hi, :] = (xhat * gains_ref[l, 1:2, :]).astype(BF)

        units += [lambda lo=lo, hi=hi: norm(lo, hi) for lo, hi in PARTS]
        units += [query, key, value]
        first = [lambda b=b: scores(*b) for b in BLOCKS]
        second = [lambda b=b: mix(*b) for b in BLOCKS]
        units += [first[0], first[1], second[0], first[2], second[1], first[3], second[2], second[3]]
        units += [lambda lo=lo, hi=hi: out(lo, hi) for lo, hi in PARTS]
        return units

    def mlp_forward(r, l):
        base = LP * r

        def chunk(c, lo, hi):
            rows = slice(base + lo, base + hi)
            ups = [mm(b_ref[l, rows, :], wup_ref[l, :, 256 * j : 256 * j + 256]) for j in (c, c + 1)]
            for j, u in zip((c, c + 1), ups):
                m, gp = gelu_pair(u)
                m_ref[l, rows, 256 * j : 256 * j + 256] = m.astype(BF)
                gp_ref[l, r, lo:hi, 256 * j : 256 * j + 256] = gp.astype(BF)

        def down(lo, hi):
            y = res_ref[r, lo:hi, :] + mm(m_ref[l, base + lo : base + hi, :], wdown_ref[l])
            y = y.astype(BF)
            if l == 0:
                ybuf_ref[r, lo:hi, :] = y
                res_ref[r, lo:hi, :] = y.astype(F32)
            else:
                end = min(hi, length)
                y0, y1 = ybuf_ref[r, lo:hi, :][: end - lo], y[: end - lo]
                yk_ref[r, lo:end, :] = jnp.where(first, y0, y1)
                ys_ref[r, lo:end, :] = jnp.where(first, y1, y0)

        return [f for lo, hi in PARTS for f in (
            lambda lo=lo, hi=hi: chunk(0, lo, hi), lambda lo=lo, hi=hi: chunk(2, lo, hi), lambda lo=lo, hi=hi: down(lo, hi))]

    def mlp_backward(r, l):
        base = LP * r

        def chunk(c, lo, hi):
            rows = slice(base + lo, base + hi)
            dms = [mm_t(gb_ref[l, rows, :], wdown_ref[l, 256 * j : 256 * j + 256, :]) for j in (c, c + 1)]
            for j, dm in zip((c, c + 1), dms):
                cols = slice(256 * j, 256 * j + 256)
                du_ref[l, rows, cols] = (dm * gp_ref[l, r, lo:hi, cols].astype(F32)).astype(BF)

        def back(lo, hi):
            rows = slice(base + lo, base + hi)
            d_b = mm_t(du_ref[l, rows, :], wup_ref[l])
            xhat = xhat2_ref[l, r, lo:hi, :]
            again_ref[l, 1] += gain_rows(d_b, xhat)
            d_h = gb_ref[l, rows, :].astype(F32) + norm_back(d_b, gains_ref[l, 1:2, :], xhat, wide(rstd2_ref[l, r, lo:hi, :]))
            dh_ref[r, lo:hi, :] = d_h
            dhb_ref[l, rows, :] = d_h.astype(BF)

        return (
            [lambda c=c, lo=lo, hi=hi: chunk(c, lo, hi) for c in (0, 2) for lo, hi in PARTS]
            + [lambda lo=lo, hi=hi: back(lo, hi) for lo, hi in PARTS]
        )

    def attn_backward(r, l):
        base = LP * r

        def out():
            d_o = mm_t(dhb_ref[l, base : base + LP, :], wout_ref[l]).astype(BF)
            prod = (-(d_o.astype(F32) * o_ref[l, base : base + LP, :].astype(F32))).astype(BF)
            for p in range(2):
                lanes = slice(128 * p, 128 * p + 128)
                for q0, q1, _, _ in BLOCKS:
                    mask = low_mask(q1 - q0)
                    do_ref[r, p, 2 * q0 : 2 * q1, 0:128] = two_heads(d_o[q0:q1, lanes], mask)
                    do_ref[r, p, 2 * q0 : 2 * q1, 128:256] = two_heads(prod[q0:q1, lanes], mask)
            dk_ref[r] = jnp.zeros((LP, D), F32)
            dv_ref[r] = jnp.zeros((LP, D), F32)

        held = {}

        def probs(q0, q1, k0, k1):
            rows = slice(2 * q0, 2 * q1)
            held[q0] = [
                mm_t(do_ref[r, p, rows, :], jnp.concatenate([v_ref[l, r, k0:k1, lanes], ones[k0:k1]], axis=1))
                for p, lanes in PAIRS
            ]

        def values(q0, q1, k0, k1):
            rows = slice(2 * q0, 2 * q1)
            for p, lanes in PAIRS:
                dv_ref[r, k0:k1, lanes] += tmm(p_ref[l, r, p, rows, 0 : k1 - k0], do_ref[r, p, rows, 0:128])

        def queries(q0, q1, k0, k1):
            n = q1 - q0
            rows = slice(2 * q0, 2 * q1)
            ds = [(p_ref[l, r, p, rows, 0 : k1 - k0].astype(F32) * held[q0][p]).astype(BF) for p, _ in PAIRS]
            for p, lanes in PAIRS:
                dq = mm(ds[p], k_ref[l, r, k0:k1, lanes])
                dqkv_ref[l, base + q0 : base + q1, lanes] = (one_pair(dq, n, low_mask(n)) * 0.125).astype(BF)
            for p, lanes in PAIRS:
                dk_ref[r, k0:k1, lanes] += tmm(ds[p], qs_ref[l, r, p, rows, :])

        def finish(lo, hi):
            rows = slice(base + lo, base + hi)
            dqkv_ref[l, rows, 256:512] = dk_ref[r, lo:hi, :].astype(BF)
            dqkv_ref[l, rows, 512:768] = dv_ref[r, lo:hi, :].astype(BF)
            d_a = mm_t(dqkv_ref[l, rows, :], wqkv_ref[l])
            xhat = xhat1_ref[l, r, lo:hi, :]
            again_ref[l, 0] += gain_rows(d_a, xhat)
            d_x = dh_ref[r, lo:hi, :] + norm_back(d_a, gains_ref[l, 0:1, :], xhat, wide(rstd1_ref[l, r, lo:hi, :]))
            if l:
                dbuf_ref[r, lo:hi, :] = d_x
                gb_ref[0, rows, :] = d_x.astype(BF)
            else:
                end = min(hi, length)
                d0, d1 = d_x[: end - lo], dbuf_ref[r, lo:hi, :][: end - lo]
                dk_out_ref[r, lo:end, :] = jnp.where(first, d0, d1)
                ds_out_ref[r, lo:end, :] = jnp.where(first, d1, d0).astype(BF)

        order = [(probs, 0), (probs, 1), (values, 0), (queries, 0), (probs, 2), (values, 1), (queries, 1)]
        order += [(probs, 3), (values, 2), (queries, 2), (values, 3), (queries, 3)]
        return (
            [out]
            + [lambda f=f, b=BLOCKS[i]: f(*b) for f, i in order]
            + [lambda lo=lo, hi=hi: finish(lo, hi) for lo, hi in PARTS]
        )

    def turn(j, ref, l):
        left_ref[j] = ref[l].T

    def mlp_weights(l):
        def down(c):
            for j in (c, c + 1):
                cols = slice(256 * j, 256 * j + 256)
                adown_ref[l, :, cols] += mm(left_ref[0], m_ref[l, :, cols])

        def up(c):
            for j in (c, c + 1):
                cols = slice(256 * j, 256 * j + 256)
                aup_ref[l, :, cols] += mm(left_ref[1], du_ref[l, :, cols])

        return [
            lambda: turn(0, gb_ref, l), lambda: turn(1, b_ref, l),
            lambda: down(0), lambda: down(2), lambda: up(0), lambda: up(2),
        ]

    def attn_weights(l):
        def out_and_query():
            aout_ref[l] += mm(left_ref[2], dhb_ref[l])
            aqkv_ref[l, :, 0:256] += mm(left_ref[3], dqkv_ref[l, :, 0:256])

        def key_and_value():
            for j in (1, 2):
                cols = slice(256 * j, 256 * j + 256)
                aqkv_ref[l, :, cols] += mm(left_ref[3], dqkv_ref[l, :, cols])

        return [lambda: turn(2, o_ref, l), lambda: turn(3, a_ref, l), out_and_query, key_and_value]

    merged(load(0) + attn_forward(0, 0))
    merged(mlp_forward(0, 0), load(1) + attn_forward(1, 0))
    merged(attn_forward(0, 1), mlp_forward(1, 0))
    merged(mlp_forward(0, 1), attn_forward(1, 1))
    merged(mlp_backward(0, 1), mlp_forward(1, 1))
    merged(attn_backward(0, 1), mlp_backward(1, 1))
    merged(mlp_backward(0, 0), attn_backward(1, 1), mlp_weights(1))
    merged(attn_backward(0, 0), mlp_backward(1, 0), attn_weights(1))
    merged(attn_backward(1, 0), mlp_weights(0))
    merged(attn_weights(0))

    @pl.when(step == last)
    def _():
        for l, p_out, q_out in ((sec, pk_ref, qk_ref), (1 - sec, psend_ref, qsend_ref)):
            for j in range(3):
                p_out[256 * j : 256 * j + 256, :] = aqkv_ref[l, :, 256 * j : 256 * j + 256].astype(BF)
            p_out[768:1024, :] = aout_ref[l].astype(BF)
            for j in range(2):
                p_out[1024 + 256 * j : 1280 + 256 * j, :] = aup_ref[l, :, 256 * j : 256 * j + 256].astype(BF)
                q_out[256 * j : 256 * j + 256, :] = aup_ref[l, :, 512 + 256 * j : 768 + 256 * j].astype(BF)
            for j in range(4):
                q_out[512 + 256 * j : 768 + 256 * j, :] = adown_ref[l, :, 256 * j : 256 * j + 256].astype(BF).T
            row = lax.broadcasted_iota(jnp.int32, (16, D), 0)
            attn = jnp.sum(again_ref[l, 0], axis=0, keepdims=True)
            mlp = jnp.sum(again_ref[l, 1], axis=0, keepdims=True)
            p_out[1536:1552, :] = jnp.where(row == 0, attn, jnp.where(row == 1, mlp, 0.0)).astype(BF)


def local_step(section, x, cot, segments, gains, other_gains, mine, other):
    rows, length, _ = x.shape
    steps = rows // 2 // TWO
    place = lambda i, sec: (sec[0] * steps + i, 0, 0)
    tok = lambda w: pl.BlockSpec((TWO, length, w), place)
    row_out = pl.BlockSpec((TWO, length, D), lambda i, sec: (i, 0, 0))
    whole = lambda shape: pl.BlockSpec(shape, lambda i, sec: (0,) * len(shape), pipeline_mode=pl.Buffered(1))
    hbm = pl.BlockSpec(memory_space=pl.ANY)
    vm = pltpu.VMEM
    flat = lambda w: vm((2, TWO * LP, w), BF)
    shape = jax.ShapeDtypeStruct
    return pl.pallas_call(
        kernel,
        grid_spec=pltpu.PrefetchScalarGridSpec(
            num_scalar_prefetch=1,
            grid=(steps,),
            in_specs=[tok(D), tok(D), pl.BlockSpec((TWO, 1, segments.shape[2]), place), whole((2, D)), whole((2, D))] + [hbm] * 8,
            out_specs=[tok(D), row_out, tok(D), row_out, whole((1552, D)), whole((1536, D)), whole((1552, D)), whole((1536, D))],
            scratch_shapes=[
                vm((2, D, 3 * D), BF), vm((2, D, D), BF), vm((2, D, FF), BF), vm((2, FF, D), BF), pltpu.SemaphoreType.DMA((8,)),
                vm((2, 2, D), F32), vm((TWO, LP, 128), BF), vm((TWO, LP, 128), BF), vm((TWO, LP, D), BF), vm((TWO, LP, D), F32),
                vm((TWO, LP, D), F32),
                vm((2, TWO, LP, D), F32), vm((2, TWO, LP, 128), F32), vm((2, TWO, LP, D), F32), vm((2, TWO, LP, 128), F32),
                flat(D), flat(D), flat(D),
                vm((2, TWO, 2, 2 * LP, 128), BF), vm((2, TWO, LP, D), BF), vm((2, TWO, LP, D), BF),
                vm((2, TWO, 2, 2 * LP, D), BF), flat(FF), vm((2, TWO, LP, FF), BF),
                flat(D), flat(FF), vm((TWO, LP, D), F32), flat(D),
                vm((TWO, 2, 2 * LP, D), BF), flat(3 * D), vm((TWO, LP, D), F32), vm((TWO, LP, D), F32),
                vm((4, D, TWO * LP), BF), vm((2, D, 3 * D), F32), vm((2, D, D), F32), vm((2, D, FF), F32), vm((2, D, FF), F32),
                vm((2, 2, 8, D), F32),
            ],
        ),
        out_shape=[
            shape((rows, length, D), BF), shape((rows // 2, length, D), BF),
            shape((rows, length, D), F32), shape((rows // 2, length, D), BF),
            shape((1552, D), BF), shape((1536, D), BF), shape((1552, D), BF), shape((1536, D), BF),
        ],
        compiler_params=pltpu.CompilerParams(
            dimension_semantics=("arbitrary",), vmem_limit_bytes=60 * 1024 * 1024
        ),
    )(section, x, cot, segments, gains, other_gains, *mine, *other)


def partner(value):
    return lax.ppermute(value, "section", [(0, 1), (1, 0)])


def cross(value, count, bits):
    pairs = [(s * count + i, s * count + (i ^ (1 << bits[s]))) for s in range(2) for i in range(count)]
    return lax.ppermute(value, ("section", "dp"), pairs)


def add(a, b):
    return (a.astype(F32) + b.astype(F32)).astype(BF)


def sum_over_dp(parts, tail, section):
    count = lax.axis_size("dp")
    place = lax.axis_index("dp")
    depth = count.bit_length() - 1
    orders = [list(range(depth)), list(range(depth))]
    if depth > 2:
        orders[1][1], orders[1][2] = 2, 1
    swap = {0: 1, 1: 0} if depth > 1 else {}
    orders = [[(b, swap.get(b, b)) for b in order] for order in orders]
    sizes = [tail, 0]
    current = list(parts)
    uppers = [[], []]
    for stage in range(depth):
        got = []
        for part in range(2):
            bits = orders[part][stage]
            upper = jnp.where(section == 0, place >> bits[0], place >> bits[1]) & 1
            uppers[part].append(upper)
            value = current[part]
            main = value.shape[0] - sizes[part]
            send = lax.dynamic_slice_in_dim(value, (1 - upper) * (main // 2), main // 2, 0)
            if sizes[part]:
                send = jnp.concatenate([send, value[main:]], axis=0)
            got.append(cross(send, count, bits))
        for part in range(2):
            value = current[part]
            main = value.shape[0] - sizes[part]
            keep = lax.dynamic_slice_in_dim(value, uppers[part][stage] * (main // 2), main // 2, 0)
            if sizes[part]:
                keep = jnp.concatenate([keep, value[main:]], axis=0)
            current[part] = add(keep, got[part])
    rest = current[0][current[0].shape[0] - tail :]
    current[0] = current[0][: current[0].shape[0] - tail]
    halves = []
    for stage in reversed(range(depth)):
        got = [cross(current[part], count, orders[part][stage]) for part in range(2)]
        for part in range(2):
            low = uppers[part][stage] == 0
            pair = (jnp.where(low, current[part], got[part]), jnp.where(low, got[part], current[part]))
            if stage == 0:
                halves.append(pair)
            else:
                current[part] = jnp.concatenate(pair, axis=0)
    return halves, rest


def shards(
    layer_input, out_cotangent, segment_ids, gain_attn, weight_qkv, weight_out, gain_mlp, weight_up, weight_down
):
    section = lax.axis_index("section")
    rows, length, _ = layer_input.shape
    half = rows // 2
    gains = jnp.concatenate([gain_attn, gain_mlp], axis=0)
    mine = (weight_qkv, weight_out, weight_up, weight_down)
    other = tuple(partner(w) for w in mine)
    other_gains = partner(gains)
    segments = jnp.pad(segment_ids, ((0, 0), (0, 384 - length)), constant_values=-1)[:, None, :]
    acts, acts_send, grads, grads_send, first, second, first_send, second_send = local_step(
        section[None].astype(jnp.int32), layer_input, out_cotangent, segments,
        gains.astype(F32), other_gains.astype(F32), mine, other,
    )
    got = partner(first_send), partner(second_send)
    parts = add(first, got[0]), add(second, got[1])
    ((qkv, out_up), (up_down, down)), rest = sum_over_dp(parts, 16, section)
    there = (1 - section) * half
    activations = lax.dynamic_update_slice_in_dim(acts, partner(acts_send), there, 0)
    input_grads = lax.dynamic_update_slice_in_dim(grads, partner(grads_send).astype(F32), there, 0)
    side = lambda *blocks: jnp.concatenate(blocks, axis=1).astype(F32)
    return (
        activations[None],
        input_grads[None],
        side(qkv[0:256], qkv[256:512], qkv[512:768])[None],
        out_up[0:256].astype(F32)[None],
        side(out_up[256:512], out_up[512:768], up_down[0:256], up_down[256:512])[None],
        jnp.concatenate([up_down[512:768], down], axis=0).astype(F32)[None],
        rest[0].astype(F32)[None],
        rest[1].astype(F32)[None],
    )


def solution(mesh):
    placed = (
        P("dp", None, None),
        P("dp", None, None),
        P("dp", None),
        P("section", None),
        P("section", None, None),
        P("section", None, None),
        P("section", None),
        P("section", None, None),
        P("section", None, None),
    )
    return jax.shard_map(
        shards,
        mesh=mesh,
        in_specs=placed,
        out_specs=(
            P("section", "dp", None, None),
            P("section", "dp", None, None),
            P("section", None, None),
            P("section", None, None),
            P("section", None, None),
            P("section", None, None),
            P("section", None),
            P("section", None),
        ),
        check_vma=False,
    )
```

```python
import jax
import jax.numpy as jnp
from jax import lax
from jax.experimental import pallas as pl
from jax.experimental.pallas import tpu as pltpu
from jax.sharding import PartitionSpec as P

D = 256
FF = 1024
FRAME = 17
LP = 352
EPS = 1e-05
BIG = -(2.0**100)
BLOCKS = ((0, 112, 0, 128), (112, 240, 0, 256), (240, 304, 64, 320), (304, 352, 96, 352))
ERF = (7.97852379e-01, 3.64383569e-02, -1.13746830e-04, -3.20493527e-05, 1.18025665e-06)
TWO = 2
F32 = jnp.float32
BF = jnp.bfloat16


def mm(a, b):
    return jnp.dot(a, b, preferred_element_type=F32)


def mm_t(a, b):
    return lax.dot_general(a, b, (((1,), (1,)), ((), ())), preferred_element_type=F32)


def tmm(a, b):
    return lax.dot_general(a, b, (((0,), (0,)), ((), ())), preferred_element_type=F32)


def norm_stats(x):
    mean = jnp.sum(x, axis=-1, keepdims=True) * (1.0 / D)
    center = x - mean
    var = jnp.sum(center * center, axis=-1, keepdims=True) * (1.0 / D)
    rstd = lax.rsqrt(var + EPS)
    return center * rstd, rstd


def norm_back(d_out, gain, xhat, rstd):
    dy = d_out * gain
    s1 = jnp.sum(dy, axis=-1, keepdims=True) * (1.0 / D)
    s2 = jnp.sum(dy * xhat, axis=-1, keepdims=True) * (1.0 / D)
    return rstd * (dy - s1 - xhat * s2)


def gain_rows(d_out, xhat):
    prod = d_out * xhat
    return jnp.sum(prod.reshape(prod.shape[0] // 8, 8, D), axis=0)


def gelu_pair(u):
    u2 = u * u
    p = jnp.full_like(u, ERF[-1])
    for c in ERF[-2::-1]:
        p = p * u2 + c
    cdf = 0.5 + 0.5 * jnp.tanh(u * p)
    pdf = jnp.exp2(u2 * -0.7213475204444817 - 1.3257480647361593)
    return u * cdf, cdf + u * pdf


def two_heads(block, lane_low):
    zero = jnp.zeros_like(block)
    return jnp.concatenate(
        [jnp.where(lane_low, block, zero), jnp.where(lane_low, zero, block)], axis=0
    )


def pair_rows(p, q0, q1):
    return slice(4 * q0 + 2 * p * (q1 - q0), 4 * q0 + 2 * (p + 1) * (q1 - q0))


def one_row(stacked, n):
    mask = low_mask(n)
    return jnp.concatenate(
        [
            jnp.where(mask, stacked[:n, 0:128], stacked[n : 2 * n, 0:128]),
            jnp.where(mask, stacked[2 * n : 3 * n, 128:256], stacked[3 * n :, 128:256]),
        ],
        axis=1,
    )


def low_mask(n):
    return lax.broadcasted_iota(jnp.int32, (n, 128), 1) < 64


def merged(*lists):
    tagged = [((i + 0.5) / len(units), j, unit) for j, units in enumerate(lists) for i, unit in enumerate(units)]
    for _, _, unit in sorted(tagged, key=lambda t: t[:2]):
        unit()


def wide(column):
    return jnp.concatenate([column, column], axis=1)


PARTS = ((0, 176), (176, 352))
WHOLE = ((0, LP),)
PAIRS = ((0, slice(0, 128)), (1, slice(128, 256)))


def kernel(
    sec_ref, seg_ref, attn_mine, mlp_mine, attn_other, mlp_other, x_hbm, cot_hbm,
    wqkv_mine, wout_mine, wup_mine, wdown_mine, wqkv_other, wout_other, wup_other, wdown_other,
    yk_ref, ys_ref, dk_out_ref, ds_out_ref, pk_ref, qk_ref, psend_ref, qsend_ref,
    wqkv_ref, wout_ref, wup_ref, wdown_ref, wsem, insem, xin_ref, cin_ref, wide_ref, xrow_ref, crow_ref, seg_pad_ref, gains_ref, eq_ref, ek_ref, ybuf_ref, dbuf_ref,
    res_ref, xhat1_ref, rstd1_ref, xhat2_ref, rstd2_ref, a_ref, b_ref, o_ref, qs_ref, k_ref, v_ref,
    p_ref, m_ref, gp_ref, gb_ref, du_ref, dh_ref, dhb_ref, do_ref, prod_ref, dqkv_ref, dk_ref, dv_ref,
    left_ref, aqkv_ref, aout_ref, aup_ref, adown_ref, again_ref,
):
    step = pl.program_id(0)
    last = pl.num_programs(0) - 1
    sec = sec_ref[0]
    first = sec == 0
    length = x_hbm.shape[0]
    loads = [
        pltpu.make_async_copy(x_hbm, xin_ref, insem.at[0]),
        pltpu.make_async_copy(cot_hbm, cin_ref, insem.at[1]),
    ]

    def spread(tokens_ref, rows_ref):
        count = tokens_ref.shape[1]
        for p in range(2):
            wide_ref[p] = tokens_ref[:, :, 128 * p : 128 * p + 128].astype(F32).reshape(length * count, 128)
        for r in range(count // 2):
            rows_ref[r, LP - 16 : LP, :] = jnp.zeros((16, D), BF)
            for p in range(2):
                row = wide_ref[p, pl.ds(sec * (count // 2) + r, length, stride=count), :]
                rows_ref[r, 0:length, 128 * p : 128 * p + 128] = row.astype(BF)


    copies = []
    for mine, other, held in (
        (wqkv_mine, wqkv_other, wqkv_ref), (wout_mine, wout_other, wout_ref),
        (wup_mine, wup_other, wup_ref), (wdown_mine, wdown_other, wdown_ref),
    ):
        copies.append(pltpu.make_async_copy(mine.at[0], held.at[sec], wsem.at[len(copies)]))
        copies.append(pltpu.make_async_copy(other.at[0], held.at[1 - sec], wsem.at[len(copies)]))

    @pl.when(step == 0)
    def _():
        loads[0].start()
        for copy in copies:
            copy.start()
        loads[1].start()
        for n, (mine, other) in enumerate(((attn_mine, attn_other), (mlp_mine, mlp_other))):
            mine, other = mine[...].astype(F32), other[...].astype(F32)
            gains_ref[0, n : n + 1, :] = jnp.where(first, mine, other)
            gains_ref[1, n : n + 1, :] = jnp.where(first, other, mine)
        seg_pad_ref[...] = jnp.full(seg_pad_ref.shape, -1, jnp.int32)
        seg_pad_ref[:, 0:length] = seg_ref[...]
        for ref in (qs_ref, do_ref, aqkv_ref, aout_ref, aup_ref, adown_ref, again_ref):
            ref[...] = jnp.zeros_like(ref)
        loads[0].wait()
        spread(xin_ref, xrow_ref)
        for copy in copies[:4]:
            copy.wait()

    def load(r):
        def tokens(lo, hi):
            res_ref[r, lo:hi, :] = xrow_ref[TWO * step + r, lo:hi, :].astype(F32)

        def visibility():
            row = sec * (seg_ref.shape[0] // 2) + TWO * step + r
            seg = jnp.broadcast_to(seg_pad_ref[pl.ds(row, 1), :], (128, seg_pad_ref.shape[1])).astype(F32).T[:LP]
            lane = lax.broadcasted_iota(jnp.int32, (LP, 128), 1)
            token = lax.broadcasted_iota(jnp.int32, (LP, 128), 0)
            same = seg == (lane - 64).astype(F32)
            start = FRAME * lane
            here = jnp.logical_and(token >= start, token < start + FRAME)
            later = token >= start + FRAME
            other = jnp.logical_and(jnp.logical_not(same), lane < 68)
            eq_ref[r] = jnp.where(lane < 64, jnp.where(here, 1.0, 0.0), jnp.where(same, 1.0, 0.0)).astype(BF)
            ek_ref[r] = jnp.where(lane < 64, jnp.where(later, BIG, 0.0), jnp.where(other, BIG, 0.0)).astype(BF)

        return [lambda lo=lo, hi=hi: tokens(lo, hi) for lo, hi in PARTS] + [visibility]

    ones = jnp.ones((LP, 128), BF)

    def attn_forward(r, l):
        base = LP * r
        units = []

        def norm(lo, hi):
            xhat, rstd = norm_stats(res_ref[r, lo:hi, :])
            xhat1_ref[l, r, lo:hi, :] = xhat
            rstd1_ref[l, r, lo:hi, :] = jnp.broadcast_to(rstd, (hi - lo, 128))
            a_ref[l, base + lo : base + hi, :] = (xhat * gains_ref[l, 0:1, :]).astype(BF)

        def query():
            q = mm(a_ref[l, base : base + LP, :], wqkv_ref[l, :, 0:256]).astype(BF) * jnp.array(0.125, BF)
            for p, lanes in PAIRS:
                for q0, q1, _, _ in BLOCKS:
                    qs_ref[l, r, pair_rows(p, q0, q1), lanes] = two_heads(q[q0:q1, lanes], low_mask(q1 - q0))

        def key():
            k_ref[l, r] = mm(a_ref[l, base : base + LP, :], wqkv_ref[l, :, 256:512]).astype(BF)

        def value():
            v_ref[l, r] = mm(a_ref[l, base : base + LP, :], wqkv_ref[l, :, 512:768]).astype(BF)

        held = {}

        def scores(q0, q1, k0, k1):
            eq = eq_ref[r, q0:q1, :]
            eq = jnp.concatenate([eq, eq], axis=0)
            ek = ek_ref[r, k0:k1, :]
            held[q0] = [
                mm_t(
                    jnp.concatenate([qs_ref[l, r, pair_rows(p, q0, q1), lanes], eq], axis=1),
                    jnp.concatenate([k_ref[l, r, k0:k1, lanes], ek], axis=1),
                )
                for p, lanes in PAIRS
            ]

        def mix(q0, q1, k0, k1):
            n = q1 - q0
            probs = []
            for p, _ in PAIRS:
                s = held[q0][p]
                e = jnp.exp(s - jnp.max(s, axis=-1, keepdims=True))
                prob = (e * (1.0 / jnp.sum(e, axis=-1, keepdims=True))).astype(BF)
                p_ref[l, r, pair_rows(p, q0, q1), 0 : k1 - k0] = prob
                probs.append(prob)
            o = mm(jnp.concatenate(probs, axis=0), v_ref[l, r, k0:k1, :])
            o_ref[l, base + q0 : base + q1, :] = one_row(o, n).astype(BF)

        def out(lo, hi):
            h = res_ref[r, lo:hi, :] + mm(o_ref[l, base + lo : base + hi, :], wout_ref[l])
            res_ref[r, lo:hi, :] = h
            xhat, rstd = norm_stats(h)
            xhat2_ref[l, r, lo:hi, :] = xhat
            rstd2_ref[l, r, lo:hi, :] = jnp.broadcast_to(rstd, (hi - lo, 128))
            b_ref[l, base + lo : base + hi, :] = (xhat * gains_ref[l, 1:2, :]).astype(BF)

        units += [lambda lo=lo, hi=hi: norm(lo, hi) for lo, hi in PARTS]
        units += [query, key, value]
        first = [lambda b=b: scores(*b) for b in BLOCKS]
        second = [lambda b=b: mix(*b) for b in BLOCKS]
        units += [first[0], first[1], second[0], first[2], second[1], first[3], second[2], second[3]]
        units += [lambda lo=lo, hi=hi: out(lo, hi) for lo, hi in WHOLE]
        return units

    def mlp_forward(r, l):
        base = LP * r

        def chunk(c, lo, hi):
            rows = slice(base + lo, base + hi)
            ups = [mm(b_ref[l, rows, :], wup_ref[l, :, 256 * j : 256 * j + 256]) for j in (c, c + 1)]
            for j, u in zip((c, c + 1), ups):
                m, gp = gelu_pair(u)
                m_ref[l, rows, 256 * j : 256 * j + 256] = m.astype(BF)
                gp_ref[l, r, lo:hi, 256 * j : 256 * j + 256] = gp.astype(BF)

        def down(lo, hi):
            y = res_ref[r, lo:hi, :] + mm(m_ref[l, base + lo : base + hi, :], wdown_ref[l])
            y = y.astype(BF)
            if l == 0:
                ybuf_ref[r, lo:hi, :] = y
                res_ref[r, lo:hi, :] = y.astype(F32)
            else:
                end = min(hi, length)
                y0, y1 = ybuf_ref[r, lo:hi, :][: end - lo], y[: end - lo]
                yk_ref[r, lo:end, :] = jnp.where(first, y0, y1)
                ys_ref[r, lo:end, :] = jnp.where(first, y1, y0)

        return [lambda: chunk(0, 0, LP), lambda: chunk(2, 0, LP), lambda: down(0, LP)]

    def mlp_backward(r, l):
        base = LP * r

        def chunk(c, lo, hi):
            rows = slice(base + lo, base + hi)
            dms = [mm_t(gb_ref[l, rows, :], wdown_ref[l, 256 * j : 256 * j + 256, :]) for j in (c, c + 1)]
            for j, dm in zip((c, c + 1), dms):
                cols = slice(256 * j, 256 * j + 256)
                du_ref[l, rows, cols] = (dm * gp_ref[l, r, lo:hi, cols].astype(F32)).astype(BF)

        def back(lo, hi):
            rows = slice(base + lo, base + hi)
            d_b = mm_t(du_ref[l, rows, :], wup_ref[l])
            xhat = xhat2_ref[l, r, lo:hi, :]
            again_ref[l, 1] += gain_rows(d_b, xhat)
            d_h = gb_ref[l, rows, :].astype(F32) + norm_back(d_b, gains_ref[l, 1:2, :], xhat, wide(rstd2_ref[l, r, lo:hi, :]))
            dh_ref[r, lo:hi, :] = d_h
            dhb_ref[l, rows, :] = d_h.astype(BF)

        return (
            [lambda c=c, lo=lo, hi=hi: chunk(c, lo, hi) for c in (0, 2) for lo, hi in WHOLE]
            + [lambda lo=lo, hi=hi: back(lo, hi) for lo, hi in WHOLE]
        )

    def attn_backward(r, l):
        base = LP * r

        def out():
            d_o = mm_t(dhb_ref[l, base : base + LP, :], wout_ref[l]).astype(BF)
            prod = (-(d_o.astype(F32) * o_ref[l, base : base + LP, :].astype(F32))).astype(BF)
            for p, lanes in PAIRS:
                for q0, q1, _, _ in BLOCKS:
                    mask = low_mask(q1 - q0)
                    do_ref[r, pair_rows(p, q0, q1), lanes] = two_heads(d_o[q0:q1, lanes], mask)
                    prod_ref[r, pair_rows(p, q0, q1), :] = two_heads(prod[q0:q1, lanes], mask)
            dk_ref[r] = jnp.zeros((LP, D), F32)
            dv_ref[r] = jnp.zeros((LP, D), F32)

        held = {}

        def probs(q0, q1, k0, k1):
            held[q0] = [
                mm_t(
                    jnp.concatenate(
                        [do_ref[r, pair_rows(p, q0, q1), lanes], prod_ref[r, pair_rows(p, q0, q1), :]], axis=1
                    ),
                    jnp.concatenate([v_ref[l, r, k0:k1, lanes], ones[k0:k1]], axis=1),
                )
                for p, lanes in PAIRS
            ]

        def values(q0, q1, k0, k1):
            rows = slice(4 * q0, 4 * q1)
            dv_ref[r, k0:k1, :] += tmm(p_ref[l, r, rows, 0 : k1 - k0], do_ref[r, rows, :])

        def queries(q0, q1, k0, k1):
            n = q1 - q0
            ds = jnp.concatenate(
                [
                    (p_ref[l, r, pair_rows(p, q0, q1), 0 : k1 - k0].astype(F32) * held[q0][p]).astype(BF)
                    for p, _ in PAIRS
                ],
                axis=0,
            )
            dq = mm(ds, k_ref[l, r, k0:k1, :])
            dqkv_ref[l, base + q0 : base + q1, 0:256] = (one_row(dq, n) * 0.125).astype(BF)
            dk_ref[r, k0:k1, :] += tmm(ds, qs_ref[l, r, 4 * q0 : 4 * q1, :])

        def finish(lo, hi):
            rows = slice(base + lo, base + hi)
            dqkv_ref[l, rows, 256:512] = dk_ref[r, lo:hi, :].astype(BF)
            dqkv_ref[l, rows, 512:768] = dv_ref[r, lo:hi, :].astype(BF)
            d_a = mm_t(dqkv_ref[l, rows, :], wqkv_ref[l])
            xhat = xhat1_ref[l, r, lo:hi, :]
            again_ref[l, 0] += gain_rows(d_a, xhat)
            d_x = dh_ref[r, lo:hi, :] + norm_back(d_a, gains_ref[l, 0:1, :], xhat, wide(rstd1_ref[l, r, lo:hi, :]))
            if l:
                dbuf_ref[r, lo:hi, :] = d_x
                gb_ref[0, rows, :] = d_x.astype(BF)
            else:
                end = min(hi, length)
                d0, d1 = d_x[: end - lo], dbuf_ref[r, lo:hi, :][: end - lo]
                dk_out_ref[r, lo:end, :] = jnp.where(first, d0, d1)
                ds_out_ref[r, lo:end, :] = jnp.where(first, d1, d0).astype(BF)

        order = [(probs, 0), (probs, 1), (values, 0), (queries, 0), (probs, 2), (values, 1), (queries, 1)]
        order += [(probs, 3), (values, 2), (queries, 2), (values, 3), (queries, 3)]
        return (
            [out]
            + [lambda f=f, b=BLOCKS[i]: f(*b) for f, i in order]
            + [lambda lo=lo, hi=hi: finish(lo, hi) for lo, hi in WHOLE]
        )

    def turn(j, ref, l):
        left_ref[j] = ref[l].T

    def mlp_weights(l):
        def down(c):
            for j in (c, c + 1):
                cols = slice(256 * j, 256 * j + 256)
                adown_ref[l, :, cols] += mm(left_ref[0], m_ref[l, :, cols])

        def up(c):
            for j in (c, c + 1):
                cols = slice(256 * j, 256 * j + 256)
                aup_ref[l, :, cols] += mm(left_ref[1], du_ref[l, :, cols])

        return [
            lambda: turn(0, gb_ref, l), lambda: turn(1, b_ref, l),
            lambda: down(0), lambda: down(2), lambda: up(0), lambda: up(2),
        ]

    def attn_weights(l):
        def out_and_query():
            aout_ref[l] += mm(left_ref[2], dhb_ref[l])
            aqkv_ref[l, :, 0:256] += mm(left_ref[3], dqkv_ref[l, :, 0:256])

        def key_and_value():
            for j in (1, 2):
                cols = slice(256 * j, 256 * j + 256)
                aqkv_ref[l, :, cols] += mm(left_ref[3], dqkv_ref[l, :, cols])

        return [lambda: turn(2, o_ref, l), lambda: turn(3, a_ref, l), out_and_query, key_and_value]

    merged(load(0) + attn_forward(0, 0), load(1) + attn_forward(1, 0))

    @pl.when(step == 0)
    def _():
        for copy in copies[4:]:
            copy.wait()
        loads[1].wait()
        spread(cin_ref, crow_ref)

    merged(mlp_forward(0, 0), mlp_forward(1, 0))
    merged(attn_forward(0, 1), attn_forward(1, 1))
    merged(mlp_forward(0, 1), mlp_forward(1, 1))
    for r in range(TWO):
        gb_ref[1, LP * r : LP * r + LP, :] = crow_ref[TWO * step + r]
    merged(mlp_backward(0, 1), mlp_backward(1, 1))
    merged(mlp_weights(1))
    merged(attn_backward(0, 1), attn_backward(1, 1))
    merged(attn_weights(1))
    merged(mlp_backward(0, 0), mlp_backward(1, 0))
    merged(mlp_weights(0))
    merged(attn_backward(0, 0), attn_backward(1, 0))
    merged(attn_weights(0))

    @pl.when(step == last)
    def _():
        for l, p_out, q_out in ((sec, pk_ref, qk_ref), (1 - sec, psend_ref, qsend_ref)):
            for j in range(3):
                p_out[256 * j : 256 * j + 256, :] = aqkv_ref[l, :, 256 * j : 256 * j + 256].astype(BF)
            p_out[768:1024, :] = aout_ref[l].astype(BF)
            for j in range(2):
                p_out[1024 + 256 * j : 1280 + 256 * j, :] = aup_ref[l, :, 256 * j : 256 * j + 256].astype(BF)
                q_out[256 * j : 256 * j + 256, :] = aup_ref[l, :, 512 + 256 * j : 768 + 256 * j].astype(BF)
            for j in range(4):
                q_out[512 + 256 * j : 768 + 256 * j, :] = adown_ref[l, :, 256 * j : 256 * j + 256].astype(BF).T
            row = lax.broadcasted_iota(jnp.int32, (16, D), 0)
            attn = jnp.sum(again_ref[l, 0], axis=0, keepdims=True)
            mlp = jnp.sum(again_ref[l, 1], axis=0, keepdims=True)
            p_out[1536:1552, :] = jnp.where(row == 0, attn, jnp.where(row == 1, mlp, 0.0)).astype(BF)


def local_step(section, x, cot, segments, gains, other_gains, mine, other):
    length, rows, _ = x.shape
    steps = rows // 2 // TWO
    row_out = pl.BlockSpec((TWO, length, D), lambda i, sec: (i, 0, 0))
    whole = lambda shape: pl.BlockSpec(shape, lambda i, sec: (0,) * len(shape), pipeline_mode=pl.Buffered(1))
    hbm = pl.BlockSpec(memory_space=pl.ANY)
    vm = pltpu.VMEM
    flat = lambda w: vm((2, TWO * LP, w), BF)
    shape = jax.ShapeDtypeStruct
    return pl.pallas_call(
        kernel,
        grid_spec=pltpu.PrefetchScalarGridSpec(
            num_scalar_prefetch=1,
            grid=(steps,),
            in_specs=[whole(segments.shape)] + [whole((1, D))] * 4 + [hbm] * 10,
            out_specs=[row_out, row_out, row_out, row_out, whole((1552, D)), whole((1536, D)), whole((1552, D)), whole((1536, D))],
            scratch_shapes=[
                vm((2, D, 3 * D), BF), vm((2, D, D), BF), vm((2, D, FF), BF), vm((2, FF, D), BF), pltpu.SemaphoreType.DMA((8,)), pltpu.SemaphoreType.DMA((2,)), vm(x.shape, BF), vm(x.shape, BF),
                vm((2, length * rows, 128), F32), vm((rows // 2, LP, D), BF), vm((rows // 2, LP, D), BF), vm((rows, 384), jnp.int32),
                vm((2, 2, D), F32), vm((TWO, LP, 128), BF), vm((TWO, LP, 128), BF), vm((TWO, LP, D), BF), vm((TWO, LP, D), F32),
                vm((TWO, LP, D), F32),
                vm((2, TWO, LP, D), F32), vm((2, TWO, LP, 128), F32), vm((2, TWO, LP, D), F32), vm((2, TWO, LP, 128), F32),
                flat(D), flat(D), flat(D),
                vm((2, TWO, 4 * LP, D), BF), vm((2, TWO, LP, D), BF), vm((2, TWO, LP, D), BF),
                vm((2, TWO, 4 * LP, D), BF), flat(FF), vm((2, TWO, LP, FF), BF),
                flat(D), flat(FF), vm((TWO, LP, D), F32), flat(D),
                vm((TWO, 4 * LP, D), BF), vm((TWO, 4 * LP, 128), BF), flat(3 * D), vm((TWO, LP, D), F32), vm((TWO, LP, D), F32),
                vm((4, D, TWO * LP), BF), vm((2, D, 3 * D), F32), vm((2, D, D), F32), vm((2, D, FF), F32), vm((2, D, FF), F32),
                vm((2, 2, 8, D), F32),
            ],
        ),
        out_shape=[
            shape((rows // 2, length, D), BF), shape((rows // 2, length, D), BF),
            shape((rows // 2, length, D), F32), shape((rows // 2, length, D), BF),
            shape((1552, D), BF), shape((1536, D), BF), shape((1552, D), BF), shape((1536, D), BF),
        ],
        compiler_params=pltpu.CompilerParams(
            dimension_semantics=("arbitrary",), vmem_limit_bytes=60 * 1024 * 1024
        ),
    )(section, segments, *gains, *other_gains, x, cot, *mine, *other)


def partner(value):
    return lax.ppermute(value, "section", [(0, 1), (1, 0)])


def cross(value, count, bits):
    pairs = [(s * count + i, s * count + (i ^ (1 << bits[s]))) for s in range(2) for i in range(count)]
    return lax.ppermute(value, ("section", "dp"), pairs)


def add(a, b):
    return (a.astype(F32) + b.astype(F32)).astype(BF)


def sum_over_dp(parts, tail, section):
    count = lax.axis_size("dp")
    place = lax.axis_index("dp")
    depth = count.bit_length() - 1
    orders = [list(range(depth)), list(range(depth))]
    if depth > 2:
        orders[1][1], orders[1][2] = 2, 1
    swap = {0: 1, 1: 0} if depth > 1 else {}
    orders = [[(b, swap.get(b, b)) for b in order] for order in orders]
    sizes = [tail, 0]
    current = list(parts)
    uppers = [[], []]
    for stage in range(depth):
        got = []
        for part in range(2):
            bits = orders[part][stage]
            upper = jnp.where(section == 0, place >> bits[0], place >> bits[1]) & 1
            uppers[part].append(upper)
            value = current[part]
            main = value.shape[0] - sizes[part]
            send = lax.dynamic_slice_in_dim(value, (1 - upper) * (main // 2), main // 2, 0)
            if sizes[part]:
                send = jnp.concatenate([send, value[main:]], axis=0)
            got.append(cross(send, count, bits))
        for part in range(2):
            value = current[part]
            main = value.shape[0] - sizes[part]
            keep = lax.dynamic_slice_in_dim(value, uppers[part][stage] * (main // 2), main // 2, 0)
            if sizes[part]:
                keep = jnp.concatenate([keep, value[main:]], axis=0)
            current[part] = add(keep, got[part])
    rest = current[0][current[0].shape[0] - tail :]
    current[0] = current[0][: current[0].shape[0] - tail]
    halves = []
    for stage in reversed(range(depth)):
        got = [cross(current[part], count, orders[part][stage]) for part in range(2)]
        for part in range(2):
            low = uppers[part][stage] == 0
            pair = (jnp.where(low, current[part], got[part]), jnp.where(low, got[part], current[part]))
            if stage == 0:
                halves.append(pair)
            else:
                current[part] = jnp.concatenate(pair, axis=0)
    return halves, rest


def shards(
    layer_input, out_cotangent, segment_ids, gain_attn, weight_qkv, weight_out, gain_mlp, weight_up, weight_down
):
    section = lax.axis_index("section")
    gains = (gain_attn, gain_mlp)
    mine = (weight_qkv, weight_out, weight_up, weight_down)
    other = tuple(partner(w) for w in mine)
    other_gains = tuple(partner(g) for g in gains)
    acts, acts_send, grads, grads_send, first, second, first_send, second_send = local_step(
        section[None].astype(jnp.int32), layer_input.swapaxes(0, 1), out_cotangent.swapaxes(0, 1), segment_ids,
        gains, other_gains, mine, other,
    )
    got = partner(first_send), partner(second_send)
    parts = add(first, got[0]), add(second, got[1])
    low = section == 0

    def whole_rows(keep, got):
        return jnp.concatenate([jnp.where(low, keep, got), jnp.where(low, got, keep)], axis=0)

    activations = whole_rows(acts, partner(acts_send))
    input_grads = whole_rows(grads, partner(grads_send).astype(F32))
    ((qkv, out_up), (up_down, down)), rest = sum_over_dp(parts, 16, section)
    side = lambda *blocks: jnp.concatenate(blocks, axis=1).astype(F32)
    return (
        activations[None],
        input_grads[None],
        side(qkv[0:256], qkv[256:512], qkv[512:768])[None],
        out_up[0:256].astype(F32)[None],
        side(out_up[256:512], out_up[512:768], up_down[0:256], up_down[256:512])[None],
        jnp.concatenate([up_down[512:768], down], axis=0).astype(F32)[None],
        rest[0].astype(F32)[None],
        rest[1].astype(F32)[None],
    )


def solution(mesh):
    placed = (
        P("dp", None, None),
        P("dp", None, None),
        P("dp", None),
        P("section", None),
        P("section", None, None),
        P("section", None, None),
        P("section", None),
        P("section", None, None),
        P("section", None, None),
    )
    return jax.shard_map(
        shards,
        mesh=mesh,
        in_specs=placed,
        out_specs=(
            P("section", "dp", None, None),
            P("section", "dp", None, None),
            P("section", None, None),
            P("section", None, None),
            P("section", None, None),
            P("section", None, None),
            P("section", None),
            P("section", None),
        ),
        check_vma=False,
    )
```

```python
import jax
import jax.numpy as jnp
from jax import lax
from jax.experimental import pallas as pl
from jax.experimental.pallas import tpu as pltpu
from jax.sharding import PartitionSpec as P

D = 256
FF = 1024
FRAME = 17
LP = 352
EPS = 1e-05
BIG = -(2.0**100)
BLOCKS = ((0, 112, 0, 128), (112, 240, 0, 256), (240, 304, 64, 320), (304, 352, 96, 352))
ODDS = (-2.296875, -0.10888671875, 0.00135040283203125, -1.1146068572998047e-05)
TWO = 2
HALF = 1536
F32 = jnp.float32
BF = jnp.bfloat16


def mm(a, b):
    return jnp.dot(a, b, preferred_element_type=F32)


def mm_t(a, b):
    return lax.dot_general(a, b, (((1,), (1,)), ((), ())), preferred_element_type=F32)


def tmm(a, b):
    return lax.dot_general(a, b, (((0,), (0,)), ((), ())), preferred_element_type=F32)


def norm_stats(x):
    mean = jnp.sum(x, axis=-1, keepdims=True) * (1.0 / D)
    center = x - mean
    var = jnp.sum(center * center, axis=-1, keepdims=True) * (1.0 / D)
    rstd = lax.rsqrt(var + EPS)
    return center * rstd, rstd


def norm_back(d_out, gain, xhat, rstd):
    dy = d_out * gain
    s1 = jnp.sum(dy, axis=-1, keepdims=True) * (1.0 / D)
    s2 = jnp.sum(dy * xhat, axis=-1, keepdims=True) * (1.0 / D)
    return rstd * (dy - s1 - xhat * s2)


def gain_rows(d_out, xhat):
    prod = d_out * xhat
    return jnp.sum(prod.reshape(prod.shape[0] // 8, 8, D), axis=0)


def gelu_pair(u):
    low = lambda value: jnp.array(value, BF)
    u = u.astype(BF)
    u2 = u * u
    x = jnp.minimum(u2, low(25.0))
    p = ((x * low(ODDS[3]) + low(ODDS[2])) * x + low(ODDS[1])) * x + low(ODDS[0])
    cdf = pl.reciprocal(low(1.0) + jnp.exp2(u * p), approx=True)
    pdf = jnp.exp2(u2 * low(-0.7213475204444817) - low(1.3257480647361593))
    return u * cdf, cdf + u * pdf


def two_heads(block, lane_low):
    zero = jnp.zeros_like(block)
    return jnp.concatenate(
        [jnp.where(lane_low, block, zero), jnp.where(lane_low, zero, block)], axis=0
    )


def pair_rows(p, q0, q1):
    return slice(4 * q0 + 2 * p * (q1 - q0), 4 * q0 + 2 * (p + 1) * (q1 - q0))


def one_row(stacked, n):
    mask = low_mask(n)
    return jnp.concatenate(
        [
            jnp.where(mask, stacked[:n, 0:128], stacked[n : 2 * n, 0:128]),
            jnp.where(mask, stacked[2 * n : 3 * n, 128:256], stacked[3 * n :, 128:256]),
        ],
        axis=1,
    )


def low_mask(n):
    return lax.broadcasted_iota(jnp.int32, (n, 128), 1) < 64


def merged(*lists):
    tagged = [((i + 0.5) / len(units), j, unit) for j, units in enumerate(lists) for i, unit in enumerate(units)]
    for _, _, unit in sorted(tagged, key=lambda t: t[:2]):
        unit()


def wide(column):
    return jnp.concatenate([column, column], axis=1)


PARTS = ((0, 176), (176, 352))
WHOLE = ((0, LP),)
PAIRS = ((0, slice(0, 128)), (1, slice(128, 256)))


def kernel(
    sec_ref, x_ref, cot_ref, eq_ref, ek_ref, gains_mine, gains_other,
    wqkv_mine, wout_mine, wup_mine, wdown_mine, wqkv_other, wout_other, wup_other, wdown_other,
    yk_ref, ys_ref, dk_out_ref, ds_out_ref, pkeep_hbm, qkeep_hbm, psend_hbm, qsend_hbm,
    wqkv_ref, wout_ref, wup_ref, wdown_ref, wsem, outsem, grads_ref, gains_ref, ybuf_ref, dbuf_ref,
    res_ref, xhat1_ref, rstd1_ref, xhat2_ref, rstd2_ref, a_ref, b_ref, o_ref, qs_ref, k_ref, v_ref,
    p_ref, m_ref, gp_ref, gb_ref, du_ref, dh_ref, dhb_ref, do_ref, prod_ref, dqkv_ref, dk_ref, dv_ref,
    left_ref, aqkv_ref, aout_ref, aup_ref, adown_ref, again_ref,
):
    step = pl.program_id(0)
    last = pl.num_programs(0) - 1
    sec = sec_ref[0]
    first = sec == 0
    length = yk_ref.shape[1]

    copies = []
    for mine, other, held in (
        (wqkv_mine, wqkv_other, wqkv_ref), (wout_mine, wout_other, wout_ref),
        (wup_mine, wup_other, wup_ref), (wdown_mine, wdown_other, wdown_ref),
    ):
        copies.append(pltpu.make_async_copy(mine.at[0], held.at[sec], wsem.at[len(copies)]))
        copies.append(pltpu.make_async_copy(other.at[0], held.at[1 - sec], wsem.at[len(copies)]))

    @pl.when(step == 0)
    def _():
        for copy in copies:
            copy.start()
        mine, other = gains_mine[...].astype(F32), gains_other[...].astype(F32)
        gains_ref[0] = jnp.where(first, mine, other)
        gains_ref[1] = jnp.where(first, other, mine)
        for ref in (qs_ref, do_ref, aqkv_ref, aout_ref, aup_ref, adown_ref, again_ref):
            ref[...] = jnp.zeros_like(ref)
        for copy in copies[:4]:
            copy.wait()

    def load(r):
        def tokens(lo, hi):
            res_ref[r, lo:hi, :] = x_ref[r, lo:hi, :].astype(F32)

        return [lambda lo=lo, hi=hi: tokens(lo, hi) for lo, hi in PARTS]

    ones = jnp.ones((LP, 128), BF)

    def attn_forward(r, l):
        base = LP * r
        units = []

        def norm(lo, hi):
            xhat, rstd = norm_stats(res_ref[r, lo:hi, :])
            xhat1_ref[l, r, lo:hi, :] = xhat
            rstd1_ref[l, r, lo:hi, :] = jnp.broadcast_to(rstd, (hi - lo, 128))
            a_ref[l, base + lo : base + hi, :] = (xhat * gains_ref[l, 0:1, :]).astype(BF)

        def query():
            q = mm(a_ref[l, base : base + LP, :], wqkv_ref[l, :, 0:256]).astype(BF) * jnp.array(0.125, BF)
            for p, lanes in PAIRS:
                for q0, q1, _, _ in BLOCKS:
                    qs_ref[l, r, pair_rows(p, q0, q1), lanes] = two_heads(q[q0:q1, lanes], low_mask(q1 - q0))

        def key():
            k_ref[l, r] = mm(a_ref[l, base : base + LP, :], wqkv_ref[l, :, 256:512]).astype(BF)

        def value():
            v_ref[l, r] = mm(a_ref[l, base : base + LP, :], wqkv_ref[l, :, 512:768]).astype(BF)

        held = {}

        def scores(q0, q1, k0, k1):
            eq = eq_ref[r, q0:q1, :]
            eq = jnp.concatenate([eq, eq], axis=0)
            ek = ek_ref[r, k0:k1, :]
            held[q0] = [
                mm_t(
                    jnp.concatenate([qs_ref[l, r, pair_rows(p, q0, q1), lanes], eq], axis=1),
                    jnp.concatenate([k_ref[l, r, k0:k1, lanes], ek], axis=1),
                )
                for p, lanes in PAIRS
            ]

        def mix(q0, q1, k0, k1):
            n = q1 - q0
            probs = []
            for p, _ in PAIRS:
                s = held[q0][p]
                e = jnp.exp(s - jnp.max(s, axis=-1, keepdims=True))
                prob = (e * (1.0 / jnp.sum(e, axis=-1, keepdims=True))).astype(BF)
                p_ref[l, r, pair_rows(p, q0, q1), 0 : k1 - k0] = prob
                probs.append(prob)
            o = mm(jnp.concatenate(probs, axis=0), v_ref[l, r, k0:k1, :])
            o_ref[l, base + q0 : base + q1, :] = one_row(o, n).astype(BF)

        def out(lo, hi):
            h = res_ref[r, lo:hi, :] + mm(o_ref[l, base + lo : base + hi, :], wout_ref[l])
            res_ref[r, lo:hi, :] = h
            xhat, rstd = norm_stats(h)
            xhat2_ref[l, r, lo:hi, :] = xhat
            rstd2_ref[l, r, lo:hi, :] = jnp.broadcast_to(rstd, (hi - lo, 128))
            b_ref[l, base + lo : base + hi, :] = (xhat * gains_ref[l, 1:2, :]).astype(BF)

        units += [lambda lo=lo, hi=hi: norm(lo, hi) for lo, hi in PARTS]
        units += [query, key, value]
        first = [lambda b=b: scores(*b) for b in BLOCKS]
        second = [lambda b=b: mix(*b) for b in BLOCKS]
        units += [first[0], first[1], second[0], first[2], second[1], first[3], second[2], second[3]]
        units += [lambda lo=lo, hi=hi: out(lo, hi) for lo, hi in WHOLE]
        return units

    def mlp_forward(r, l):
        base = LP * r

        def chunk(c, lo, hi):
            rows = slice(base + lo, base + hi)
            ups = [mm(b_ref[l, rows, :], wup_ref[l, :, 256 * j : 256 * j + 256]) for j in (c, c + 1)]
            for j, u in zip((c, c + 1), ups):
                m, gp = gelu_pair(u)
                m_ref[l, rows, 256 * j : 256 * j + 256] = m.astype(BF)
                gp_ref[l, r, lo:hi, 256 * j : 256 * j + 256] = gp.astype(BF)

        def down(lo, hi):
            y = res_ref[r, lo:hi, :] + mm(m_ref[l, base + lo : base + hi, :], wdown_ref[l])
            y = y.astype(BF)
            if l == 0:
                ybuf_ref[r, lo:hi, :] = y
                res_ref[r, lo:hi, :] = y.astype(F32)
            else:
                end = min(hi, length)
                y0, y1 = ybuf_ref[r, lo:hi, :][: end - lo], y[: end - lo]
                yk_ref[r, lo:end, :] = jnp.where(first, y0, y1)
                ys_ref[r, lo:end, :] = jnp.where(first, y1, y0)

        return [lambda: chunk(0, 0, LP), lambda: chunk(2, 0, LP), lambda: down(0, LP)]

    def mlp_backward(r, l):
        base = LP * r

        def chunk(c, lo, hi):
            rows = slice(base + lo, base + hi)
            dms = [mm_t(gb_ref[l, rows, :], wdown_ref[l, 256 * j : 256 * j + 256, :]) for j in (c, c + 1)]
            for j, dm in zip((c, c + 1), dms):
                cols = slice(256 * j, 256 * j + 256)
                du_ref[l, rows, cols] = (dm * gp_ref[l, r, lo:hi, cols].astype(F32)).astype(BF)

        def back(lo, hi):
            rows = slice(base + lo, base + hi)
            d_b = mm_t(du_ref[l, rows, :], wup_ref[l])
            xhat = xhat2_ref[l, r, lo:hi, :]
            again_ref[l, 1] += gain_rows(d_b, xhat)
            d_h = gb_ref[l, rows, :].astype(F32) + norm_back(d_b, gains_ref[l, 1:2, :], xhat, wide(rstd2_ref[l, r, lo:hi, :]))
            dh_ref[r, lo:hi, :] = d_h
            dhb_ref[l, rows, :] = d_h.astype(BF)

        return (
            [lambda c=c, lo=lo, hi=hi: chunk(c, lo, hi) for c in (0, 2) for lo, hi in WHOLE]
            + [lambda lo=lo, hi=hi: back(lo, hi) for lo, hi in WHOLE]
        )

    def attn_backward(r, l):
        base = LP * r

        def out():
            d_o = mm_t(dhb_ref[l, base : base + LP, :], wout_ref[l]).astype(BF)
            prod = (-(d_o.astype(F32) * o_ref[l, base : base + LP, :].astype(F32))).astype(BF)
            for p, lanes in PAIRS:
                for q0, q1, _, _ in BLOCKS:
                    mask = low_mask(q1 - q0)
                    do_ref[r, pair_rows(p, q0, q1), lanes] = two_heads(d_o[q0:q1, lanes], mask)
                    prod_ref[r, pair_rows(p, q0, q1), :] = two_heads(prod[q0:q1, lanes], mask)
            dk_ref[r] = jnp.zeros((LP, D), F32)
            dv_ref[r] = jnp.zeros((LP, D), F32)

        held = {}

        def probs(q0, q1, k0, k1):
            held[q0] = [
                mm_t(
                    jnp.concatenate(
                        [do_ref[r, pair_rows(p, q0, q1), lanes], prod_ref[r, pair_rows(p, q0, q1), :]], axis=1
                    ),
                    jnp.concatenate([v_ref[l, r, k0:k1, lanes], ones[k0:k1]], axis=1),
                )
                for p, lanes in PAIRS
            ]

        def values(q0, q1, k0, k1):
            rows = slice(4 * q0, 4 * q1)
            dv_ref[r, k0:k1, :] += tmm(p_ref[l, r, rows, 0 : k1 - k0], do_ref[r, rows, :])

        def queries(q0, q1, k0, k1):
            n = q1 - q0
            ds = jnp.concatenate(
                [
                    (p_ref[l, r, pair_rows(p, q0, q1), 0 : k1 - k0].astype(F32) * held[q0][p]).astype(BF)
                    for p, _ in PAIRS
                ],
                axis=0,
            )
            dq = mm(ds, k_ref[l, r, k0:k1, :])
            dqkv_ref[l, base + q0 : base + q1, 0:256] = (one_row(dq, n) * 0.125).astype(BF)
            dk_ref[r, k0:k1, :] += tmm(ds, qs_ref[l, r, 4 * q0 : 4 * q1, :])

        def finish(lo, hi):
            rows = slice(base + lo, base + hi)
            dqkv_ref[l, rows, 256:512] = dk_ref[r, lo:hi, :].astype(BF)
            dqkv_ref[l, rows, 512:768] = dv_ref[r, lo:hi, :].astype(BF)
            d_a = mm_t(dqkv_ref[l, rows, :], wqkv_ref[l])
            xhat = xhat1_ref[l, r, lo:hi, :]
            again_ref[l, 0] += gain_rows(d_a, xhat)
            d_x = dh_ref[r, lo:hi, :] + norm_back(d_a, gains_ref[l, 0:1, :], xhat, wide(rstd1_ref[l, r, lo:hi, :]))
            if l:
                dbuf_ref[r, lo:hi, :] = d_x
                gb_ref[0, rows, :] = d_x.astype(BF)
            else:
                end = min(hi, length)
                d0, d1 = d_x[: end - lo], dbuf_ref[r, lo:hi, :][: end - lo]
                dk_out_ref[r, lo:end, :] = jnp.where(first, d0, d1)
                ds_out_ref[r, lo:end, :] = jnp.where(first, d1, d0).astype(BF)

        order = [(probs, 0), (probs, 1), (values, 0), (queries, 0), (probs, 2), (values, 1), (queries, 1)]
        order += [(probs, 3), (values, 2), (queries, 2), (values, 3), (queries, 3)]
        return (
            [out]
            + [lambda f=f, b=BLOCKS[i]: f(*b) for f, i in order]
            + [lambda lo=lo, hi=hi: finish(lo, hi) for lo, hi in WHOLE]
        )

    def turn(j, ref, l):
        left_ref[j] = ref[l].T

    def mlp_weights(l):
        def down(c):
            for j in (c, c + 1):
                cols = slice(256 * j, 256 * j + 256)
                adown_ref[l, :, cols] += mm(left_ref[0], m_ref[l, :, cols])

        def up(c):
            for j in (c, c + 1):
                cols = slice(256 * j, 256 * j + 256)
                aup_ref[l, :, cols] += mm(left_ref[1], du_ref[l, :, cols])

        return [
            lambda: turn(0, gb_ref, l), lambda: turn(1, b_ref, l),
            lambda: down(0), lambda: down(2), lambda: up(0), lambda: up(2),
        ]

    def attn_weights(l):
        def out_and_query():
            aout_ref[l] += mm(left_ref[2], dhb_ref[l])
            aqkv_ref[l, :, 0:256] += mm(left_ref[3], dqkv_ref[l, :, 0:256])

        def key_and_value():
            for j in (1, 2):
                cols = slice(256 * j, 256 * j + 256)
                aqkv_ref[l, :, cols] += mm(left_ref[3], dqkv_ref[l, :, cols])

        return [lambda: turn(2, o_ref, l), lambda: turn(3, a_ref, l), out_and_query, key_and_value]

    merged(load(0) + attn_forward(0, 0), load(1) + attn_forward(1, 0))

    @pl.when(step == 0)
    def _():
        for copy in copies[4:]:
            copy.wait()

    merged(mlp_forward(0, 0), mlp_forward(1, 0))
    merged(attn_forward(0, 1), attn_forward(1, 1))
    merged(mlp_forward(0, 1), mlp_forward(1, 1))
    for r in range(TWO):
        gb_ref[1, LP * r : LP * r + LP, :] = cot_ref[r]
    merged(mlp_backward(0, 1), mlp_backward(1, 1))
    merged(mlp_weights(1))
    merged(attn_backward(0, 1), attn_backward(1, 1))
    merged(attn_weights(1))
    merged(mlp_backward(0, 0), mlp_backward(1, 0))
    merged(mlp_weights(0))
    merged(attn_backward(0, 0), attn_backward(1, 0))
    merged(attn_weights(0))

    @pl.when(step == last)
    def _():
        copies = []

        def hand(n, lo, rows, out):
            copies.append(pltpu.make_async_copy(grads_ref.at[n, pl.ds(lo, rows)], out, outsem.at[len(copies)]))
            copies[-1].start()

        for n, l, p_out, q_out in ((0, 1 - sec, psend_hbm, qsend_hbm), (1, sec, pkeep_hbm, qkeep_hbm)):
            for j in range(3):
                grads_ref[n, 256 * j : 256 * j + 256, :] = aqkv_ref[l, :, 256 * j : 256 * j + 256].astype(BF)
            grads_ref[n, 768:1024, :] = aout_ref[l].astype(BF)
            for j in range(2):
                grads_ref[n, 1024 + 256 * j : 1280 + 256 * j, :] = aup_ref[l, :, 256 * j : 256 * j + 256].astype(BF)
            row = lax.broadcasted_iota(jnp.int32, (16, D), 0)
            attn = jnp.sum(again_ref[l, 0], axis=0, keepdims=True)
            mlp = jnp.sum(again_ref[l, 1], axis=0, keepdims=True)
            grads_ref[n, HALF : HALF + 16, :] = jnp.where(row == 0, attn, jnp.where(row == 1, mlp, 0.0)).astype(BF)
            hand(n, 0, HALF + 16, p_out)
            for j in range(2):
                grads_ref[n, 1552 + 256 * j : 1808 + 256 * j, :] = aup_ref[l, :, 512 + 256 * j : 768 + 256 * j].astype(BF)
            for j in range(4):
                grads_ref[n, 2064 + 256 * j : 2320 + 256 * j, :] = adown_ref[l, :, 256 * j : 256 * j + 256].astype(BF).T
            hand(n, HALF + 16, HALF, q_out)
        for copy in copies:
            copy.wait()


def spread(sec_ref, seg_ref, x_hbm, cot_hbm, x_out, cot_out, eq_ref, ek_ref, x_ref, cot_ref, wide_ref, seg_pad_ref, sem):
    length, count, _ = x_ref.shape
    begin = sec_ref[0] * (count // 2)
    copies = [pltpu.make_async_copy(x_hbm, x_ref, sem.at[0]), pltpu.make_async_copy(cot_hbm, cot_ref, sem.at[1])]
    for copy in copies:
        copy.start()
    seg_pad_ref[...] = jnp.full(seg_pad_ref.shape, -1, jnp.int32)
    seg_pad_ref[:, 0:length] = seg_ref[...]
    lane = lax.broadcasted_iota(jnp.int32, (LP, 128), 1)
    token = lax.broadcasted_iota(jnp.int32, (LP, 128), 0)
    here = jnp.logical_and(token >= FRAME * lane, token < FRAME * lane + FRAME)
    later = token >= FRAME * lane + FRAME
    for r in range(count // 2):
        seg = jnp.broadcast_to(seg_pad_ref[pl.ds(begin + r, 1), :], (128, seg_pad_ref.shape[1])).astype(F32).T[:LP]
        same = seg == (lane - 64).astype(F32)
        other = jnp.logical_and(jnp.logical_not(same), lane < 68)
        eq_ref[r] = jnp.where(lane < 64, jnp.where(here, 1.0, 0.0), jnp.where(same, 1.0, 0.0)).astype(BF)
        ek_ref[r] = jnp.where(lane < 64, jnp.where(later, BIG, 0.0), jnp.where(other, BIG, 0.0)).astype(BF)
    for copy, taken, out in ((copies[0], x_ref, x_out), (copies[1], cot_ref, cot_out)):
        copy.wait()
        for p in range(2):
            wide_ref[p] = taken[:, :, 128 * p : 128 * p + 128].astype(F32).reshape(length * count, 128)
        for r in range(count // 2):
            out[r, LP - 16 : LP, :] = jnp.zeros((16, D), BF)
            for p in range(2):
                row = wide_ref[p, pl.ds(begin + r, length, stride=count), :]
                out[r, 0:length, 128 * p : 128 * p + 128] = row.astype(BF)


def prepare(section, x, cot, segments):
    length, rows, _ = x.shape
    hbm = pl.BlockSpec(memory_space=pl.ANY)
    vmem = pl.BlockSpec(memory_space=pltpu.VMEM)
    vm = pltpu.VMEM
    tokens = jax.ShapeDtypeStruct((rows // 2, LP, D), BF)
    columns = jax.ShapeDtypeStruct((rows // 2, LP, 128), BF)
    return pl.pallas_call(
        spread,
        in_specs=[pl.BlockSpec(memory_space=pltpu.SMEM), vmem, hbm, hbm],
        out_specs=[vmem] * 4,
        out_shape=[tokens, tokens, columns, columns],
        scratch_shapes=[
            vm(x.shape, BF), vm(x.shape, BF), vm((2, length * rows, 128), F32), vm((rows, 384), jnp.int32),
            pltpu.SemaphoreType.DMA((2,)),
        ],
        compiler_params=pltpu.CompilerParams(vmem_limit_bytes=60 * 1024 * 1024),
    )(section, segments, x, cot)


def local_step(section, rows_in, length, gains, other_gains, mine, other):
    count = rows_in[0].shape[0]
    steps = count // TWO
    tok = lambda w: pl.BlockSpec((TWO, LP, w), lambda i, sec: (i, 0, 0))
    row_out = pl.BlockSpec((TWO, length, D), lambda i, sec: (i, 0, 0))
    whole = lambda shape: pl.BlockSpec(shape, lambda i, sec: (0,) * len(shape), pipeline_mode=pl.Buffered(1))
    hbm = pl.BlockSpec(memory_space=pl.ANY)
    vm = pltpu.VMEM
    flat = lambda w: vm((2, TWO * LP, w), BF)
    shape = jax.ShapeDtypeStruct
    return pl.pallas_call(
        kernel,
        grid_spec=pltpu.PrefetchScalarGridSpec(
            num_scalar_prefetch=1,
            grid=(steps,),
            in_specs=[tok(D), tok(D), tok(128), tok(128)] + [whole((2, D))] * 2 + [hbm] * 8,
            out_specs=[row_out, row_out, row_out, row_out, hbm, hbm, hbm, hbm],
            scratch_shapes=[
                vm((2, D, 3 * D), BF), vm((2, D, D), BF), vm((2, D, FF), BF), vm((2, FF, D), BF), pltpu.SemaphoreType.DMA((8,)), pltpu.SemaphoreType.DMA((4,)), vm((2, 3088, D), BF),
                vm((2, 2, D), F32), vm((TWO, LP, D), BF), vm((TWO, LP, D), F32),
                vm((TWO, LP, D), F32),
                vm((2, TWO, LP, D), F32), vm((2, TWO, LP, 128), F32), vm((2, TWO, LP, D), F32), vm((2, TWO, LP, 128), F32),
                flat(D), flat(D), flat(D),
                vm((2, TWO, 4 * LP, D), BF), vm((2, TWO, LP, D), BF), vm((2, TWO, LP, D), BF),
                vm((2, TWO, 4 * LP, D), BF), flat(FF), vm((2, TWO, LP, FF), BF),
                flat(D), flat(FF), vm((TWO, LP, D), F32), flat(D),
                vm((TWO, 4 * LP, D), BF), vm((TWO, 4 * LP, 128), BF), flat(3 * D), vm((TWO, LP, D), F32), vm((TWO, LP, D), F32),
                vm((4, D, TWO * LP), BF), vm((2, D, 3 * D), F32), vm((2, D, D), F32), vm((2, D, FF), F32), vm((2, D, FF), F32),
                vm((2, 2, 8, D), F32),
            ],
        ),
        out_shape=[
            shape((count, length, D), BF), shape((count, length, D), BF),
            shape((count, length, D), F32), shape((count, length, D), BF),
            shape((HALF + 16, D), BF), shape((HALF, D), BF), shape((HALF + 16, D), BF), shape((HALF, D), BF),
        ],
        compiler_params=pltpu.CompilerParams(
            dimension_semantics=("arbitrary",), vmem_limit_bytes=60 * 1024 * 1024
        ),
    )(section, *rows_in, gains, other_gains, *mine, *other)


def partner(value):
    return lax.ppermute(value, "section", [(0, 1), (1, 0)])


def cross(value, count, bits):
    pairs = [(s * count + i, s * count + (i ^ (1 << bits[s]))) for s in range(2) for i in range(count)]
    return lax.ppermute(value, ("section", "dp"), pairs)


def add(a, b):
    return (a.astype(F32) + b.astype(F32)).astype(BF)


def after(values, event):
    return lax.optimization_barrier((values, event))[0]


def sum_over_dp(parts, tail, section, follow):
    count = lax.axis_size("dp")
    place = lax.axis_index("dp")
    depth = count.bit_length() - 1
    orders = [list(range(depth)), list(range(depth))]
    if depth > 2:
        orders[1][1], orders[1][2] = 2, 1
    swap = {0: 1, 1: 0} if depth > 1 else {}
    orders = [[(b, swap.get(b, b)) for b in order] for order in orders]
    sizes = [tail, 0]
    current = list(parts)
    uppers = [[], []]
    sent = []
    for stage in range(depth):
        got = []
        for part in range(2):
            bits = orders[part][stage]
            upper = jnp.where(section == 0, place >> bits[0], place >> bits[1]) & 1
            uppers[part].append(upper)
            value = current[part]
            main = value.shape[0] - sizes[part]
            send = lax.dynamic_slice_in_dim(value, (1 - upper) * (main // 2), main // 2, 0)
            if sizes[part]:
                send = jnp.concatenate([send, value[main:]], axis=0)
            got.append(cross(send, count, bits))
            if stage == 0:
                sent.append(send)
        if stage == 0:
            followed = follow(sent)
        for part in range(2):
            value = current[part]
            main = value.shape[0] - sizes[part]
            keep = lax.dynamic_slice_in_dim(value, uppers[part][stage] * (main // 2), main // 2, 0)
            if sizes[part]:
                keep = jnp.concatenate([keep, value[main:]], axis=0)
            current[part] = add(keep, got[part])
    rest = current[0][current[0].shape[0] - tail :]
    current[0] = current[0][: current[0].shape[0] - tail]
    halves = []
    for stage in reversed(range(depth)):
        got = [cross(current[part], count, orders[part][stage]) for part in range(2)]
        for part in range(2):
            low = uppers[part][stage] == 0
            pair = (jnp.where(low, current[part], got[part]), jnp.where(low, got[part], current[part]))
            if stage == 0:
                halves.append(pair)
            else:
                current[part] = jnp.concatenate(pair, axis=0)
    return halves, rest, followed


def shards(
    layer_input, out_cotangent, segment_ids, gain_attn, weight_qkv, weight_out, gain_mlp, weight_up, weight_down
):
    section = lax.axis_index("section")
    here = section[None].astype(jnp.int32)
    rows_in = prepare(here, layer_input.swapaxes(0, 1), out_cotangent.swapaxes(0, 1), segment_ids)
    mine = (weight_qkv, weight_out, weight_up, weight_down)
    other = tuple(partner(w) for w in mine)
    gains = jnp.concatenate([gain_attn, gain_mlp], axis=0)
    other_gains = partner(gains)
    acts, acts_send, grads, grads_send, first, second, first_send, second_send = local_step(
        here, rows_in, layer_input.shape[1], gains, other_gains, mine, other,
    )
    got = partner(first_send), partner(second_send)
    parts = add(first, got[0]), add(second, got[1])
    low = section == 0

    def whole_rows(keep, got):
        return jnp.concatenate([jnp.where(low, keep, got), jnp.where(low, got, keep)], axis=0)

    def rows_out(sent):
        sends = (acts_send, grads_send)
        got = partner(sends[0]), partner(sends[1])
        got = after(got, sent[1])
        return whole_rows(acts, got[0]), whole_rows(grads, got[1].astype(F32))

    ((qkv, out_up), (up_down, down)), rest, (activations, input_grads) = sum_over_dp(parts, 16, section, rows_out)
    side = lambda *blocks: jnp.concatenate(blocks, axis=1).astype(F32)
    return (
        activations[None],
        input_grads[None],
        side(qkv[0:256], qkv[256:512], qkv[512:768])[None],
        out_up[0:256].astype(F32)[None],
        side(out_up[256:512], out_up[512:768], up_down[0:256], up_down[256:512])[None],
        jnp.concatenate([up_down[512:768], down], axis=0).astype(F32)[None],
        rest[0].astype(F32)[None],
        rest[1].astype(F32)[None],
    )


def solution(mesh):
    placed = (
        P("dp", None, None),
        P("dp", None, None),
        P("dp", None),
        P("section", None),
        P("section", None, None),
        P("section", None, None),
        P("section", None),
        P("section", None, None),
        P("section", None, None),
    )
    return jax.shard_map(
        shards,
        mesh=mesh,
        in_specs=placed,
        out_specs=(
            P("section", "dp", None, None),
            P("section", "dp", None, None),
            P("section", None, None),
            P("section", None, None),
            P("section", None, None),
            P("section", None, None),
            P("section", None),
            P("section", None),
        ),
        check_vma=False,
    )
```

```python
import jax
import jax.numpy as jnp
from jax import lax
from jax.experimental import pallas as pl
from jax.experimental.pallas import tpu as pltpu
from jax.sharding import PartitionSpec as P

D = 256
FF = 1024
FRAME = 17
LP = 352
EPS = 1e-05
BIG = -(2.0**100)
BLOCKS = ((0, 112, 0, 128), (112, 240, 0, 256), (240, 304, 64, 320), (304, 352, 96, 352))
ODDS = (-2.296875, -0.10888671875, 0.00135040283203125, -1.1146068572998047e-05)
TWO = 2
HALF = 1536
F32 = jnp.float32
BF = jnp.bfloat16


def mm(a, b):
    return jnp.dot(a, b, preferred_element_type=F32)


def mm_t(a, b):
    return lax.dot_general(a, b, (((1,), (1,)), ((), ())), preferred_element_type=F32)


def tmm(a, b):
    return lax.dot_general(a, b, (((0,), (0,)), ((), ())), preferred_element_type=F32)


def norm_stats(x):
    mean = jnp.sum(x, axis=-1, keepdims=True) * (1.0 / D)
    center = x - mean
    var = jnp.sum(center * center, axis=-1, keepdims=True) * (1.0 / D)
    rstd = lax.rsqrt(var + EPS)
    return center * rstd, rstd


def norm_back(d_out, gain, xhat, rstd):
    dy = d_out * gain
    s1 = jnp.sum(dy, axis=-1, keepdims=True) * (1.0 / D)
    s2 = jnp.sum(dy * xhat, axis=-1, keepdims=True) * (1.0 / D)
    return rstd * (dy - s1 - xhat * s2)


def gain_rows(d_out, xhat):
    prod = d_out * xhat
    return jnp.sum(prod.reshape(prod.shape[0] // 8, 8, D), axis=0)


def gelu_pair(u):
    low = lambda value: jnp.array(value, BF)
    u = u.astype(BF)
    u2 = u * u
    x = jnp.minimum(u2, low(25.0))
    p = ((x * low(ODDS[3]) + low(ODDS[2])) * x + low(ODDS[1])) * x + low(ODDS[0])
    cdf = pl.reciprocal(low(1.0) + jnp.exp2(u * p), approx=True)
    pdf = jnp.exp2(u2 * low(-0.7213475204444817) - low(1.3257480647361593))
    return u * cdf, cdf + u * pdf


def two_heads(block, lane_low):
    zero = jnp.zeros_like(block)
    return jnp.concatenate(
        [jnp.where(lane_low, block, zero), jnp.where(lane_low, zero, block)], axis=0
    )


def pair_rows(p, q0, q1):
    return slice(4 * q0 + 2 * p * (q1 - q0), 4 * q0 + 2 * (p + 1) * (q1 - q0))


def one_row(stacked, n):
    mask = low_mask(n)
    return jnp.concatenate(
        [
            jnp.where(mask, stacked[:n, 0:128], stacked[n : 2 * n, 0:128]),
            jnp.where(mask, stacked[2 * n : 3 * n, 128:256], stacked[3 * n :, 128:256]),
        ],
        axis=1,
    )


def low_mask(n):
    return lax.broadcasted_iota(jnp.int32, (n, 128), 1) < 64


def merged(*lists):
    tagged = [((i + 0.5) / len(units), j, unit) for j, units in enumerate(lists) for i, unit in enumerate(units)]
    for _, _, unit in sorted(tagged, key=lambda t: t[:2]):
        unit()


def wide(column):
    return jnp.concatenate([column, column], axis=1)


PARTS = ((0, 176), (176, 352))
WHOLE = ((0, LP),)
PAIRS = ((0, slice(0, 128)), (1, slice(128, 256)))


def kernel(
    sec_ref, x_ref, cot_ref, eq_ref, ek_ref, gains_mine, gains_other,
    wqkv_mine, wout_mine, wup_mine, wdown_mine, wqkv_other, wout_other, wup_other, wdown_other,
    yk_ref, ys_ref, dk_out_ref, ds_out_ref, pkeep_hbm, qkeep_hbm, psend_hbm, qsend_hbm,
    wqkv_ref, wout_ref, wup_ref, wdown_ref, wsem, outsem, grads_ref, gains_ref, ybuf_ref, dbuf_ref,
    res_ref, xhat1_ref, rstd1_ref, xhat2_ref, rstd2_ref, a_ref, b_ref, o_ref, qs_ref, k_ref, v_ref,
    p_ref, m_ref, gp_ref, gb_ref, du_ref, dh_ref, dhb_ref, do_ref, prod_ref, dqkv_ref, dk_ref, dv_ref,
    left_ref, aqkv_ref, aout_ref, aup_ref, adown_ref, again_ref,
):
    step = pl.program_id(0)
    last = pl.num_programs(0) - 1
    sec = sec_ref[0]
    first = sec == 0
    length = yk_ref.shape[1]

    copies = []
    for mine, other, held in (
        (wqkv_mine, wqkv_other, wqkv_ref), (wout_mine, wout_other, wout_ref),
        (wup_mine, wup_other, wup_ref), (wdown_mine, wdown_other, wdown_ref),
    ):
        copies.append(pltpu.make_async_copy(mine.at[0], held.at[sec], wsem.at[len(copies)]))
        copies.append(pltpu.make_async_copy(other.at[0], held.at[1 - sec], wsem.at[len(copies)]))

    @pl.when(step == 0)
    def _():
        for copy in copies:
            copy.start()
        mine, other = gains_mine[...].astype(F32), gains_other[...].astype(F32)
        gains_ref[0] = jnp.where(first, mine, other)
        gains_ref[1] = jnp.where(first, other, mine)
        for ref in (qs_ref, do_ref, aqkv_ref, aout_ref, aup_ref, adown_ref, again_ref):
            ref[...] = jnp.zeros_like(ref)
        for copy in copies[:4]:
            copy.wait()

    def load(r):
        def tokens(lo, hi):
            res_ref[r, lo:hi, :] = x_ref[r, lo:hi, :].astype(F32)

        return [lambda lo=lo, hi=hi: tokens(lo, hi) for lo, hi in PARTS]

    ones = jnp.ones((LP, 128), BF)

    def attn_forward(r, l):
        base = LP * r
        units = []

        def norm(lo, hi):
            xhat, rstd = norm_stats(res_ref[r, lo:hi, :])
            xhat1_ref[l, r, lo:hi, :] = xhat
            rstd1_ref[l, r, lo:hi, :] = jnp.broadcast_to(rstd, (hi - lo, 128))
            a_ref[l, base + lo : base + hi, :] = (xhat * gains_ref[l, 0:1, :]).astype(BF)

        def query():
            q = mm(a_ref[l, base : base + LP, :], wqkv_ref[l, :, 0:256]).astype(BF) * jnp.array(0.125, BF)
            for p, lanes in PAIRS:
                for q0, q1, _, _ in BLOCKS:
                    qs_ref[l, r, pair_rows(p, q0, q1), lanes] = two_heads(q[q0:q1, lanes], low_mask(q1 - q0))

        def key():
            k_ref[l, r] = mm(a_ref[l, base : base + LP, :], wqkv_ref[l, :, 256:512]).astype(BF)

        def value():
            v_ref[l, r] = mm(a_ref[l, base : base + LP, :], wqkv_ref[l, :, 512:768]).astype(BF)

        held = {}

        def scores(q0, q1, k0, k1):
            eq = eq_ref[r, q0:q1, :]
            eq = jnp.concatenate([eq, eq], axis=0)
            ek = ek_ref[r, k0:k1, :]
            held[q0] = [
                mm_t(
                    jnp.concatenate([qs_ref[l, r, pair_rows(p, q0, q1), lanes], eq], axis=1),
                    jnp.concatenate([k_ref[l, r, k0:k1, lanes], ek], axis=1),
                )
                for p, lanes in PAIRS
            ]

        def mix(q0, q1, k0, k1):
            n = q1 - q0
            probs = []
            for p, _ in PAIRS:
                s = held[q0][p]
                e = jnp.exp(s - jnp.max(s, axis=-1, keepdims=True))
                prob = (e * (1.0 / jnp.sum(e, axis=-1, keepdims=True))).astype(BF)
                p_ref[l, r, pair_rows(p, q0, q1), 0 : k1 - k0] = prob
                probs.append(prob)
            o = mm(jnp.concatenate(probs, axis=0), v_ref[l, r, k0:k1, :])
            o_ref[l, base + q0 : base + q1, :] = one_row(o, n).astype(BF)

        def out(lo, hi):
            h = res_ref[r, lo:hi, :] + mm(o_ref[l, base + lo : base + hi, :], wout_ref[l])
            res_ref[r, lo:hi, :] = h
            xhat, rstd = norm_stats(h)
            xhat2_ref[l, r, lo:hi, :] = xhat
            rstd2_ref[l, r, lo:hi, :] = jnp.broadcast_to(rstd, (hi - lo, 128))
            b_ref[l, base + lo : base + hi, :] = (xhat * gains_ref[l, 1:2, :]).astype(BF)

        units += [lambda lo=lo, hi=hi: norm(lo, hi) for lo, hi in PARTS]
        units += [query, key, value]
        first = [lambda b=b: scores(*b) for b in BLOCKS]
        second = [lambda b=b: mix(*b) for b in BLOCKS]
        units += [first[0], first[1], second[0], first[2], second[1], first[3], second[2], second[3]]
        units += [lambda lo=lo, hi=hi: out(lo, hi) for lo, hi in WHOLE]
        return units

    def mlp_forward(r, l):
        base = LP * r

        def chunk(c, lo, hi):
            rows = slice(base + lo, base + hi)
            ups = [mm(b_ref[l, rows, :], wup_ref[l, :, 256 * j : 256 * j + 256]) for j in (c, c + 1)]
            for j, u in zip((c, c + 1), ups):
                m, gp = gelu_pair(u)
                m_ref[l, rows, 256 * j : 256 * j + 256] = m.astype(BF)
                gp_ref[l, r, lo:hi, 256 * j : 256 * j + 256] = gp.astype(BF)

        def down(lo, hi):
            y = res_ref[r, lo:hi, :] + mm(m_ref[l, base + lo : base + hi, :], wdown_ref[l])
            y = y.astype(BF)
            if l == 0:
                ybuf_ref[r, lo:hi, :] = y
                res_ref[r, lo:hi, :] = y.astype(F32)
            else:
                end = min(hi, length)
                y0, y1 = ybuf_ref[r, lo:hi, :][: end - lo], y[: end - lo]
                yk_ref[r, lo:end, :] = jnp.where(first, y0, y1)
                ys_ref[r, lo:hi, :] = jnp.where(first, y, ybuf_ref[r, lo:hi, :])

        return [lambda: chunk(0, 0, LP), lambda: chunk(2, 0, LP), lambda: down(0, LP)]

    def mlp_backward(r, l):
        base = LP * r

        def chunk(c, lo, hi):
            rows = slice(base + lo, base + hi)
            dms = [mm_t(gb_ref[l, rows, :], wdown_ref[l, 256 * j : 256 * j + 256, :]) for j in (c, c + 1)]
            for j, dm in zip((c, c + 1), dms):
                cols = slice(256 * j, 256 * j + 256)
                du_ref[l, rows, cols] = (dm * gp_ref[l, r, lo:hi, cols].astype(F32)).astype(BF)

        def back(lo, hi):
            rows = slice(base + lo, base + hi)
            d_b = mm_t(du_ref[l, rows, :], wup_ref[l])
            xhat = xhat2_ref[l, r, lo:hi, :]
            again_ref[l, 1] += gain_rows(d_b, xhat)
            d_h = gb_ref[l, rows, :].astype(F32) + norm_back(d_b, gains_ref[l, 1:2, :], xhat, wide(rstd2_ref[l, r, lo:hi, :]))
            dh_ref[r, lo:hi, :] = d_h
            dhb_ref[l, rows, :] = d_h.astype(BF)

        return (
            [lambda c=c, lo=lo, hi=hi: chunk(c, lo, hi) for c in (0, 2) for lo, hi in WHOLE]
            + [lambda lo=lo, hi=hi: back(lo, hi) for lo, hi in WHOLE]
        )

    def attn_backward(r, l):
        base = LP * r

        def out():
            d_o = mm_t(dhb_ref[l, base : base + LP, :], wout_ref[l]).astype(BF)
            prod = (-(d_o.astype(F32) * o_ref[l, base : base + LP, :].astype(F32))).astype(BF)
            for p, lanes in PAIRS:
                for q0, q1, _, _ in BLOCKS:
                    mask = low_mask(q1 - q0)
                    do_ref[r, pair_rows(p, q0, q1), lanes] = two_heads(d_o[q0:q1, lanes], mask)
                    prod_ref[r, pair_rows(p, q0, q1), :] = two_heads(prod[q0:q1, lanes], mask)
            dk_ref[r] = jnp.zeros((LP, D), F32)
            dv_ref[r] = jnp.zeros((LP, D), F32)

        held = {}

        def probs(q0, q1, k0, k1):
            held[q0] = [
                mm_t(
                    jnp.concatenate(
                        [do_ref[r, pair_rows(p, q0, q1), lanes], prod_ref[r, pair_rows(p, q0, q1), :]], axis=1
                    ),
                    jnp.concatenate([v_ref[l, r, k0:k1, lanes], ones[k0:k1]], axis=1),
                )
                for p, lanes in PAIRS
            ]

        def values(q0, q1, k0, k1):
            rows = slice(4 * q0, 4 * q1)
            dv_ref[r, k0:k1, :] += tmm(p_ref[l, r, rows, 0 : k1 - k0], do_ref[r, rows, :])

        def queries(q0, q1, k0, k1):
            n = q1 - q0
            ds = jnp.concatenate(
                [
                    (p_ref[l, r, pair_rows(p, q0, q1), 0 : k1 - k0].astype(F32) * held[q0][p]).astype(BF)
                    for p, _ in PAIRS
                ],
                axis=0,
            )
            dq = mm(ds, k_ref[l, r, k0:k1, :])
            dqkv_ref[l, base + q0 : base + q1, 0:256] = (one_row(dq, n) * 0.125).astype(BF)
            dk_ref[r, k0:k1, :] += tmm(ds, qs_ref[l, r, 4 * q0 : 4 * q1, :])

        def finish(lo, hi):
            rows = slice(base + lo, base + hi)
            dqkv_ref[l, rows, 256:512] = dk_ref[r, lo:hi, :].astype(BF)
            dqkv_ref[l, rows, 512:768] = dv_ref[r, lo:hi, :].astype(BF)
            d_a = mm_t(dqkv_ref[l, rows, :], wqkv_ref[l])
            xhat = xhat1_ref[l, r, lo:hi, :]
            again_ref[l, 0] += gain_rows(d_a, xhat)
            d_x = dh_ref[r, lo:hi, :] + norm_back(d_a, gains_ref[l, 0:1, :], xhat, wide(rstd1_ref[l, r, lo:hi, :]))
            if l:
                dbuf_ref[r, lo:hi, :] = d_x
                gb_ref[0, rows, :] = d_x.astype(BF)
            else:
                end = min(hi, length)
                d0, d1 = d_x[: end - lo], dbuf_ref[r, lo:hi, :][: end - lo]
                dk_out_ref[r, lo:end, :] = jnp.where(first, d0, d1)
                ds_out_ref[r, lo:hi, :] = jnp.where(first, dbuf_ref[r, lo:hi, :], d_x).astype(BF)

        order = [(probs, 0), (probs, 1), (values, 0), (queries, 0), (probs, 2), (values, 1), (queries, 1)]
        order += [(probs, 3), (values, 2), (queries, 2), (values, 3), (queries, 3)]
        return (
            [out]
            + [lambda f=f, b=BLOCKS[i]: f(*b) for f, i in order]
            + [lambda lo=lo, hi=hi: finish(lo, hi) for lo, hi in WHOLE]
        )

    def turn(j, ref, l):
        left_ref[j] = ref[l].T

    def mlp_weights(l):
        def down(c):
            for j in (c, c + 1):
                cols = slice(256 * j, 256 * j + 256)
                adown_ref[l, :, cols] += mm(left_ref[0], m_ref[l, :, cols])

        def up(c):
            for j in (c, c + 1):
                cols = slice(256 * j, 256 * j + 256)
                aup_ref[l, :, cols] += mm(left_ref[1], du_ref[l, :, cols])

        return [
            lambda: turn(0, gb_ref, l), lambda: turn(1, b_ref, l),
            lambda: down(0), lambda: down(2), lambda: up(0), lambda: up(2),
        ]

    def attn_weights(l):
        def out_and_query():
            aout_ref[l] += mm(left_ref[2], dhb_ref[l])
            aqkv_ref[l, :, 0:256] += mm(left_ref[3], dqkv_ref[l, :, 0:256])

        def key_and_value():
            for j in (1, 2):
                cols = slice(256 * j, 256 * j + 256)
                aqkv_ref[l, :, cols] += mm(left_ref[3], dqkv_ref[l, :, cols])

        return [lambda: turn(2, o_ref, l), lambda: turn(3, a_ref, l), out_and_query, key_and_value]

    merged(load(0) + attn_forward(0, 0), load(1) + attn_forward(1, 0))

    @pl.when(step == 0)
    def _():
        for copy in copies[4:]:
            copy.wait()

    merged(mlp_forward(0, 0), mlp_forward(1, 0))
    merged(attn_forward(0, 1), attn_forward(1, 1))
    merged(mlp_forward(0, 1), mlp_forward(1, 1))
    for r in range(TWO):
        gb_ref[1, LP * r : LP * r + LP, :] = cot_ref[r]
    merged(mlp_backward(0, 1), mlp_backward(1, 1))
    merged(mlp_weights(1))
    merged(attn_backward(0, 1), attn_backward(1, 1))
    merged(attn_weights(1))
    merged(mlp_backward(0, 0), mlp_backward(1, 0))
    merged(mlp_weights(0))
    merged(attn_backward(0, 0), attn_backward(1, 0))
    merged(attn_weights(0))

    @pl.when(step == last)
    def _():
        copies = []

        def hand(n, lo, rows, out):
            copies.append(pltpu.make_async_copy(grads_ref.at[n, pl.ds(lo, rows)], out, outsem.at[len(copies)]))
            copies[-1].start()

        for n, l, p_out, q_out in ((0, 1 - sec, psend_hbm, qsend_hbm), (1, sec, pkeep_hbm, qkeep_hbm)):
            for j in range(4):
                grads_ref[n, 256 * j : 256 * j + 256, :] = aup_ref[l, :, 256 * j : 256 * j + 256].astype(BF)
            for j in range(2):
                grads_ref[n, 1024 + 256 * j : 1280 + 256 * j, :] = adown_ref[l, :, 256 * j : 256 * j + 256].astype(BF).T
            row = lax.broadcasted_iota(jnp.int32, (16, D), 0)
            attn = jnp.sum(again_ref[l, 0], axis=0, keepdims=True)
            mlp = jnp.sum(again_ref[l, 1], axis=0, keepdims=True)
            grads_ref[n, HALF : HALF + 16, :] = jnp.where(row == 0, attn, jnp.where(row == 1, mlp, 0.0)).astype(BF)
            hand(n, 0, HALF + 16, p_out)
            for j in range(3):
                grads_ref[n, 1552 + 256 * j : 1808 + 256 * j, :] = aqkv_ref[l, :, 256 * j : 256 * j + 256].astype(BF)
            grads_ref[n, 2320:2576, :] = aout_ref[l].astype(BF)
            for j in range(2):
                grads_ref[n, 2576 + 256 * j : 2832 + 256 * j, :] = adown_ref[l, :, 512 + 256 * j : 768 + 256 * j].astype(BF).T
            hand(n, HALF + 16, HALF, q_out)
        for copy in copies:
            copy.wait()


def spread(
    sec_ref, seg_ref, x_hbm, cot_hbm, x_out, cot_out, eq_out, ek_out,
    x_ref, cot_ref, x_rows, cot_rows, eq_ref, ek_ref, wide_ref, seg_pad_ref, sem, outsem,
):
    length, count, _ = x_ref.shape
    begin = sec_ref[0] * (count // 2)
    loads = [pltpu.make_async_copy(x_hbm, x_ref, sem.at[0]), pltpu.make_async_copy(cot_hbm, cot_ref, sem.at[1])]
    stores = [
        pltpu.make_async_copy(held, out, outsem.at[n])
        for n, (held, out) in enumerate(((eq_ref, eq_out), (ek_ref, ek_out), (x_rows, x_out), (cot_rows, cot_out)))
    ]
    for copy in loads:
        copy.start()
    seg_pad_ref[...] = jnp.full(seg_pad_ref.shape, -1, jnp.int32)
    seg_pad_ref[:, 0:length] = seg_ref[...]
    lane = lax.broadcasted_iota(jnp.int32, (LP, 128), 1)
    token = lax.broadcasted_iota(jnp.int32, (LP, 128), 0)
    framed = lane < 64
    here = jnp.logical_and(token >= FRAME * lane, token < FRAME * lane + FRAME)
    here = jnp.where(jnp.logical_and(framed, here), 1.0, 0.0)
    later = jnp.where(jnp.logical_and(framed, token >= FRAME * lane + FRAME), BIG, 0.0)
    piece = lax.broadcasted_iota(jnp.int32, (16, seg_pad_ref.shape[1]), 0)
    column = lax.broadcasted_iota(jnp.int32, (16, 128), 1) - 64
    unit = jnp.where(column == lax.broadcasted_iota(jnp.int32, (16, 128), 0), 1.0, 0.0).astype(BF)
    for r in range(count // 2):
        seg = jnp.broadcast_to(seg_pad_ref[pl.ds(begin + r, 1), :], piece.shape)
        same = jnp.where(seg == piece, 1.0, 0.0).astype(BF)[:, :LP]
        other = jnp.where(jnp.logical_and(seg != piece, piece < 4), BIG, 0.0).astype(BF)[:, :LP]
        eq_ref[r] = (here + tmm(same, unit)).astype(BF)
        ek_ref[r] = (later + tmm(other, unit)).astype(BF)
    stores[0].start()
    stores[1].start()
    for n, (taken, rows) in enumerate(((x_ref, x_rows), (cot_ref, cot_rows))):
        loads[n].wait()
        for p in range(2):
            wide_ref[p] = taken[:, :, 128 * p : 128 * p + 128].astype(F32).reshape(length * count, 128)
        for r in range(count // 2):
            rows[r, LP - 16 : LP, :] = jnp.zeros((16, D), BF)
            for p in range(2):
                row = wide_ref[p, pl.ds(begin + r, length, stride=count), :]
                rows[r, 0:length, 128 * p : 128 * p + 128] = row.astype(BF)
        stores[2 + n].start()
    for copy in stores:
        copy.wait()


def prepare(section, x, cot, segments):
    length, rows, _ = x.shape
    hbm = pl.BlockSpec(memory_space=pl.ANY)
    vm = pltpu.VMEM
    tokens, columns = (rows // 2, LP, D), (rows // 2, LP, 128)
    return pl.pallas_call(
        spread,
        in_specs=[pl.BlockSpec(memory_space=pltpu.SMEM), pl.BlockSpec(memory_space=pltpu.VMEM), hbm, hbm],
        out_specs=[hbm] * 4,
        out_shape=[jax.ShapeDtypeStruct(dims, BF) for dims in (tokens, tokens, columns, columns)],
        scratch_shapes=[
            vm(x.shape, BF), vm(x.shape, BF), vm(tokens, BF), vm(tokens, BF), vm(columns, BF), vm(columns, BF),
            vm((2, length * rows, 128), F32), vm((rows, 384), jnp.int32),
            pltpu.SemaphoreType.DMA((2,)), pltpu.SemaphoreType.DMA((4,)),
        ],
        compiler_params=pltpu.CompilerParams(vmem_limit_bytes=65400 * 1024),
    )(section, segments, x, cot)


def local_step(section, rows_in, length, gains, other_gains, mine, other):
    count = rows_in[0].shape[0]
    steps = count // TWO
    tok = lambda w: pl.BlockSpec((TWO, LP, w), lambda i, sec: (i, 0, 0))
    row_out = pl.BlockSpec((TWO, length, D), lambda i, sec: (i, 0, 0))
    whole = lambda shape: pl.BlockSpec(shape, lambda i, sec: (0,) * len(shape), pipeline_mode=pl.Buffered(1))
    hbm = pl.BlockSpec(memory_space=pl.ANY)
    vm = pltpu.VMEM
    flat = lambda w: vm((2, TWO * LP, w), BF)
    shape = jax.ShapeDtypeStruct
    return pl.pallas_call(
        kernel,
        grid_spec=pltpu.PrefetchScalarGridSpec(
            num_scalar_prefetch=1,
            grid=(steps,),
            in_specs=[tok(D), tok(D), tok(128), tok(128)] + [whole((2, D))] * 2 + [hbm] * 8,
            out_specs=[row_out, tok(D), row_out, tok(D), hbm, hbm, hbm, hbm],
            scratch_shapes=[
                vm((2, D, 3 * D), BF), vm((2, D, D), BF), vm((2, D, FF), BF), vm((2, FF, D), BF), pltpu.SemaphoreType.DMA((8,)), pltpu.SemaphoreType.DMA((4,)), vm((2, 3088, D), BF),
                vm((2, 2, D), F32), vm((TWO, LP, D), BF), vm((TWO, LP, D), F32),
                vm((TWO, LP, D), F32),
                vm((2, TWO, LP, D), F32), vm((2, TWO, LP, 128), F32), vm((2, TWO, LP, D), F32), vm((2, TWO, LP, 128), F32),
                flat(D), flat(D), flat(D),
                vm((2, TWO, 4 * LP, D), BF), vm((2, TWO, LP, D), BF), vm((2, TWO, LP, D), BF),
                vm((2, TWO, 4 * LP, D), BF), flat(FF), vm((2, TWO, LP, FF), BF),
                flat(D), flat(FF), vm((TWO, LP, D), F32), flat(D),
                vm((TWO, 4 * LP, D), BF), vm((TWO, 4 * LP, 128), BF), flat(3 * D), vm((TWO, LP, D), F32), vm((TWO, LP, D), F32),
                vm((4, D, TWO * LP), BF), vm((2, D, 3 * D), F32), vm((2, D, D), F32), vm((2, D, FF), F32), vm((2, D, FF), F32),
                vm((2, 2, 8, D), F32),
            ],
        ),
        out_shape=[
            shape((count, length, D), BF), shape((count, LP, D), BF),
            shape((count, length, D), F32), shape((count, LP, D), BF),
            shape((HALF + 16, D), BF), shape((HALF, D), BF), shape((HALF + 16, D), BF), shape((HALF, D), BF),
        ],
        compiler_params=pltpu.CompilerParams(
            dimension_semantics=("arbitrary",), vmem_limit_bytes=60 * 1024 * 1024
        ),
    )(section, *rows_in, gains, other_gains, *mine, *other)


def partner(value):
    return lax.ppermute(value, "section", [(0, 1), (1, 0)])


def cross(value, count, bits):
    pairs = [(s * count + i, s * count + (i ^ (1 << bits[s]))) for s in range(2) for i in range(count)]
    return lax.ppermute(value, ("section", "dp"), pairs)


def add(a, b):
    return (a.astype(F32) + b.astype(F32)).astype(BF)


def idle(value_ref, event_ref, out_ref):
    pass


def after(value, event):
    hbm = pl.BlockSpec(memory_space=pl.ANY)
    return pl.pallas_call(
        idle,
        in_specs=[hbm, hbm],
        out_specs=hbm,
        out_shape=jax.ShapeDtypeStruct(value.shape, value.dtype),
        input_output_aliases={0: 0},
        compiler_params=pltpu.CompilerParams(vmem_limit_bytes=1024 * 1024),
    )(value, event)


def sum_over_dp(parts, tail, section, follow):
    count = lax.axis_size("dp")
    place = lax.axis_index("dp")
    depth = count.bit_length() - 1
    orders = [list(range(depth)), list(range(depth))]
    if depth > 2:
        orders[1][1], orders[1][2] = 2, 1
    swap = {0: 1, 1: 0} if depth > 1 else {}
    orders = [[(b, swap.get(b, b)) for b in order] for order in orders]
    sizes = [tail, 0]
    current = list(parts)
    uppers = [[], []]
    sent = []
    for stage in range(depth):
        got = []
        for part in range(2):
            bits = orders[part][stage]
            upper = jnp.where(section == 0, place >> bits[0], place >> bits[1]) & 1
            uppers[part].append(upper)
            value = current[part]
            main = value.shape[0] - sizes[part]
            send = lax.dynamic_slice_in_dim(value, (1 - upper) * (main // 2), main // 2, 0)
            if sizes[part]:
                send = jnp.concatenate([send, value[main:]], axis=0)
            got.append(cross(send, count, bits))
            if stage == 0:
                sent.append(send)
        if stage == 0:
            followed = follow(sent)
        for part in range(2):
            value = current[part]
            main = value.shape[0] - sizes[part]
            keep = lax.dynamic_slice_in_dim(value, uppers[part][stage] * (main // 2), main // 2, 0)
            if sizes[part]:
                keep = jnp.concatenate([keep, value[main:]], axis=0)
            current[part] = add(keep, got[part])
    rest = current[0][current[0].shape[0] - tail :]
    current[0] = current[0][: current[0].shape[0] - tail]
    halves = []
    for stage in reversed(range(depth)):
        got = [cross(current[part], count, orders[part][stage]) for part in range(2)]
        for part in range(2):
            low = uppers[part][stage] == 0
            pair = (jnp.where(low, current[part], got[part]), jnp.where(low, got[part], current[part]))
            if stage == 0:
                halves.append(pair)
            else:
                current[part] = jnp.concatenate(pair, axis=0)
    return halves, rest, followed


def shards(
    layer_input, out_cotangent, segment_ids, gain_attn, weight_qkv, weight_out, gain_mlp, weight_up, weight_down
):
    section = lax.axis_index("section")
    here = section[None].astype(jnp.int32)
    rows_in = prepare(here, layer_input.swapaxes(0, 1), out_cotangent.swapaxes(0, 1), segment_ids)
    mine = (weight_qkv, weight_out, weight_up, weight_down)
    other = tuple(partner(w) for w in mine)
    gains = jnp.concatenate([gain_attn, gain_mlp], axis=0)
    other_gains = partner(gains)
    acts, acts_send, grads, grads_send, first, second, first_send, second_send = local_step(
        here, rows_in, layer_input.shape[1], gains, other_gains, mine, other,
    )
    length = layer_input.shape[1]
    rows_sent = lambda a: partner(a.reshape(-1, D))
    got = partner(first_send), partner(second_send)
    parts = add(first, got[0]), add(second, got[1])
    low = section == 0

    def whole_rows(keep, got):
        return jnp.concatenate([jnp.where(low, keep, got), jnp.where(low, got, keep)], axis=0)

    received = [rows_sent(a) for a in (acts_send, grads_send)]

    def rows_out(sent):
        got = [after(a, sent[0]) for a in received]
        got = [a.reshape(acts_send.shape)[:, :length] for a in got]
        return whole_rows(acts, got[0]), whole_rows(grads, got[1].astype(F32))

    ((up, up_down), (qkv, out_down)), rest, (activations, input_grads) = sum_over_dp(parts, 16, section, rows_out)
    side = lambda *blocks: jnp.concatenate(blocks, axis=1).astype(F32)
    return (
        activations[None],
        input_grads[None],
        side(qkv[0:256], qkv[256:512], qkv[512:768])[None],
        out_down[0:256].astype(F32)[None],
        side(up[0:256], up[256:512], up[512:768], up_down[0:256])[None],
        jnp.concatenate([up_down[256:768], out_down[256:768]], axis=0).astype(F32)[None],
        rest[0].astype(F32)[None],
        rest[1].astype(F32)[None],
    )


def solution(mesh):
    placed = (
        P("dp", None, None),
        P("dp", None, None),
        P("dp", None),
        P("section", None),
        P("section", None, None),
        P("section", None, None),
        P("section", None),
        P("section", None, None),
        P("section", None, None),
    )
    return jax.shard_map(
        shards,
        mesh=mesh,
        in_specs=placed,
        out_specs=(
            P("section", "dp", None, None),
            P("section", "dp", None, None),
            P("section", None, None),
            P("section", None, None),
            P("section", None, None),
            P("section", None, None),
            P("section", None),
            P("section", None),
        ),
        check_vma=False,
    )
```

```python
import jax
import jax.numpy as jnp
from jax import lax
from jax.experimental import pallas as pl
from jax.experimental.pallas import tpu as pltpu
from jax.sharding import PartitionSpec as P

D = 256
FF = 1024
FRAME = 17
LP = 352
EPS = 1e-05
BIG = -(2.0**100)
BLOCKS = ((0, 112, 0, 128), (112, 240, 0, 256), (240, 304, 64, 320), (304, 352, 96, 352))
ODDS = (-2.296875, -0.10888671875, 0.00135040283203125, -1.1146068572998047e-05)
TWO = 2
HALF = 1536
F32 = jnp.float32
BF = jnp.bfloat16


def mm(a, b):
    return jnp.dot(a, b, preferred_element_type=F32)


def mm_t(a, b):
    return lax.dot_general(a, b, (((1,), (1,)), ((), ())), preferred_element_type=F32)


def tmm(a, b):
    return lax.dot_general(a, b, (((0,), (0,)), ((), ())), preferred_element_type=F32)


def norm_stats(x):
    mean = jnp.sum(x, axis=-1, keepdims=True) * (1.0 / D)
    center = x - mean
    var = jnp.sum(center * center, axis=-1, keepdims=True) * (1.0 / D)
    rstd = lax.rsqrt(var + EPS)
    return center * rstd, rstd


def norm_back(d_out, gain, xhat, rstd):
    dy = d_out * gain
    s1 = jnp.sum(dy, axis=-1, keepdims=True) * (1.0 / D)
    s2 = jnp.sum(dy * xhat, axis=-1, keepdims=True) * (1.0 / D)
    return rstd * (dy - s1 - xhat * s2)


def gain_rows(d_out, xhat):
    prod = d_out * xhat
    return jnp.sum(prod.reshape(prod.shape[0] // 8, 8, D), axis=0)


def gelu_pair(u):
    low = lambda value: jnp.array(value, BF)
    u = u.astype(BF)
    u2 = u * u
    x = jnp.minimum(u2, low(25.0))
    p = ((x * low(ODDS[3]) + low(ODDS[2])) * x + low(ODDS[1])) * x + low(ODDS[0])
    cdf = pl.reciprocal(low(1.0) + jnp.exp2(u * p), approx=True)
    pdf = jnp.exp2(u2 * low(-0.7213475204444817) - low(1.3257480647361593))
    return u * cdf, cdf + u * pdf


def two_heads(block, lane_low):
    zero = jnp.zeros_like(block)
    return jnp.concatenate(
        [jnp.where(lane_low, block, zero), jnp.where(lane_low, zero, block)], axis=0
    )


def pair_rows(p, q0, q1):
    return slice(4 * q0 + 2 * p * (q1 - q0), 4 * q0 + 2 * (p + 1) * (q1 - q0))


def one_row(stacked, n):
    mask = low_mask(n)
    return jnp.concatenate(
        [
            jnp.where(mask, stacked[:n, 0:128], stacked[n : 2 * n, 0:128]),
            jnp.where(mask, stacked[2 * n : 3 * n, 128:256], stacked[3 * n :, 128:256]),
        ],
        axis=1,
    )


def low_mask(n):
    return lax.broadcasted_iota(jnp.int32, (n, 128), 1) < 64


def merged(*lists):
    tagged = [((i + 0.5) / len(units), j, unit) for j, units in enumerate(lists) for i, unit in enumerate(units)]
    for _, _, unit in sorted(tagged, key=lambda t: t[:2]):
        unit()


def wide(column):
    return jnp.concatenate([column, column], axis=1)


PARTS = ((0, 176), (176, 352))
WHOLE = ((0, LP),)
PAIRS = ((0, slice(0, 128)), (1, slice(128, 256)))


def kernel(
    sec_ref, x_ref, cot_ref, eq_ref, ek_ref, gains_mine, gains_other,
    wqkv_mine, wout_mine, wup_mine, wdown_mine, wqkv_other, wout_other, wup_other, wdown_other,
    yk_ref, ys_ref, dk_out_ref, ds_out_ref, pkeep_hbm, qkeep_hbm, psend_hbm, qsend_hbm,
    wqkv_ref, wout_ref, wup_ref, wdown_ref, wsem, outsem, grads_ref, gains_ref, ybuf_ref, dbuf_ref,
    res_ref, xhat1_ref, rstd1_ref, xhat2_ref, rstd2_ref, a_ref, b_ref, o_ref, qs_ref, k_ref, v_ref,
    p_ref, m_ref, gp_ref, gb_ref, du_ref, dh_ref, dhb_ref, do_ref, prod_ref, dqkv_ref, dk_ref, dv_ref,
    left_ref, aqkv_ref, aout_ref, aup_ref, adown_ref, again_ref,
):
    step = pl.program_id(0)
    last = pl.num_programs(0) - 1
    sec = sec_ref[0]
    first = sec == 0
    length = yk_ref.shape[1]

    copies = []
    for mine, other, held in (
        (wqkv_mine, wqkv_other, wqkv_ref), (wout_mine, wout_other, wout_ref),
        (wup_mine, wup_other, wup_ref), (wdown_mine, wdown_other, wdown_ref),
    ):
        copies.append(pltpu.make_async_copy(mine.at[0], held.at[sec], wsem.at[len(copies)]))
        copies.append(pltpu.make_async_copy(other.at[0], held.at[1 - sec], wsem.at[len(copies)]))

    @pl.when(step == 0)
    def _():
        for copy in copies:
            copy.start()
        mine, other = gains_mine[...].astype(F32), gains_other[...].astype(F32)
        gains_ref[0] = jnp.where(first, mine, other)
        gains_ref[1] = jnp.where(first, other, mine)
        for ref in (qs_ref, do_ref, aqkv_ref, aout_ref, aup_ref, adown_ref, again_ref):
            ref[...] = jnp.zeros_like(ref)
        for copy in copies[:4]:
            copy.wait()

    def load(r):
        def tokens(lo, hi):
            res_ref[r, lo:hi, :] = x_ref[r, lo:hi, :].astype(F32)

        return [lambda lo=lo, hi=hi: tokens(lo, hi) for lo, hi in PARTS]

    ones = jnp.ones((LP, 128), BF)

    def attn_forward(r, l):
        base = LP * r
        units = []

        def norm(lo, hi):
            xhat, rstd = norm_stats(res_ref[r, lo:hi, :])
            xhat1_ref[l, r, lo:hi, :] = xhat
            rstd1_ref[l, r, lo:hi, :] = jnp.broadcast_to(rstd, (hi - lo, 128))
            a_ref[l, base + lo : base + hi, :] = (xhat * gains_ref[l, 0:1, :]).astype(BF)

        def query():
            q = mm(a_ref[l, base : base + LP, :], wqkv_ref[l, :, 0:256]).astype(BF) * jnp.array(0.125, BF)
            for p, lanes in PAIRS:
                for q0, q1, _, _ in BLOCKS:
                    qs_ref[l, r, pair_rows(p, q0, q1), lanes] = two_heads(q[q0:q1, lanes], low_mask(q1 - q0))

        def key():
            k_ref[l, r] = mm(a_ref[l, base : base + LP, :], wqkv_ref[l, :, 256:512]).astype(BF)

        def value():
            v_ref[l, r] = mm(a_ref[l, base : base + LP, :], wqkv_ref[l, :, 512:768]).astype(BF)

        held = {}

        def scores(q0, q1, k0, k1):
            eq = eq_ref[r, q0:q1, :]
            eq = jnp.concatenate([eq, eq], axis=0)
            ek = ek_ref[r, k0:k1, :]
            held[q0] = [
                mm_t(
                    jnp.concatenate([qs_ref[l, r, pair_rows(p, q0, q1), lanes], eq], axis=1),
                    jnp.concatenate([k_ref[l, r, k0:k1, lanes], ek], axis=1),
                )
                for p, lanes in PAIRS
            ]

        def mix(q0, q1, k0, k1):
            n = q1 - q0
            probs = []
            for p, _ in PAIRS:
                s = held[q0][p]
                e = jnp.exp(s - jnp.max(s, axis=-1, keepdims=True))
                prob = (e * (1.0 / jnp.sum(e, axis=-1, keepdims=True))).astype(BF)
                p_ref[l, r, pair_rows(p, q0, q1), 0 : k1 - k0] = prob
                probs.append(prob)
            o = mm(jnp.concatenate(probs, axis=0), v_ref[l, r, k0:k1, :])
            o_ref[l, base + q0 : base + q1, :] = one_row(o, n).astype(BF)

        def out(lo, hi):
            h = res_ref[r, lo:hi, :] + mm(o_ref[l, base + lo : base + hi, :], wout_ref[l])
            res_ref[r, lo:hi, :] = h
            xhat, rstd = norm_stats(h)
            xhat2_ref[l, r, lo:hi, :] = xhat
            rstd2_ref[l, r, lo:hi, :] = jnp.broadcast_to(rstd, (hi - lo, 128))
            b_ref[l, base + lo : base + hi, :] = (xhat * gains_ref[l, 1:2, :]).astype(BF)

        units += [lambda lo=lo, hi=hi: norm(lo, hi) for lo, hi in PARTS]
        units += [query, key, value]
        first = [lambda b=b: scores(*b) for b in BLOCKS]
        second = [lambda b=b: mix(*b) for b in BLOCKS]
        units += [first[0], first[1], second[0], first[2], second[1], first[3], second[2], second[3]]
        units += [lambda lo=lo, hi=hi: out(lo, hi) for lo, hi in WHOLE]
        return units

    def mlp_forward(r, l):
        base = LP * r

        def chunk(c, lo, hi):
            rows = slice(base + lo, base + hi)
            ups = [mm(b_ref[l, rows, :], wup_ref[l, :, 256 * j : 256 * j + 256]) for j in (c, c + 1)]
            for j, u in zip((c, c + 1), ups):
                m, gp = gelu_pair(u)
                m_ref[l, rows, 256 * j : 256 * j + 256] = m.astype(BF)
                gp_ref[l, r, lo:hi, 256 * j : 256 * j + 256] = gp.astype(BF)

        def down(lo, hi):
            y = res_ref[r, lo:hi, :] + mm(m_ref[l, base + lo : base + hi, :], wdown_ref[l])
            y = y.astype(BF)
            if l == 0:
                ybuf_ref[r, lo:hi, :] = y
                res_ref[r, lo:hi, :] = y.astype(F32)
            else:
                end = min(hi, length)
                y0, y1 = ybuf_ref[r, lo:hi, :][: end - lo], y[: end - lo]
                yk_ref[r, lo:end, :] = jnp.where(first, y0, y1)
                ys_ref[r, lo:hi, :] = jnp.where(first, y, ybuf_ref[r, lo:hi, :])

        return [lambda: chunk(0, 0, LP), lambda: chunk(2, 0, LP), lambda: down(0, LP)]

    def mlp_backward(r, l):
        base = LP * r

        def chunk(c, lo, hi):
            rows = slice(base + lo, base + hi)
            dms = [mm_t(gb_ref[l, rows, :], wdown_ref[l, 256 * j : 256 * j + 256, :]) for j in (c, c + 1)]
            for j, dm in zip((c, c + 1), dms):
                cols = slice(256 * j, 256 * j + 256)
                du_ref[l, rows, cols] = (dm * gp_ref[l, r, lo:hi, cols].astype(F32)).astype(BF)

        def back(lo, hi):
            rows = slice(base + lo, base + hi)
            d_b = mm_t(du_ref[l, rows, :], wup_ref[l])
            xhat = xhat2_ref[l, r, lo:hi, :]
            again_ref[l, 1] += gain_rows(d_b, xhat)
            d_h = gb_ref[l, rows, :].astype(F32) + norm_back(d_b, gains_ref[l, 1:2, :], xhat, wide(rstd2_ref[l, r, lo:hi, :]))
            dh_ref[r, lo:hi, :] = d_h
            dhb_ref[l, rows, :] = d_h.astype(BF)

        return (
            [lambda c=c, lo=lo, hi=hi: chunk(c, lo, hi) for c in (0, 2) for lo, hi in WHOLE]
            + [lambda lo=lo, hi=hi: back(lo, hi) for lo, hi in WHOLE]
        )

    def attn_backward(r, l):
        base = LP * r

        def out():
            d_o = mm_t(dhb_ref[l, base : base + LP, :], wout_ref[l]).astype(BF)
            prod = (-(d_o.astype(F32) * o_ref[l, base : base + LP, :].astype(F32))).astype(BF)
            for p, lanes in PAIRS:
                for q0, q1, _, _ in BLOCKS:
                    mask = low_mask(q1 - q0)
                    do_ref[r, pair_rows(p, q0, q1), lanes] = two_heads(d_o[q0:q1, lanes], mask)
                    prod_ref[r, pair_rows(p, q0, q1), :] = two_heads(prod[q0:q1, lanes], mask)
            dk_ref[r] = jnp.zeros((LP, D), F32)
            dv_ref[r] = jnp.zeros((LP, D), F32)

        held = {}

        def probs(q0, q1, k0, k1):
            held[q0] = [
                mm_t(
                    jnp.concatenate(
                        [do_ref[r, pair_rows(p, q0, q1), lanes], prod_ref[r, pair_rows(p, q0, q1), :]], axis=1
                    ),
                    jnp.concatenate([v_ref[l, r, k0:k1, lanes], ones[k0:k1]], axis=1),
                )
                for p, lanes in PAIRS
            ]

        def values(q0, q1, k0, k1):
            rows = slice(4 * q0, 4 * q1)
            dv_ref[r, k0:k1, :] += tmm(p_ref[l, r, rows, 0 : k1 - k0], do_ref[r, rows, :])

        def queries(q0, q1, k0, k1):
            n = q1 - q0
            ds = jnp.concatenate(
                [
                    (p_ref[l, r, pair_rows(p, q0, q1), 0 : k1 - k0].astype(F32) * held[q0][p]).astype(BF)
                    for p, _ in PAIRS
                ],
                axis=0,
            )
            dq = mm(ds, k_ref[l, r, k0:k1, :])
            dqkv_ref[l, base + q0 : base + q1, 0:256] = (one_row(dq, n) * 0.125).astype(BF)
            dk_ref[r, k0:k1, :] += tmm(ds, qs_ref[l, r, 4 * q0 : 4 * q1, :])

        def finish(lo, hi):
            rows = slice(base + lo, base + hi)
            dqkv_ref[l, rows, 256:512] = dk_ref[r, lo:hi, :].astype(BF)
            dqkv_ref[l, rows, 512:768] = dv_ref[r, lo:hi, :].astype(BF)
            d_a = mm_t(dqkv_ref[l, rows, :], wqkv_ref[l])
            xhat = xhat1_ref[l, r, lo:hi, :]
            again_ref[l, 0] += gain_rows(d_a, xhat)
            d_x = dh_ref[r, lo:hi, :] + norm_back(d_a, gains_ref[l, 0:1, :], xhat, wide(rstd1_ref[l, r, lo:hi, :]))
            if l:
                dbuf_ref[r, lo:hi, :] = d_x
                gb_ref[0, rows, :] = d_x.astype(BF)
            else:
                end = min(hi, length)
                d0, d1 = d_x[: end - lo], dbuf_ref[r, lo:hi, :][: end - lo]
                dk_out_ref[r, lo:end, :] = jnp.where(first, d0, d1)
                ds_out_ref[r, lo:hi, :] = jnp.where(first, dbuf_ref[r, lo:hi, :], d_x).astype(BF)

        order = [(probs, 0), (probs, 1), (values, 0), (queries, 0), (probs, 2), (values, 1), (queries, 1)]
        order += [(probs, 3), (values, 2), (queries, 2), (values, 3), (queries, 3)]
        return (
            [out]
            + [lambda f=f, b=BLOCKS[i]: f(*b) for f, i in order]
            + [lambda lo=lo, hi=hi: finish(lo, hi) for lo, hi in WHOLE]
        )

    def turn(j, ref, l):
        left_ref[j] = ref[l].T

    def mlp_weights(l):
        def down(c):
            for j in (c, c + 1):
                cols = slice(256 * j, 256 * j + 256)
                adown_ref[l, :, cols] += mm(left_ref[0], m_ref[l, :, cols])

        def up(c):
            for j in (c, c + 1):
                cols = slice(256 * j, 256 * j + 256)
                aup_ref[l, :, cols] += mm(left_ref[1], du_ref[l, :, cols])

        return [
            lambda: turn(0, gb_ref, l), lambda: turn(1, b_ref, l),
            lambda: down(0), lambda: down(2), lambda: up(0), lambda: up(2),
        ]

    def attn_weights(l):
        def out_and_query():
            aout_ref[l] += mm(left_ref[2], dhb_ref[l])
            aqkv_ref[l, :, 0:256] += mm(left_ref[3], dqkv_ref[l, :, 0:256])

        def key_and_value():
            for j in (1, 2):
                cols = slice(256 * j, 256 * j + 256)
                aqkv_ref[l, :, cols] += mm(left_ref[3], dqkv_ref[l, :, cols])

        return [lambda: turn(2, o_ref, l), lambda: turn(3, a_ref, l), out_and_query, key_and_value]

    merged(load(0) + attn_forward(0, 0), load(1) + attn_forward(1, 0))

    @pl.when(step == 0)
    def _():
        for copy in copies[4:]:
            copy.wait()

    merged(mlp_forward(0, 0), mlp_forward(1, 0))
    merged(attn_forward(0, 1), attn_forward(1, 1))
    merged(mlp_forward(0, 1), mlp_forward(1, 1))
    for r in range(TWO):
        gb_ref[1, LP * r : LP * r + LP, :] = cot_ref[r]
    merged(mlp_backward(0, 1), mlp_backward(1, 1))
    merged(mlp_weights(1))
    merged(attn_backward(0, 1), attn_backward(1, 1))
    merged(attn_weights(1))
    merged(mlp_backward(0, 0), mlp_backward(1, 0))
    merged(mlp_weights(0))
    merged(attn_backward(0, 0), attn_backward(1, 0))
    merged(attn_weights(0))

    @pl.when(step == last)
    def _():
        copies = []

        def hand(n, lo, rows, out):
            copies.append(pltpu.make_async_copy(grads_ref.at[n, pl.ds(lo, rows)], out, outsem.at[len(copies)]))
            copies[-1].start()

        for n, l, p_out, q_out in ((0, 1 - sec, psend_hbm, qsend_hbm), (1, sec, pkeep_hbm, qkeep_hbm)):
            for j in range(4):
                grads_ref[n, 256 * j : 256 * j + 256, :] = aup_ref[l, :, 256 * j : 256 * j + 256].astype(BF)
            for j in range(2):
                grads_ref[n, 1024 + 256 * j : 1280 + 256 * j, :] = adown_ref[l, :, 256 * j : 256 * j + 256].astype(BF).T
            row = lax.broadcasted_iota(jnp.int32, (16, D), 0)
            attn = jnp.sum(again_ref[l, 0], axis=0, keepdims=True)
            mlp = jnp.sum(again_ref[l, 1], axis=0, keepdims=True)
            grads_ref[n, HALF : HALF + 16, :] = jnp.where(row == 0, attn, jnp.where(row == 1, mlp, 0.0)).astype(BF)
            hand(n, 0, HALF + 16, p_out)
            for j in range(3):
                grads_ref[n, 1552 + 256 * j : 1808 + 256 * j, :] = aqkv_ref[l, :, 256 * j : 256 * j + 256].astype(BF)
            grads_ref[n, 2320:2576, :] = aout_ref[l].astype(BF)
            for j in range(2):
                grads_ref[n, 2576 + 256 * j : 2832 + 256 * j, :] = adown_ref[l, :, 512 + 256 * j : 768 + 256 * j].astype(BF).T
            hand(n, HALF + 16, HALF, q_out)
        for copy in copies:
            copy.wait()


def spread(
    sec_ref, seg_ref, x_hbm, cot_hbm, x_out, cot_out, eq_out, ek_out,
    x_ref, cot_ref, x_rows, cot_rows, eq_ref, ek_ref, wide_ref, seg_pad_ref, sem, outsem,
):
    length, count, _ = x_ref.shape
    begin = sec_ref[0] * (count // 2)
    loads = [pltpu.make_async_copy(x_hbm, x_ref, sem.at[0]), pltpu.make_async_copy(cot_hbm, cot_ref, sem.at[1])]
    stores = [
        pltpu.make_async_copy(held, out, outsem.at[n])
        for n, (held, out) in enumerate(((eq_ref, eq_out), (ek_ref, ek_out), (x_rows, x_out), (cot_rows, cot_out)))
    ]
    for copy in loads:
        copy.start()
    seg_pad_ref[...] = jnp.full(seg_pad_ref.shape, -1, jnp.int32)
    seg_pad_ref[:, 0:length] = seg_ref[...]
    lane = lax.broadcasted_iota(jnp.int32, (LP, 128), 1)
    token = lax.broadcasted_iota(jnp.int32, (LP, 128), 0)
    framed = lane < 64
    here = jnp.logical_and(token >= FRAME * lane, token < FRAME * lane + FRAME)
    here = jnp.where(jnp.logical_and(framed, here), 1.0, 0.0)
    later = jnp.where(jnp.logical_and(framed, token >= FRAME * lane + FRAME), BIG, 0.0)
    piece = lax.broadcasted_iota(jnp.int32, (16, seg_pad_ref.shape[1]), 0)
    column = lax.broadcasted_iota(jnp.int32, (16, 128), 1) - 64
    unit = jnp.where(column == lax.broadcasted_iota(jnp.int32, (16, 128), 0), 1.0, 0.0).astype(BF)
    for r in range(count // 2):
        seg = jnp.broadcast_to(seg_pad_ref[pl.ds(begin + r, 1), :], piece.shape)
        same = jnp.where(seg == piece, 1.0, 0.0).astype(BF)[:, :LP]
        other = jnp.where(jnp.logical_and(seg != piece, piece < 4), BIG, 0.0).astype(BF)[:, :LP]
        eq_ref[r] = (here + tmm(same, unit)).astype(BF)
        ek_ref[r] = (later + tmm(other, unit)).astype(BF)
    stores[0].start()
    stores[1].start()
    for n, (taken, rows) in enumerate(((x_ref, x_rows), (cot_ref, cot_rows))):
        loads[n].wait()
        for p in range(2):
            wide_ref[p] = taken[:, :, 128 * p : 128 * p + 128].astype(F32).reshape(length * count, 128)
        for r in range(count // 2):
            rows[r, LP - 16 : LP, :] = jnp.zeros((16, D), BF)
            for p in range(2):
                row = wide_ref[p, pl.ds(begin + r, length, stride=count), :]
                rows[r, 0:length, 128 * p : 128 * p + 128] = row.astype(BF)
        stores[2 + n].start()
    for copy in stores:
        copy.wait()


def prepare(section, x, cot, segments):
    length, rows, _ = x.shape
    hbm = pl.BlockSpec(memory_space=pl.ANY)
    vm = pltpu.VMEM
    tokens, columns = (rows // 2, LP, D), (rows // 2, LP, 128)
    return pl.pallas_call(
        spread,
        in_specs=[pl.BlockSpec(memory_space=pltpu.SMEM), pl.BlockSpec(memory_space=pltpu.VMEM), hbm, hbm],
        out_specs=[hbm] * 4,
        out_shape=[jax.ShapeDtypeStruct(dims, BF) for dims in (tokens, tokens, columns, columns)],
        scratch_shapes=[
            vm(x.shape, BF), vm(x.shape, BF), vm(tokens, BF), vm(tokens, BF), vm(columns, BF), vm(columns, BF),
            vm((2, length * rows, 128), F32), vm((rows, 384), jnp.int32),
            pltpu.SemaphoreType.DMA((2,)), pltpu.SemaphoreType.DMA((4,)),
        ],
        compiler_params=pltpu.CompilerParams(vmem_limit_bytes=65400 * 1024),
    )(section, segments, x, cot)


def local_step(section, rows_in, length, gains, other_gains, mine, other):
    count = rows_in[0].shape[0]
    steps = count // TWO
    tok = lambda w: pl.BlockSpec((TWO, LP, w), lambda i, sec: (i, 0, 0))
    row_out = pl.BlockSpec((TWO, length, D), lambda i, sec: (i, 0, 0))
    whole = lambda shape: pl.BlockSpec(shape, lambda i, sec: (0,) * len(shape), pipeline_mode=pl.Buffered(1))
    hbm = pl.BlockSpec(memory_space=pl.ANY)
    vm = pltpu.VMEM
    flat = lambda w: vm((2, TWO * LP, w), BF)
    shape = jax.ShapeDtypeStruct
    return pl.pallas_call(
        kernel,
        grid_spec=pltpu.PrefetchScalarGridSpec(
            num_scalar_prefetch=1,
            grid=(steps,),
            in_specs=[tok(D), tok(D), tok(128), tok(128)] + [whole((2, D))] * 2 + [hbm] * 8,
            out_specs=[row_out, tok(D), row_out, tok(D), hbm, hbm, hbm, hbm],
            scratch_shapes=[
                vm((2, D, 3 * D), BF), vm((2, D, D), BF), vm((2, D, FF), BF), vm((2, FF, D), BF), pltpu.SemaphoreType.DMA((8,)), pltpu.SemaphoreType.DMA((4,)), vm((2, 3088, D), BF),
                vm((2, 2, D), F32), vm((TWO, LP, D), BF), vm((TWO, LP, D), F32),
                vm((TWO, LP, D), F32),
                vm((2, TWO, LP, D), F32), vm((2, TWO, LP, 128), F32), vm((2, TWO, LP, D), F32), vm((2, TWO, LP, 128), F32),
                flat(D), flat(D), flat(D),
                vm((2, TWO, 4 * LP, D), BF), vm((2, TWO, LP, D), BF), vm((2, TWO, LP, D), BF),
                vm((2, TWO, 4 * LP, D), BF), flat(FF), vm((2, TWO, LP, FF), BF),
                flat(D), flat(FF), vm((TWO, LP, D), F32), flat(D),
                vm((TWO, 4 * LP, D), BF), vm((TWO, 4 * LP, 128), BF), flat(3 * D), vm((TWO, LP, D), F32), vm((TWO, LP, D), F32),
                vm((4, D, TWO * LP), BF), vm((2, D, 3 * D), F32), vm((2, D, D), F32), vm((2, D, FF), F32), vm((2, D, FF), F32),
                vm((2, 2, 8, D), F32),
            ],
        ),
        out_shape=[
            shape((count, length, D), BF), shape((count, LP, D), BF),
            shape((count, length, D), F32), shape((count, LP, D), BF),
            shape((HALF + 16, D), BF), shape((HALF, D), BF), shape((HALF + 16, D), BF), shape((HALF, D), BF),
        ],
        compiler_params=pltpu.CompilerParams(
            dimension_semantics=("arbitrary",), vmem_limit_bytes=60 * 1024 * 1024
        ),
    )(section, *rows_in, gains, other_gains, *mine, *other)


def partner(value):
    return lax.ppermute(value, "section", [(0, 1), (1, 0)])


def cross(value, count, bits):
    pairs = [(s * count + i, s * count + (i ^ (1 << bits[s]))) for s in range(2) for i in range(count)]
    return lax.ppermute(value, ("section", "dp"), pairs)


def add(a, b):
    return (a.astype(F32) + b.astype(F32)).astype(BF)


def idle(value_ref, event_ref, out_ref):
    pass


def after(value, event):
    hbm = pl.BlockSpec(memory_space=pl.ANY)
    return pl.pallas_call(
        idle,
        in_specs=[hbm, hbm],
        out_specs=hbm,
        out_shape=jax.ShapeDtypeStruct(value.shape, value.dtype),
        input_output_aliases={0: 0},
        compiler_params=pltpu.CompilerParams(vmem_limit_bytes=1024 * 1024),
    )(value, event)


def half_of(terms, tail, upper):
    main = terms[0].shape[0] - tail
    halves = [lax.dynamic_slice_in_dim(term, upper * (main // 2), main // 2, 0) for term in terms]
    out = halves[0] if len(terms) == 1 else add(*halves)
    if tail:
        ends = [term[main:] for term in terms]
        out = jnp.concatenate([out, ends[0] if len(terms) == 1 else add(*ends)], axis=0)
    return out


def sum_over_dp(parts, tail, section, follow):
    count = lax.axis_size("dp")
    place = lax.axis_index("dp")
    depth = count.bit_length() - 1
    orders = [list(range(depth)), list(range(depth))]
    if depth > 2:
        orders[1][1], orders[1][2] = 2, 1
    swap = {0: 1, 1: 0} if depth > 1 else {}
    orders = [[(b, swap.get(b, b)) for b in order] for order in orders]
    sizes = [tail, 0]
    current = list(parts)
    uppers = [[], []]
    sent = []
    for stage in range(depth):
        got = []
        for part in range(2):
            bits = orders[part][stage]
            upper = jnp.where(section == 0, place >> bits[0], place >> bits[1]) & 1
            uppers[part].append(upper)
            send = half_of(current[part], sizes[part], 1 - upper)
            got.append(cross(send, count, bits))
            sent.append(send)
        if stage == 0:
            followed = follow(sent)
        elif stage == 1:
            followed = followed[0], after(followed[1], sent[3])
        for part in range(2):
            keep = half_of(current[part], sizes[part], uppers[part][stage])
            current[part] = (add(keep, got[part]),)
    current = [value for value, in current]
    rest = current[0][current[0].shape[0] - tail :]
    current[0] = current[0][: current[0].shape[0] - tail]
    halves = []
    for stage in reversed(range(depth)):
        got = [cross(current[part], count, orders[part][stage]) for part in range(2)]
        for part in range(2):
            low = uppers[part][stage] == 0
            pair = (jnp.where(low, current[part], got[part]), jnp.where(low, got[part], current[part]))
            if stage == 0:
                halves.append(pair)
            else:
                current[part] = jnp.concatenate(pair, axis=0)
    return halves, rest, followed


def shards(
    layer_input, out_cotangent, segment_ids, gain_attn, weight_qkv, weight_out, gain_mlp, weight_up, weight_down
):
    section = lax.axis_index("section")
    here = section[None].astype(jnp.int32)
    rows_in = prepare(here, layer_input.swapaxes(0, 1), out_cotangent.swapaxes(0, 1), segment_ids)
    mine = (weight_qkv, weight_out, weight_up, weight_down)
    other = tuple(partner(w) for w in mine)
    gains = jnp.concatenate([gain_attn, gain_mlp], axis=0)
    other_gains = partner(gains)
    acts, acts_send, grads, grads_send, first, second, first_send, second_send = local_step(
        here, rows_in, layer_input.shape[1], gains, other_gains, mine, other,
    )
    length = layer_input.shape[1]
    rows_sent = lambda a: partner(a.reshape(-1, D))
    got = partner(first_send), partner(second_send)
    parts = (first, got[0]), (second, got[1])
    low = section == 0

    def whole_rows(keep, got):
        return jnp.concatenate([jnp.where(low, keep, got), jnp.where(low, got, keep)], axis=0)

    received = [rows_sent(a) for a in (acts_send, grads_send)]

    def rows_out(sent):
        got = [after(a, sent[0]) for a in received]
        got = [a.reshape(acts_send.shape)[:, :length] for a in got]
        return whole_rows(acts, got[0]), whole_rows(grads, got[1].astype(F32))

    ((up, up_down), (qkv, out_down)), rest, (activations, input_grads) = sum_over_dp(parts, 16, section, rows_out)
    side = lambda *blocks: jnp.concatenate(blocks, axis=1).astype(F32)
    return (
        activations[None],
        input_grads[None],
        side(qkv[0:256], qkv[256:512], qkv[512:768])[None],
        out_down[0:256].astype(F32)[None],
        side(up[0:256], up[256:512], up[512:768], up_down[0:256])[None],
        jnp.concatenate([up_down[256:768], out_down[256:768]], axis=0).astype(F32)[None],
        rest[0].astype(F32)[None],
        rest[1].astype(F32)[None],
    )


def solution(mesh):
    placed = (
        P("dp", None, None),
        P("dp", None, None),
        P("dp", None),
        P("section", None),
        P("section", None, None),
        P("section", None, None),
        P("section", None),
        P("section", None, None),
        P("section", None, None),
    )
    return jax.shard_map(
        shards,
        mesh=mesh,
        in_specs=placed,
        out_specs=(
            P("section", "dp", None, None),
            P("section", "dp", None, None),
            P("section", None, None),
            P("section", None, None),
            P("section", None, None),
            P("section", None, None),
            P("section", None),
            P("section", None),
        ),
        check_vma=False,
    )
```

```python
import jax
import jax.numpy as jnp
from jax import lax
from jax.experimental import pallas as pl
from jax.experimental.pallas import tpu as pltpu
from jax.sharding import PartitionSpec as P

D = 256
FF = 1024
FRAME = 17
LP = 352
EPS = 1e-05
BIG = -(2.0**100)
BLOCKS = ((0, 112, 0, 128), (112, 240, 0, 256), (240, 304, 64, 320), (304, 352, 96, 352))
ODDS = (-2.296875, -0.10888671875, 0.00135040283203125, -1.1146068572998047e-05)
TWO = 2
HALF = 1536
F32 = jnp.float32
BF = jnp.bfloat16


def mm(a, b):
    return jnp.dot(a, b, preferred_element_type=F32)


def mm_t(a, b):
    return lax.dot_general(a, b, (((1,), (1,)), ((), ())), preferred_element_type=F32)


def tmm(a, b):
    return lax.dot_general(a, b, (((0,), (0,)), ((), ())), preferred_element_type=F32)


def norm_stats(x):
    mean = jnp.sum(x, axis=-1, keepdims=True) * (1.0 / D)
    center = x - mean
    var = jnp.sum(center * center, axis=-1, keepdims=True) * (1.0 / D)
    rstd = lax.rsqrt(var + EPS)
    return center * rstd, rstd


def norm_back(d_out, gain, xhat, rstd):
    dy = d_out * gain
    s1 = jnp.sum(dy, axis=-1, keepdims=True) * (1.0 / D)
    s2 = jnp.sum(dy * xhat, axis=-1, keepdims=True) * (1.0 / D)
    return rstd * (dy - s1 - xhat * s2)


def gain_rows(d_out, xhat):
    prod = d_out * xhat
    return jnp.sum(prod.reshape(prod.shape[0] // 8, 8, D), axis=0)


def gelu_pair(u):
    low = lambda value: jnp.array(value, BF)
    u = u.astype(BF)
    u2 = u * u
    x = jnp.minimum(u2, low(25.0))
    p = ((x * low(ODDS[3]) + low(ODDS[2])) * x + low(ODDS[1])) * x + low(ODDS[0])
    cdf = pl.reciprocal(low(1.0) + jnp.exp2(u * p), approx=True)
    pdf = jnp.exp2(u2 * low(-0.7213475204444817) - low(1.3257480647361593))
    return u * cdf, cdf + u * pdf


def two_heads(block, lane_low):
    zero = jnp.zeros_like(block)
    return jnp.concatenate(
        [jnp.where(lane_low, block, zero), jnp.where(lane_low, zero, block)], axis=0
    )


def pair_rows(p, q0, q1):
    return slice(4 * q0 + 2 * p * (q1 - q0), 4 * q0 + 2 * (p + 1) * (q1 - q0))


def one_row(stacked, n):
    mask = low_mask(n)
    return jnp.concatenate(
        [
            jnp.where(mask, stacked[:n, 0:128], stacked[n : 2 * n, 0:128]),
            jnp.where(mask, stacked[2 * n : 3 * n, 128:256], stacked[3 * n :, 128:256]),
        ],
        axis=1,
    )


def low_mask(n):
    return lax.broadcasted_iota(jnp.int32, (n, 128), 1) < 64


def merged(*lists):
    tagged = [((i + 0.5) / len(units), j, unit) for j, units in enumerate(lists) for i, unit in enumerate(units)]
    for _, _, unit in sorted(tagged, key=lambda t: t[:2]):
        unit()


def wide(column):
    return jnp.concatenate([column, column], axis=1)


PARTS = ((0, 176), (176, 352))
WHOLE = ((0, LP),)
PAIRS = ((0, slice(0, 128)), (1, slice(128, 256)))


def kernel(
    sec_ref, x_ref, cot_ref, eq_ref, ek_ref, gains_mine, gains_other,
    wqkv_mine, wout_mine, wup_mine, wdown_mine, wqkv_other, wout_other, wup_other, wdown_other,
    yk_ref, ys_ref, dk_out_ref, ds_out_ref, pkeep_hbm, qkeep_hbm, psend_hbm, qsend_hbm,
    wqkv_ref, wout_ref, wup_ref, wdown_ref, wsem, outsem, grads_ref, gains_ref, ybuf_ref, dbuf_ref,
    res_ref, xhat1_ref, rstd1_ref, xhat2_ref, rstd2_ref, a_ref, b_ref, o_ref, qs_ref, k_ref, v_ref,
    p_ref, m_ref, gp_ref, gb_ref, du_ref, dh_ref, dhb_ref, do_ref, prod_ref, dqkv_ref, dk_ref, dv_ref,
    left_ref, aqkv_ref, aout_ref, aup_ref, adown_ref, again_ref,
):
    step = pl.program_id(0)
    last = pl.num_programs(0) - 1
    sec = sec_ref[0]
    first = sec == 0
    length = yk_ref.shape[1]

    copies = []
    for mine, other, held in (
        (wqkv_mine, wqkv_other, wqkv_ref), (wout_mine, wout_other, wout_ref),
        (wup_mine, wup_other, wup_ref), (wdown_mine, wdown_other, wdown_ref),
    ):
        copies.append(pltpu.make_async_copy(mine.at[0], held.at[sec], wsem.at[len(copies)]))
        copies.append(pltpu.make_async_copy(other.at[0], held.at[1 - sec], wsem.at[len(copies)]))

    @pl.when(step == 0)
    def _():
        for copy in copies:
            copy.start()
        mine, other = gains_mine[...].astype(F32), gains_other[...].astype(F32)
        gains_ref[0] = jnp.where(first, mine, other)
        gains_ref[1] = jnp.where(first, other, mine)
        for ref in (qs_ref, do_ref, aqkv_ref, aout_ref, aup_ref, adown_ref, again_ref):
            ref[...] = jnp.zeros_like(ref)
        for copy in copies[:4]:
            copy.wait()

    def load(r):
        def tokens(lo, hi):
            res_ref[r, lo:hi, :] = x_ref[r, lo:hi, :].astype(F32)

        return [lambda lo=lo, hi=hi: tokens(lo, hi) for lo, hi in PARTS]

    ones = jnp.ones((LP, 128), BF)

    def attn_forward(r, l):
        base = LP * r
        units = []

        def norm(lo, hi):
            xhat, rstd = norm_stats(res_ref[r, lo:hi, :])
            xhat1_ref[l, r, lo:hi, :] = xhat
            rstd1_ref[l, r, lo:hi, :] = jnp.broadcast_to(rstd, (hi - lo, 128))
            a_ref[l, base + lo : base + hi, :] = (xhat * gains_ref[l, 0:1, :]).astype(BF)

        def query():
            q = mm(a_ref[l, base : base + LP, :], wqkv_ref[l, :, 0:256]).astype(BF) * jnp.array(0.125, BF)
            for p, lanes in PAIRS:
                for q0, q1, _, _ in BLOCKS:
                    qs_ref[l, r, pair_rows(p, q0, q1), lanes] = two_heads(q[q0:q1, lanes], low_mask(q1 - q0))

        def key():
            k_ref[l, r] = mm(a_ref[l, base : base + LP, :], wqkv_ref[l, :, 256:512]).astype(BF)

        def value():
            v_ref[l, r] = mm(a_ref[l, base : base + LP, :], wqkv_ref[l, :, 512:768]).astype(BF)

        held = {}

        def scores(q0, q1, k0, k1):
            eq = eq_ref[r, q0:q1, :]
            eq = jnp.concatenate([eq, eq], axis=0)
            ek = ek_ref[r, k0:k1, :]
            held[q0] = [
                mm_t(
                    jnp.concatenate([qs_ref[l, r, pair_rows(p, q0, q1), lanes], eq], axis=1),
                    jnp.concatenate([k_ref[l, r, k0:k1, lanes], ek], axis=1),
                )
                for p, lanes in PAIRS
            ]

        def mix(q0, q1, k0, k1):
            n = q1 - q0
            probs = []
            for p, _ in PAIRS:
                s = held[q0][p]
                e = jnp.exp(s - jnp.max(s, axis=-1, keepdims=True))
                prob = (e * pl.reciprocal(jnp.sum(e, axis=-1, keepdims=True), approx=True)).astype(BF)
                p_ref[l, r, pair_rows(p, q0, q1), 0 : k1 - k0] = prob
                probs.append(prob)
            o = mm(jnp.concatenate(probs, axis=0), v_ref[l, r, k0:k1, :])
            o_ref[l, base + q0 : base + q1, :] = one_row(o, n).astype(BF)

        def out(lo, hi):
            h = res_ref[r, lo:hi, :] + mm(o_ref[l, base + lo : base + hi, :], wout_ref[l])
            res_ref[r, lo:hi, :] = h
            xhat, rstd = norm_stats(h)
            xhat2_ref[l, r, lo:hi, :] = xhat
            rstd2_ref[l, r, lo:hi, :] = jnp.broadcast_to(rstd, (hi - lo, 128))
            b_ref[l, base + lo : base + hi, :] = (xhat * gains_ref[l, 1:2, :]).astype(BF)

        units += [lambda lo=lo, hi=hi: norm(lo, hi) for lo, hi in PARTS]
        units += [query, key, value]
        first = [lambda b=b: scores(*b) for b in BLOCKS]
        second = [lambda b=b: mix(*b) for b in BLOCKS]
        units += [first[0], first[1], second[0], first[2], second[1], first[3], second[2], second[3]]
        units += [lambda lo=lo, hi=hi: out(lo, hi) for lo, hi in WHOLE]
        return units

    def mlp_forward(r, l):
        base = LP * r

        def chunk(c, lo, hi):
            rows = slice(base + lo, base + hi)
            ups = [mm(b_ref[l, rows, :], wup_ref[l, :, 256 * j : 256 * j + 256]) for j in (c, c + 1)]
            for j, u in zip((c, c + 1), ups):
                m, gp = gelu_pair(u)
                m_ref[l, rows, 256 * j : 256 * j + 256] = m.astype(BF)
                gp_ref[l, r, lo:hi, 256 * j : 256 * j + 256] = gp.astype(BF)

        def down(lo, hi):
            y = res_ref[r, lo:hi, :] + mm(m_ref[l, base + lo : base + hi, :], wdown_ref[l])
            y = y.astype(BF)
            if l == 0:
                ybuf_ref[r, lo:hi, :] = y
                res_ref[r, lo:hi, :] = y.astype(F32)
            else:
                end = min(hi, length)
                y0, y1 = ybuf_ref[r, lo:hi, :][: end - lo], y[: end - lo]
                yk_ref[r, lo:end, :] = jnp.where(first, y0, y1)
                ys_ref[r, lo:hi, :] = jnp.where(first, y, ybuf_ref[r, lo:hi, :])

        return [lambda: chunk(0, 0, LP), lambda: chunk(2, 0, LP), lambda: down(0, LP)]

    def mlp_backward(r, l):
        base = LP * r

        def chunk(c, lo, hi):
            rows = slice(base + lo, base + hi)
            dms = [mm_t(gb_ref[l, rows, :], wdown_ref[l, 256 * j : 256 * j + 256, :]) for j in (c, c + 1)]
            for j, dm in zip((c, c + 1), dms):
                cols = slice(256 * j, 256 * j + 256)
                du_ref[l, rows, cols] = (dm * gp_ref[l, r, lo:hi, cols].astype(F32)).astype(BF)

        def back(lo, hi):
            rows = slice(base + lo, base + hi)
            d_b = mm_t(du_ref[l, rows, :], wup_ref[l])
            xhat = xhat2_ref[l, r, lo:hi, :]
            again_ref[l, 1] += gain_rows(d_b, xhat)
            d_h = gb_ref[l, rows, :].astype(F32) + norm_back(d_b, gains_ref[l, 1:2, :], xhat, wide(rstd2_ref[l, r, lo:hi, :]))
            dh_ref[r, lo:hi, :] = d_h
            dhb_ref[l, rows, :] = d_h.astype(BF)

        return (
            [lambda c=c, lo=lo, hi=hi: chunk(c, lo, hi) for c in (0, 2) for lo, hi in WHOLE]
            + [lambda lo=lo, hi=hi: back(lo, hi) for lo, hi in WHOLE]
        )

    def attn_backward(r, l):
        base = LP * r

        def out():
            d_o = mm_t(dhb_ref[l, base : base + LP, :], wout_ref[l]).astype(BF)
            prod = (-(d_o.astype(F32) * o_ref[l, base : base + LP, :].astype(F32))).astype(BF)
            for p, lanes in PAIRS:
                for q0, q1, _, _ in BLOCKS:
                    mask = low_mask(q1 - q0)
                    do_ref[r, pair_rows(p, q0, q1), lanes] = two_heads(d_o[q0:q1, lanes], mask)
                    prod_ref[r, pair_rows(p, q0, q1), :] = two_heads(prod[q0:q1, lanes], mask)
            dk_ref[r] = jnp.zeros((LP, D), F32)
            dv_ref[r] = jnp.zeros((LP, D), F32)

        held = {}

        def probs(q0, q1, k0, k1):
            held[q0] = [
                mm_t(
                    jnp.concatenate(
                        [do_ref[r, pair_rows(p, q0, q1), lanes], prod_ref[r, pair_rows(p, q0, q1), :]], axis=1
                    ),
                    jnp.concatenate([v_ref[l, r, k0:k1, lanes], ones[k0:k1]], axis=1),
                )
                for p, lanes in PAIRS
            ]

        def values(q0, q1, k0, k1):
            rows = slice(4 * q0, 4 * q1)
            dv_ref[r, k0:k1, :] += tmm(p_ref[l, r, rows, 0 : k1 - k0], do_ref[r, rows, :])

        def queries(q0, q1, k0, k1):
            n = q1 - q0
            ds = jnp.concatenate(
                [
                    (p_ref[l, r, pair_rows(p, q0, q1), 0 : k1 - k0].astype(F32) * held[q0][p]).astype(BF)
                    for p, _ in PAIRS
                ],
                axis=0,
            )
            dq = mm(ds, k_ref[l, r, k0:k1, :])
            dqkv_ref[l, base + q0 : base + q1, 0:256] = (one_row(dq, n) * 0.125).astype(BF)
            dk_ref[r, k0:k1, :] += tmm(ds, qs_ref[l, r, 4 * q0 : 4 * q1, :])

        def finish(lo, hi):
            rows = slice(base + lo, base + hi)
            dqkv_ref[l, rows, 256:512] = dk_ref[r, lo:hi, :].astype(BF)
            dqkv_ref[l, rows, 512:768] = dv_ref[r, lo:hi, :].astype(BF)
            d_a = mm_t(dqkv_ref[l, rows, :], wqkv_ref[l])
            xhat = xhat1_ref[l, r, lo:hi, :]
            again_ref[l, 0] += gain_rows(d_a, xhat)
            d_x = dh_ref[r, lo:hi, :] + norm_back(d_a, gains_ref[l, 0:1, :], xhat, wide(rstd1_ref[l, r, lo:hi, :]))
            if l:
                dbuf_ref[r, lo:hi, :] = d_x
                gb_ref[0, rows, :] = d_x.astype(BF)
            else:
                end = min(hi, length)
                d0, d1 = d_x[: end - lo], dbuf_ref[r, lo:hi, :][: end - lo]
                dk_out_ref[r, lo:end, :] = jnp.where(first, d0, d1)
                ds_out_ref[r, lo:hi, :] = jnp.where(first, dbuf_ref[r, lo:hi, :], d_x).astype(BF)

        order = [(probs, 0), (probs, 1), (values, 0), (queries, 0), (probs, 2), (values, 1), (queries, 1)]
        order += [(probs, 3), (values, 2), (queries, 2), (values, 3), (queries, 3)]
        return (
            [out]
            + [lambda f=f, b=BLOCKS[i]: f(*b) for f, i in order]
            + [lambda lo=lo, hi=hi: finish(lo, hi) for lo, hi in WHOLE]
        )

    def turn(j, ref, l):
        left_ref[j] = ref[l].T

    def mlp_weights(l):
        def down(c):
            for j in (c, c + 1):
                cols = slice(256 * j, 256 * j + 256)
                adown_ref[l, :, cols] += mm(left_ref[0], m_ref[l, :, cols])

        def up(c):
            for j in (c, c + 1):
                cols = slice(256 * j, 256 * j + 256)
                aup_ref[l, :, cols] += mm(left_ref[1], du_ref[l, :, cols])

        return [
            lambda: turn(0, gb_ref, l), lambda: turn(1, b_ref, l),
            lambda: down(0), lambda: down(2), lambda: up(0), lambda: up(2),
        ]

    def attn_weights(l):
        def out_and_query():
            aout_ref[l] += mm(left_ref[2], dhb_ref[l])
            aqkv_ref[l, :, 0:256] += mm(left_ref[3], dqkv_ref[l, :, 0:256])

        def key_and_value():
            for j in (1, 2):
                cols = slice(256 * j, 256 * j + 256)
                aqkv_ref[l, :, cols] += mm(left_ref[3], dqkv_ref[l, :, cols])

        return [lambda: turn(2, o_ref, l), lambda: turn(3, a_ref, l), out_and_query, key_and_value]

    merged(load(0) + attn_forward(0, 0), load(1) + attn_forward(1, 0))

    @pl.when(step == 0)
    def _():
        for copy in copies[4:]:
            copy.wait()

    merged(mlp_forward(0, 0), mlp_forward(1, 0))
    merged(attn_forward(0, 1), attn_forward(1, 1))
    merged(mlp_forward(0, 1), mlp_forward(1, 1))
    for r in range(TWO):
        gb_ref[1, LP * r : LP * r + LP, :] = cot_ref[r]
    merged(mlp_backward(0, 1), mlp_backward(1, 1))
    merged(mlp_weights(1))
    merged(attn_backward(0, 1), attn_backward(1, 1))
    merged(attn_weights(1))
    merged(mlp_backward(0, 0), mlp_backward(1, 0))
    merged(mlp_weights(0))
    merged(attn_backward(0, 0), attn_backward(1, 0))
    merged(attn_weights(0))

    @pl.when(step == last)
    def _():
        copies = []

        def hand(n, lo, rows, out):
            copies.append(pltpu.make_async_copy(grads_ref.at[n, pl.ds(lo, rows)], out, outsem.at[len(copies)]))
            copies[-1].start()

        for n, l, p_out, q_out in ((0, 1 - sec, psend_hbm, qsend_hbm), (1, sec, pkeep_hbm, qkeep_hbm)):
            for j in range(4):
                grads_ref[n, 256 * j : 256 * j + 256, :] = aup_ref[l, :, 256 * j : 256 * j + 256].astype(BF)
            for j in range(2):
                grads_ref[n, 1024 + 256 * j : 1280 + 256 * j, :] = adown_ref[l, :, 256 * j : 256 * j + 256].astype(BF).T
            row = lax.broadcasted_iota(jnp.int32, (16, D), 0)
            attn = jnp.sum(again_ref[l, 0], axis=0, keepdims=True)
            mlp = jnp.sum(again_ref[l, 1], axis=0, keepdims=True)
            grads_ref[n, HALF : HALF + 16, :] = jnp.where(row == 0, attn, jnp.where(row == 1, mlp, 0.0)).astype(BF)
            hand(n, 0, HALF + 16, p_out)
            for j in range(3):
                grads_ref[n, 1552 + 256 * j : 1808 + 256 * j, :] = aqkv_ref[l, :, 256 * j : 256 * j + 256].astype(BF)
            grads_ref[n, 2320:2576, :] = aout_ref[l].astype(BF)
            for j in range(2):
                grads_ref[n, 2576 + 256 * j : 2832 + 256 * j, :] = adown_ref[l, :, 512 + 256 * j : 768 + 256 * j].astype(BF).T
            hand(n, HALF + 16, HALF, q_out)
        for copy in copies:
            copy.wait()


def spread(
    sec_ref, seg_ref, x_hbm, cot_hbm, x_out, cot_out, eq_out, ek_out,
    x_ref, cot_ref, x_rows, cot_rows, eq_ref, ek_ref, wide_ref, seg_pad_ref, sem, outsem,
):
    length, count, _ = x_ref.shape
    begin = sec_ref[0] * (count // 2)
    loads = [pltpu.make_async_copy(x_hbm, x_ref, sem.at[0]), pltpu.make_async_copy(cot_hbm, cot_ref, sem.at[1])]
    stores = [
        pltpu.make_async_copy(held, out, outsem.at[n])
        for n, (held, out) in enumerate(((eq_ref, eq_out), (ek_ref, ek_out), (x_rows, x_out), (cot_rows, cot_out)))
    ]
    for copy in loads:
        copy.start()
    seg_pad_ref[...] = jnp.full(seg_pad_ref.shape, -1, jnp.int32)
    seg_pad_ref[:, 0:length] = seg_ref[...]
    lane = lax.broadcasted_iota(jnp.int32, (LP, 128), 1)
    token = lax.broadcasted_iota(jnp.int32, (LP, 128), 0)
    framed = lane < 64
    here = jnp.logical_and(token >= FRAME * lane, token < FRAME * lane + FRAME)
    here = jnp.where(jnp.logical_and(framed, here), 1.0, 0.0)
    later = jnp.where(jnp.logical_and(framed, token >= FRAME * lane + FRAME), BIG, 0.0)
    piece = lax.broadcasted_iota(jnp.int32, (16, seg_pad_ref.shape[1]), 0)
    column = lax.broadcasted_iota(jnp.int32, (16, 128), 1) - 64
    unit = jnp.where(column == lax.broadcasted_iota(jnp.int32, (16, 128), 0), 1.0, 0.0).astype(BF)
    for r in range(count // 2):
        seg = jnp.broadcast_to(seg_pad_ref[pl.ds(begin + r, 1), :], piece.shape)
        same = jnp.where(seg == piece, 1.0, 0.0).astype(BF)[:, :LP]
        other = jnp.where(jnp.logical_and(seg != piece, piece < 4), BIG, 0.0).astype(BF)[:, :LP]
        eq_ref[r] = (here + tmm(same, unit)).astype(BF)
        ek_ref[r] = (later + tmm(other, unit)).astype(BF)
    stores[0].start()
    stores[1].start()
    for n, (taken, rows) in enumerate(((x_ref, x_rows), (cot_ref, cot_rows))):
        loads[n].wait()
        for p in range(2):
            wide_ref[p] = taken[:, :, 128 * p : 128 * p + 128].astype(F32).reshape(length * count, 128)
        for r in range(count // 2):
            rows[r, LP - 16 : LP, :] = jnp.zeros((16, D), BF)
            for p in range(2):
                row = wide_ref[p, pl.ds(begin + r, length, stride=count), :]
                rows[r, 0:length, 128 * p : 128 * p + 128] = row.astype(BF)
        stores[2 + n].start()
    for copy in stores:
        copy.wait()


def prepare(section, x, cot, segments):
    length, rows, _ = x.shape
    hbm = pl.BlockSpec(memory_space=pl.ANY)
    vm = pltpu.VMEM
    tokens, columns = (rows // 2, LP, D), (rows // 2, LP, 128)
    return pl.pallas_call(
        spread,
        in_specs=[pl.BlockSpec(memory_space=pltpu.SMEM), pl.BlockSpec(memory_space=pltpu.VMEM), hbm, hbm],
        out_specs=[hbm] * 4,
        out_shape=[jax.ShapeDtypeStruct(dims, BF) for dims in (tokens, tokens, columns, columns)],
        scratch_shapes=[
            vm(x.shape, BF), vm(x.shape, BF), vm(tokens, BF), vm(tokens, BF), vm(columns, BF), vm(columns, BF),
            vm((2, length * rows, 128), F32), vm((rows, 384), jnp.int32),
            pltpu.SemaphoreType.DMA((2,)), pltpu.SemaphoreType.DMA((4,)),
        ],
        compiler_params=pltpu.CompilerParams(vmem_limit_bytes=65400 * 1024),
    )(section, segments, x, cot)


def local_step(section, rows_in, length, gains, other_gains, mine, other):
    count = rows_in[0].shape[0]
    steps = count // TWO
    tok = lambda w: pl.BlockSpec((TWO, LP, w), lambda i, sec: (i, 0, 0))
    row_out = pl.BlockSpec((TWO, length, D), lambda i, sec: (i, 0, 0))
    whole = lambda shape: pl.BlockSpec(shape, lambda i, sec: (0,) * len(shape), pipeline_mode=pl.Buffered(1))
    hbm = pl.BlockSpec(memory_space=pl.ANY)
    vm = pltpu.VMEM
    flat = lambda w: vm((2, TWO * LP, w), BF)
    shape = jax.ShapeDtypeStruct
    return pl.pallas_call(
        kernel,
        grid_spec=pltpu.PrefetchScalarGridSpec(
            num_scalar_prefetch=1,
            grid=(steps,),
            in_specs=[tok(D), tok(D), tok(128), tok(128)] + [whole((2, D))] * 2 + [hbm] * 8,
            out_specs=[row_out, tok(D), row_out, tok(D), hbm, hbm, hbm, hbm],
            scratch_shapes=[
                vm((2, D, 3 * D), BF), vm((2, D, D), BF), vm((2, D, FF), BF), vm((2, FF, D), BF), pltpu.SemaphoreType.DMA((8,)), pltpu.SemaphoreType.DMA((4,)), vm((2, 3088, D), BF),
                vm((2, 2, D), F32), vm((TWO, LP, D), BF), vm((TWO, LP, D), F32),
                vm((TWO, LP, D), F32),
                vm((2, TWO, LP, D), F32), vm((2, TWO, LP, 128), F32), vm((2, TWO, LP, D), F32), vm((2, TWO, LP, 128), F32),
                flat(D), flat(D), flat(D),
                vm((2, TWO, 4 * LP, D), BF), vm((2, TWO, LP, D), BF), vm((2, TWO, LP, D), BF),
                vm((2, TWO, 4 * LP, D), BF), flat(FF), vm((2, TWO, LP, FF), BF),
                flat(D), flat(FF), vm((TWO, LP, D), F32), flat(D),
                vm((TWO, 4 * LP, D), BF), vm((TWO, 4 * LP, 128), BF), flat(3 * D), vm((TWO, LP, D), F32), vm((TWO, LP, D), F32),
                vm((4, D, TWO * LP), BF), vm((2, D, 3 * D), F32), vm((2, D, D), F32), vm((2, D, FF), F32), vm((2, D, FF), F32),
                vm((2, 2, 8, D), F32),
            ],
        ),
        out_shape=[
            shape((count, length, D), BF), shape((count, LP, D), BF),
            shape((count, length, D), F32), shape((count, LP, D), BF),
            shape((HALF + 16, D), BF), shape((HALF, D), BF), shape((HALF + 16, D), BF), shape((HALF, D), BF),
        ],
        compiler_params=pltpu.CompilerParams(
            dimension_semantics=("arbitrary",), vmem_limit_bytes=60 * 1024 * 1024
        ),
    )(section, *rows_in, gains, other_gains, *mine, *other)


def partner(value):
    return lax.ppermute(value, "section", [(0, 1), (1, 0)])


def cross(value, count, bits):
    pairs = [(s * count + i, s * count + (i ^ (1 << bits[s]))) for s in range(2) for i in range(count)]
    return lax.ppermute(value, ("section", "dp"), pairs)


def add(a, b):
    return (a.astype(F32) + b.astype(F32)).astype(BF)


def idle(value_ref, event_ref, out_ref):
    pass


def after(value, event):
    hbm = pl.BlockSpec(memory_space=pl.ANY)
    return pl.pallas_call(
        idle,
        in_specs=[hbm, hbm],
        out_specs=hbm,
        out_shape=jax.ShapeDtypeStruct(value.shape, value.dtype),
        input_output_aliases={0: 0},
        compiler_params=pltpu.CompilerParams(vmem_limit_bytes=1024 * 1024),
    )(value, event)


def half_of(terms, tail, upper):
    main = terms[0].shape[0] - tail
    halves = [lax.dynamic_slice_in_dim(term, upper * (main // 2), main // 2, 0) for term in terms]
    out = halves[0] if len(terms) == 1 else add(*halves)
    if tail:
        ends = [term[main:] for term in terms]
        out = jnp.concatenate([out, ends[0] if len(terms) == 1 else add(*ends)], axis=0)
    return out


def sum_over_dp(parts, tail, section, follow):
    count = lax.axis_size("dp")
    place = lax.axis_index("dp")
    depth = count.bit_length() - 1
    orders = [list(range(depth)), list(range(depth))]
    if depth > 2:
        orders[1][1], orders[1][2] = 2, 1
    swap = {0: 1, 1: 0} if depth > 1 else {}
    orders = [[(b, swap.get(b, b)) for b in order] for order in orders]
    sizes = [tail, 0]
    current = list(parts)
    uppers = [[], []]
    sent = []
    for stage in range(depth):
        got = []
        for part in range(2):
            bits = orders[part][stage]
            upper = jnp.where(section == 0, place >> bits[0], place >> bits[1]) & 1
            uppers[part].append(upper)
            send = half_of(current[part], sizes[part], 1 - upper)
            got.append(cross(send, count, bits))
            sent.append(send)
        if stage == 0:
            followed = follow(sent)
        elif stage == 1:
            followed = followed[0], after(followed[1], sent[3])
        for part in range(2):
            keep = half_of(current[part], sizes[part], uppers[part][stage])
            current[part] = (add(keep, got[part]),)
    current = [value for value, in current]
    rest = current[0][current[0].shape[0] - tail :]
    current[0] = current[0][: current[0].shape[0] - tail]
    halves = []
    for stage in reversed(range(depth)):
        got = [cross(current[part], count, orders[part][stage]) for part in range(2)]
        for part in range(2):
            low = uppers[part][stage] == 0
            pair = (jnp.where(low, current[part], got[part]), jnp.where(low, got[part], current[part]))
            if stage == 0:
                halves.append(pair)
            else:
                current[part] = jnp.concatenate(pair, axis=0)
    return halves, rest, followed


def shards(
    layer_input, out_cotangent, segment_ids, gain_attn, weight_qkv, weight_out, gain_mlp, weight_up, weight_down
):
    section = lax.axis_index("section")
    here = section[None].astype(jnp.int32)
    rows_in = prepare(here, layer_input.swapaxes(0, 1), out_cotangent.swapaxes(0, 1), segment_ids)
    mine = (weight_qkv, weight_out, weight_up, weight_down)
    other = tuple(partner(w) for w in mine)
    gains = jnp.concatenate([gain_attn, gain_mlp], axis=0)
    other_gains = partner(gains)
    acts, acts_send, grads, grads_send, first, second, first_send, second_send = local_step(
        here, rows_in, layer_input.shape[1], gains, other_gains, mine, other,
    )
    length = layer_input.shape[1]
    rows_sent = lambda a: partner(a.reshape(-1, D))
    got = partner(first_send), partner(second_send)
    parts = (first, got[0]), (second, got[1])
    low = section == 0

    def whole_rows(keep, got):
        return jnp.concatenate([jnp.where(low, keep, got), jnp.where(low, got, keep)], axis=0)

    received = [rows_sent(a) for a in (acts_send, grads_send)]

    def rows_out(sent):
        got = [after(a, sent[0]) for a in received]
        got = [a.reshape(acts_send.shape)[:, :length] for a in got]
        return whole_rows(acts, got[0]), whole_rows(grads, got[1].astype(F32))

    ((up, up_down), (qkv, out_down)), rest, (activations, input_grads) = sum_over_dp(parts, 16, section, rows_out)
    side = lambda *blocks: jnp.concatenate(blocks, axis=1).astype(F32)
    return (
        activations[None],
        input_grads[None],
        side(qkv[0:256], qkv[256:512], qkv[512:768])[None],
        out_down[0:256].astype(F32)[None],
        side(up[0:256], up[256:512], up[512:768], up_down[0:256])[None],
        jnp.concatenate([up_down[256:768], out_down[256:768]], axis=0).astype(F32)[None],
        rest[0].astype(F32)[None],
        rest[1].astype(F32)[None],
    )


def solution(mesh):
    placed = (
        P("dp", None, None),
        P("dp", None, None),
        P("dp", None),
        P("section", None),
        P("section", None, None),
        P("section", None, None),
        P("section", None),
        P("section", None, None),
        P("section", None, None),
    )
    return jax.shard_map(
        shards,
        mesh=mesh,
        in_specs=placed,
        out_specs=(
            P("section", "dp", None, None),
            P("section", "dp", None, None),
            P("section", None, None),
            P("section", None, None),
            P("section", None, None),
            P("section", None, None),
            P("section", None),
            P("section", None),
        ),
        check_vma=False,
    )
```
